32 devices in a mesh: dp: 4 (over y, x), seq: 8 (over z, core).
Axes of the slice: x: 2, y: 2, z: 4, core: 2. Of those that a mesh axis runs over, the one named last changes fastest.
Arguments:
- tokens: bfloat16 [4, 1024, 1024], P('dp', 'seq'), may hold values from -7 to 7
- cotangent: bfloat16 [4, 1024, 1024], P('dp', 'seq'), may hold values from -6 to 6
- weight_qkv: float32 [1024, 3072], P(('dp', 'seq')), may hold values from -0.1875 to 0.1875
- weight_out: float32 [1024, 1024], P(('dp', 'seq')), may hold values from -3.5 to 3.5
- weight_up: float32 [1024, 4096], P(('dp', 'seq')), may hold values from -0.1875 to 0.1875
- weight_down: float32 [4096, 1024], P(('dp', 'seq')), may hold values from -0.09375 to 0.09375
- small_params: float32 [1024, 12], P(('dp', 'seq')), may hold values from -1.3 to 3, as said below
- moment_qkv: float32 [1024, 3072], P(('dp', 'seq')), may hold values from -0.0017089844 to 0.0017089844
- moment_out: float32 [1024, 1024], P(('dp', 'seq')), may hold values from -9.1552734e-05 to 9.1552734e-05
- moment_up: float32 [1024, 4096], P(('dp', 'seq')), may hold values from -0.0017089844 to 0.0017089844
- moment_down: float32 [4096, 1024], P(('dp', 'seq')), may hold values from -0.0017089844 to 0.0017089844
- moment_small: float32 [1024, 12], P(('dp', 'seq')), may hold values from -0.0034179688 to 0.0034179688
- second_qkv: float32 [1024, 3072], P(('dp', 'seq')), may hold values from 6.510417e-08 to 2.6200456e-07
- second_out: float32 [1024, 1024], P(('dp', 'seq')), may hold values from 1.9036306e-10 to 7.6609524e-10
- second_up: float32 [1024, 4096], P(('dp', 'seq')), may hold values from 6.510417e-08 to 2.6200456e-07
- second_down: float32 [4096, 1024], P(('dp', 'seq')), may hold values from 6.510417e-08 to 2.6200456e-07
- second_small: float32 [1024, 12], P(('dp', 'seq')), may hold values from 2.6200456e-07 to 1.0321393e-06
Outputs:
- layer_output: bfloat16 [4, 1024, 1024], P('dp', 'seq')
- grad_tokens: float32 [4, 1024, 1024], P('dp', 'seq')
- grad_norm: float32 [], replicated
- new_qkv: float32 [1024, 3072], P(('dp', 'seq'))
- new_out: float32 [1024, 1024], P(('dp', 'seq'))
- new_up: float32 [1024, 4096], P(('dp', 'seq'))
- new_down: float32 [4096, 1024], P(('dp', 'seq'))
- new_small: float32 [1024, 12], P(('dp', 'seq'))
- new_moment_qkv: float32 [1024, 3072], P(('dp', 'seq'))
- new_moment_out: float32 [1024, 1024], P(('dp', 'seq'))
- new_moment_up: float32 [1024, 4096], P(('dp', 'seq'))
- new_moment_down: float32 [4096, 1024], P(('dp', 'seq'))
- new_moment_small: float32 [1024, 12], P(('dp', 'seq'))
- new_second_qkv: float32 [1024, 3072], P(('dp', 'seq'))
- new_second_out: float32 [1024, 1024], P(('dp', 'seq'))
- new_second_up: float32 [1024, 4096], P(('dp', 'seq'))
- new_second_down: float32 [4096, 1024], P(('dp', 'seq'))
- new_second_small: float32 [1024, 12], P(('dp', 'seq'))
The draws below stay inside these ranges and needn't reach their ends.
Inputs may be any that keep to these rules, and one draw needn't show every extreme that they name: `small_params`: gain columns are positive.
All inputs are finite; a program needn't handle non-finite values.
Results may differ from the reference program's by a relative error of at most 0.015.
Values may be sent and summed in bfloat16 or wider, within the bound.
No kernel may reach another device: no remote copies, remote signals or barrier semaphores. Data moves between devices by JAX's collectives and lax.ppermute only.
A program may use at most 192 MiB of HBM per device.

```python
import math
import jax
import jax.numpy as jnp
from jax import lax

D = 1024
FF = 4096
HEAD = 64
TOK_SEQ = 128
STEP = 5
LENGTH = 1024
SEQUENCES = 4
SMALL_COLS = 12
NPARAM = 12595200
N_DP = 4
N_SEQ = 8
DEVICES = 32


def rising_scale(rise):
    column = jnp.arange(D)
    owner = column // (D // DEVICES)
    first = (owner // N_SEQ).astype(jnp.float32) / max(N_DP - 1, 1)
    second = (owner % N_SEQ).astype(jnp.float32) / max(N_SEQ - 1, 1)
    return rise ** (0.5 * (first + second) - 0.5)


def draw_tokens(key, part):
    key = jax.random.fold_in(key, 11)
    scale = rising_scale(3.0)
    base = jnp.clip(jax.random.normal(key, (N_DP, LENGTH, D), jnp.float32), -4.0, 4.0)
    return (base * scale).astype(jnp.bfloat16)


def draw_small_params(key, part):
    key = jax.random.fold_in(key, 23)
    ratio = FF // D
    columns = 8 + ratio
    scale = rising_scale(3.0)
    noise = jnp.clip(jax.random.normal(key, (D, columns), jnp.float32), -4.0, 4.0)
    gains = scale[:, None] * (1.0 + 0.1 * noise)
    biases = 0.3 * noise
    column = jnp.arange(columns)
    is_gain = (column == 4 + ratio) | (column == 6 + ratio)
    return jnp.where(is_gain[None, :], gains, biases).astype(jnp.float32)


def block_scale(stream_key, shape, split, smallest, high):
    level, own = 1.0, jax.random.fold_in(stream_key, 6)
    for dim, shards_of in split:
        draws = jnp.exp(jax.random.uniform(jax.random.fold_in(own, dim), (shards_of,), jnp.float32, smallest / len(split), high / len(split)))
        level = level * jnp.repeat(draws, shape[dim] // shards_of).reshape([-1 if axis == dim else 1 for axis in range(len(shape))])
    return level


def gaussian(own_key, extent, deviation, most, pieces=(), kind=jnp.bfloat16):
    loudness = block_scale(own_key, extent, pieces, -0.22, 0.18) if pieces else 1.0
    result = jax.random.normal(own_key, extent, jnp.float32) * deviation * loudness
    return jnp.minimum(jnp.maximum(result, -most), most).astype(kind)


def setup_inputs(seed: int = 0) -> dict:
    arg_keys = jax.random.split(jax.random.key(seed), 18)
    return {
        "tokens": draw_tokens(jax.random.fold_in(arg_keys[17], 71), 0),
        "cotangent": gaussian(arg_keys[1], (SEQUENCES, LENGTH, D), 1.0, 6.0, ((0, 4), (1, 8))),
        "weight_qkv": gaussian(arg_keys[2], (D, 3 * D), D ** -0.5, 0.1875, ((0, 32),), jnp.float32),
        "weight_out": gaussian(arg_keys[3], (D, D), (((LENGTH + 2) // 3) ** 0.5 * D ** -0.5), 3.5, ((0, 32),), jnp.float32),
        "weight_up": gaussian(arg_keys[4], (D, FF), D ** -0.5, 0.1875, ((0, 32),), jnp.float32),
        "weight_down": gaussian(arg_keys[5], (FF, D), FF ** -0.5, 0.09375, ((0, 32),), jnp.float32),
        "small_params": draw_small_params(jax.random.fold_in(arg_keys[17], 71), 0),
        "moment_qkv": gaussian(arg_keys[7], (D, 3 * D), (NPARAM ** -0.5), 0.0017089844, ((0, 32),), jnp.float32),
        "moment_out": gaussian(arg_keys[8], (D, D), (NPARAM ** -0.5 * ((LENGTH + 2) // 3) ** -0.5), 9.1552734375e-05, ((0, 32),), jnp.float32),
        "moment_up": gaussian(arg_keys[9], (D, FF), (NPARAM ** -0.5), 0.0017089844, ((0, 32),), jnp.float32),
        "moment_down": gaussian(arg_keys[10], (FF, D), (NPARAM ** -0.5), 0.0017089844, ((0, 32),), jnp.float32),
        "moment_small": gaussian(arg_keys[11], (D, SMALL_COLS), (2 * NPARAM ** -0.5), 0.0034179688, ((0, 32),), jnp.float32),
        "second_qkv": jnp.clip(jnp.exp(math.log(2.620045620460587e-07) - 1.39237335 * jax.random.uniform(arg_keys[12], (D, 3 * D), jnp.float32) ** block_scale(arg_keys[12], (D, 3 * D), ((0, 32),), -0.2, 0.2)), 6.510416739047287e-08, 2.620045620460587e-07),
        "second_out": jnp.clip(jnp.exp(math.log(7.660952427990253e-10) - 1.3923734 * jax.random.uniform(arg_keys[13], (D, D), jnp.float32) ** block_scale(arg_keys[13], (D, D), ((0, 32),), -0.2, 0.2)), 1.9036305864972292e-10, 7.660952427990253e-10),
        "second_up": jnp.clip(jnp.exp(math.log(2.620045620460587e-07) - 1.39237335 * jax.random.uniform(arg_keys[14], (D, FF), jnp.float32) ** block_scale(arg_keys[14], (D, FF), ((0, 32),), -0.2, 0.2)), 6.510416739047287e-08, 2.620045620460587e-07),
        "second_down": jnp.clip(jnp.exp(math.log(2.620045620460587e-07) - 1.39237335 * jax.random.uniform(arg_keys[15], (FF, D), jnp.float32) ** block_scale(arg_keys[15], (FF, D), ((0, 32),), -0.2, 0.2)), 6.510416739047287e-08, 2.620045620460587e-07),
        "second_small": jnp.clip(jnp.exp(math.log(1.0321392664991436e-06) - 1.371027 * jax.random.uniform(arg_keys[16], (D, SMALL_COLS), jnp.float32) ** block_scale(arg_keys[16], (D, SMALL_COLS), ((0, 32),), -0.2, 0.2)), 2.620045620460587e-07, 1.0321392664991436e-06),
    }


NORM_EPSILON = 1e-05
ADAM_EPSILON = 1e-08
BETA_FIRST = 0.5
BETA_SECOND = 0.55
CLIP_LIMIT = 1.0
RATE_MATRIX = 0.04
RATE_OUTPUT = 0.5
RATE_SMALL = 0.3
WEIGHT_DECAY = 0.01
SCORE_SCALE = 0.125
HIGHEST = lax.Precision.HIGHEST

@jax.custom_vjp
def low(v):
    return lax.optimization_barrier(v.astype(jnp.bfloat16)).astype(jnp.float32)

@jax.custom_vjp
def low_back(v):
    return v

def low_keep(v):
    return (low(v), None)

def low_pass(kept, grad):
    return (grad,)

def back_keep(v):
    return (v, None)

def back_low(kept, grad):
    return (low(grad),)
low.defvjp(low_keep, low_pass)
low_back.defvjp(back_keep, back_low)

def layer_norm(value, gain, shift):
    center = lax.optimization_barrier(jnp.mean(value, axis=-1, keepdims=True))
    centered = value - center
    variance = lax.optimization_barrier(jnp.mean(centered * centered, axis=-1, keepdims=True))
    return centered * lax.rsqrt(variance + NORM_EPSILON) * gain + shift

def unpack(table):
    ratio = FF // D
    bias_up = table[:, 3:3 + ratio].T.reshape(-1)
    return (table[:, 0], table[:, 1], table[:, 2], bias_up, table[:, 3 + ratio], table[:, 4 + ratio], table[:, 5 + ratio], table[:, 6 + ratio], table[:, 7 + ratio])

def attend_rows(query_rows, key_heads, value_heads):
    scores = low_back(jnp.einsum('qhd,khd->hqk', query_rows, key_heads, precision=HIGHEST) * SCORE_SCALE)
    probs = jax.nn.softmax(scores, axis=-1)
    return jnp.einsum('hqk,khd->qhd', low(probs), value_heads, precision=HIGHEST)

def sequence_forward(rows, params):
    full_qkv, full_out, full_up, full_down, full_small = params
    bias_query, bias_value, bias_out, bias_up, bias_down, gain_one, shift_one, gain_two, shift_two = unpack(full_small)
    heads = D // HEAD
    block = 4 * TOK_SEQ
    projected = jnp.dot(rows, full_qkv, precision=HIGHEST)
    query = low_back(low(projected[:, :D] + bias_query))
    keys = low_back(low(projected[:, D:2 * D]))
    values = low_back(low(projected[:, 2 * D:] + bias_value))
    key_heads = keys.reshape(LENGTH, heads, HEAD)
    value_heads = values.reshape(LENGTH, heads, HEAD)
    checked = jax.checkpoint(attend_rows)
    query_blocks = query.reshape(LENGTH // block, block, heads, HEAD)
    attended = lax.map(lambda part_rows: checked(part_rows, key_heads, value_heads), query_blocks)
    attended = low_back(low(attended.reshape(LENGTH, D)))
    branch = low_back(jnp.dot(attended, full_out, precision=HIGHEST) + bias_out)
    middle = rows + branch
    hidden = layer_norm(middle, gain_one, shift_one)
    upward = low_back(jnp.dot(low(hidden), full_up, precision=HIGHEST) + bias_up)
    activation = low(jax.nn.gelu(upward, approximate=False))
    downward = low_back(jnp.dot(activation, full_down, precision=HIGHEST) + bias_down)
    return layer_norm(hidden + downward, gain_two, shift_two)

def adam_update(weight, grad, moment, second, rate, decay):
    moment_new = BETA_FIRST * moment + (1.0 - BETA_FIRST) * grad
    second_new = BETA_SECOND * second + (1.0 - BETA_SECOND) * grad * grad
    direction = moment_new / (1.0 - BETA_FIRST ** STEP) / (jnp.sqrt(second_new / (1.0 - BETA_SECOND ** STEP)) + ADAM_EPSILON)
    return (weight - rate * (direction + decay * weight), moment_new, second_new)

def reference(tokens, cotangent, weight_qkv, weight_out, weight_up, weight_down, small_params, moment_qkv, moment_out, moment_up, moment_down, moment_small, second_qkv, second_out, second_up, second_down, second_small):

    def forward(inputs, master_qkv, master_out, master_up, master_down, master_small):
        params = (low(master_qkv), low(master_out), low(master_up), low(master_down), low(master_small))
        return lax.map(lambda rows: sequence_forward(rows, params), inputs)
    output, pullback = jax.vjp(forward, tokens.astype(jnp.float32), weight_qkv, weight_out, weight_up, weight_down, small_params)
    grads = pullback(cotangent.astype(jnp.float32))
    grad_tokens = grads[0]
    squares = jnp.sum(grads[1] * grads[1]) + jnp.sum(grads[2] * grads[2])
    squares = squares + jnp.sum(grads[3] * grads[3]) + jnp.sum(grads[4] * grads[4])
    squares = squares + jnp.sum(grads[5] * grads[5])
    grad_norm = jnp.sqrt(squares)
    factor = jnp.minimum(1.0, CLIP_LIMIT / (grad_norm + 1e-06))
    new_qkv, new_moment_qkv, new_second_qkv = adam_update(weight_qkv, grads[1] * factor, moment_qkv, second_qkv, RATE_MATRIX, WEIGHT_DECAY)
    new_out, new_moment_out, new_second_out = adam_update(weight_out, grads[2] * factor, moment_out, second_out, RATE_OUTPUT, WEIGHT_DECAY)
    new_up, new_moment_up, new_second_up = adam_update(weight_up, grads[3] * factor, moment_up, second_up, RATE_MATRIX, WEIGHT_DECAY)
    new_down, new_moment_down, new_second_down = adam_update(weight_down, grads[4] * factor, moment_down, second_down, RATE_MATRIX, WEIGHT_DECAY)
    new_small, new_moment_small, new_second_small = adam_update(small_params, grads[5] * factor, moment_small, second_small, RATE_SMALL, 0.0)
    return (output.astype(jnp.bfloat16), grad_tokens, grad_norm, new_qkv, new_out, new_up, new_down, new_small, new_moment_qkv, new_moment_out, new_moment_up, new_moment_down, new_moment_small, new_second_qkv, new_second_out, new_second_up, new_second_down, new_second_small)
```

```python
import jax
import jax.numpy as jnp
from jax import lax
from jax.experimental import pallas as pl
from jax.experimental.pallas import tpu as pltpu
from jax.sharding import Mesh
from jax.sharding import PartitionSpec as P

HEAD = 64
STEP = 5


NORM_EPSILON = 1e-05
ADAM_EPSILON = 1e-08
BETA_FIRST = 0.5
BETA_SECOND = 0.55
CLIP_LIMIT = 1.0
RATE_MATRIX = 0.04
RATE_OUTPUT = 0.5
RATE_SMALL = 0.3
WEIGHT_DECAY = 0.01
SCORE_SCALE = 0.125


def layer_norm(value, gain, shift):
    center = jnp.mean(value, axis=-1, keepdims=True)
    centered = value - center
    variance = jnp.mean(centered * centered, axis=-1, keepdims=True)
    return centered * lax.rsqrt(variance + NORM_EPSILON) * gain + shift


def exact_gelu(value):
    return jax.nn.gelu(value, approximate=False)


def unpack(table_low):
    table = table_low.astype(jnp.float32)
    ratio = table.shape[1] - 8
    bias_up = table[:, 3 : 3 + ratio].T.reshape(-1)
    return (
        table[:, 0],
        table[:, 1],
        table[:, 2],
        bias_up,
        table[:, 3 + ratio],
        table[:, 4 + ratio],
        table[:, 5 + ratio],
        table[:, 6 + ratio],
        table[:, 7 + ratio],
    )


def cross(left, right):
    return lax.dot_general(
        left, right, (((0,), (0,)), ((), ())), preferred_element_type=jnp.float32
    )


def against(left, right):
    return lax.dot_general(
        left, right, (((1,), (1,)), ((), ())), preferred_element_type=jnp.float32
    )


def take_block(source, index, block, heads):
    piece = lax.dynamic_slice_in_dim(source, index * block, block, 0)
    return piece.reshape(block, heads, HEAD)


def scores_of(query_heads, key_heads):
    return (
        jnp.einsum("qhd,khd->hqk", query_heads, key_heads, preferred_element_type=jnp.float32)
        * SCORE_SCALE
    )


def block_grads(query_heads, key_heads, value_heads, dout_heads, log_total, delta):
    scores = scores_of(query_heads, key_heads)
    probs = jnp.exp(scores - log_total[..., None])
    grad_probs = jnp.einsum(
        "qhd,khd->hqk", dout_heads, value_heads, preferred_element_type=jnp.float32
    )
    grad_scores = (probs * (grad_probs - delta[..., None])).astype(jnp.bfloat16)
    return (probs, grad_scores)


def attention_forward(query_heads, keys_all, values_all, block):
    count_rows, heads = (query_heads.shape[0], query_heads.shape[1])
    count = keys_all.shape[0] // block

    def stats_step(index, carry):
        run_top, run_total = carry
        scores = scores_of(query_heads, take_block(keys_all, index, block, heads))
        new_top = jnp.maximum(run_top, jnp.max(scores, axis=-1))
        run_total = run_total * jnp.exp(run_top - new_top) + jnp.sum(
            jnp.exp(scores - new_top[..., None]), axis=-1
        )
        return (new_top, run_total)

    start_top = jnp.full((heads, count_rows), -1e30, jnp.float32)
    start_total = jnp.zeros((heads, count_rows), jnp.float32)
    run_top, run_total = lax.fori_loop(0, count, stats_step, (start_top, start_total))
    log_total = run_top + jnp.log(run_total)

    def value_step(index, accum):
        scores = scores_of(query_heads, take_block(keys_all, index, block, heads))
        weights = jnp.exp(scores - log_total[..., None]).astype(jnp.bfloat16)
        return accum + jnp.einsum(
            "hqk,khd->qhd",
            weights,
            take_block(values_all, index, block, heads),
            preferred_element_type=jnp.float32,
        )

    accum = lax.fori_loop(0, count, value_step, jnp.zeros((count_rows, heads, HEAD), jnp.float32))
    return (accum.reshape(count_rows, heads * HEAD), log_total)


def adam_update(weight, grad, moment, second, rate, decay):
    moment_new = BETA_FIRST * moment + (1.0 - BETA_FIRST) * grad
    second_new = BETA_SECOND * second + (1.0 - BETA_SECOND) * grad * grad
    direction = (
        moment_new
        / (1.0 - BETA_FIRST**STEP)
        / (jnp.sqrt(second_new / (1.0 - BETA_SECOND**STEP)) + ADAM_EPSILON)
    )
    return (weight - rate * (direction + decay * weight), moment_new, second_new)


def on_device(
    tokens,
    cotangent,
    weight_qkv,
    weight_out,
    weight_up,
    weight_down,
    small_params,
    moment_qkv,
    moment_out,
    moment_up,
    moment_down,
    moment_small,
    second_qkv,
    second_out,
    second_up,
    second_down,
    second_small,
):
    rows = tokens[0]
    count_rows = rows.shape[0]
    width = rows.shape[1]
    heads = width // HEAD
    block = 4 * count_rows
    full_qkv, full_out, full_up, full_down, full_small = (
        lax.all_gather(weight_qkv.astype(jnp.bfloat16), ("dp", "seq"), axis=0, tiled=True),
        lax.all_gather(weight_out.astype(jnp.bfloat16), ("dp", "seq"), axis=0, tiled=True),
        lax.all_gather(weight_up.astype(jnp.bfloat16), ("dp", "seq"), axis=0, tiled=True),
        lax.all_gather(weight_down.astype(jnp.bfloat16), ("dp", "seq"), axis=0, tiled=True),
        lax.all_gather(small_params.astype(jnp.bfloat16), ("dp", "seq"), axis=0, tiled=True),
    )
    (
        bias_query,
        bias_value,
        bias_out,
        bias_up,
        bias_down,
        gain_one,
        shift_one,
        gain_two,
        shift_two,
    ) = unpack(full_small)
    projected = jnp.dot(rows, full_qkv, preferred_element_type=jnp.float32)
    query = (projected[:, :width] + bias_query).astype(jnp.bfloat16)
    key_rows = projected[:, width : 2 * width].astype(jnp.bfloat16)
    value_rows = (projected[:, 2 * width :] + bias_value).astype(jnp.bfloat16)
    keys_all, values_all = (
        lax.all_gather(key_rows, "seq", axis=0, tiled=True),
        lax.all_gather(value_rows, "seq", axis=0, tiled=True),
    )
    query_heads = query.reshape(count_rows, heads, HEAD)
    attended, log_total = attention_forward(query_heads, keys_all, values_all, block)
    attended_low = attended.astype(jnp.bfloat16)
    branch = jnp.dot(attended_low, full_out, preferred_element_type=jnp.float32) + bias_out
    middle = rows.astype(jnp.float32) + branch
    hidden, norm_one_back = jax.vjp(layer_norm, middle, gain_one, shift_one)
    hidden_low = hidden.astype(jnp.bfloat16)
    upward = jnp.dot(hidden_low, full_up, preferred_element_type=jnp.float32) + bias_up
    activation, gelu_back = jax.vjp(exact_gelu, upward)
    activation_low = activation.astype(jnp.bfloat16)
    downward = jnp.dot(activation_low, full_down, preferred_element_type=jnp.float32) + bias_down
    output, norm_two_back = jax.vjp(layer_norm, hidden + downward, gain_two, shift_two)
    back_qkv, back_out, back_up, back_down = (full_qkv, full_out, full_up, full_down)
    grad_sum_two, grad_gain_two, grad_shift_two = norm_two_back(cotangent[0].astype(jnp.float32))
    grad_down_low = grad_sum_two.astype(jnp.bfloat16)
    grad_bias_down = jnp.sum(grad_down_low.astype(jnp.float32), axis=0)
    grad_weight_down = cross(activation_low, grad_down_low)
    grad_activation = against(grad_down_low, back_down)
    grad_up_low = gelu_back(grad_activation)[0].astype(jnp.bfloat16)
    grad_bias_up = jnp.sum(grad_up_low.astype(jnp.float32), axis=0)
    grad_weight_up = cross(hidden_low, grad_up_low)
    grad_hidden = grad_sum_two + against(grad_up_low, back_up)
    grad_middle, grad_gain_one, grad_shift_one = norm_one_back(grad_hidden)
    grad_branch_low = grad_middle.astype(jnp.bfloat16)
    grad_bias_out = jnp.sum(grad_branch_low.astype(jnp.float32), axis=0)
    grad_weight_out = cross(attended_low, grad_branch_low)
    grad_attended = against(grad_branch_low, back_out).astype(jnp.bfloat16)
    delta = jnp.sum(
        (grad_attended.astype(jnp.float32) * attended).reshape(count_rows, heads, HEAD), axis=-1
    ).T
    dout_heads = grad_attended.reshape(count_rows, heads, HEAD)
    count = keys_all.shape[0] // block

    def both_step(index, carry):
        grad_query, grad_keys, grad_values = carry
        key_heads = take_block(keys_all, index, block, heads)
        value_heads = take_block(values_all, index, block, heads)
        probs, grad_scores = block_grads(
            query_heads, key_heads, value_heads, dout_heads, log_total, delta
        )
        grad_query = (
            grad_query
            + jnp.einsum("hqk,khd->qhd", grad_scores, key_heads, preferred_element_type=jnp.float32)
            * SCORE_SCALE
        )
        part_keys = (
            jnp.einsum("hqk,qhd->khd", grad_scores, query_heads, preferred_element_type=jnp.float32)
            * SCORE_SCALE
        )
        part_values = jnp.einsum(
            "hqk,qhd->khd",
            probs.astype(jnp.bfloat16),
            dout_heads,
            preferred_element_type=jnp.float32,
        )
        grad_keys = lax.dynamic_update_slice_in_dim(
            grad_keys, part_keys.reshape(block, width), index * block, 0
        )
        grad_values = lax.dynamic_update_slice_in_dim(
            grad_values, part_values.reshape(block, width), index * block, 0
        )
        return (grad_query, grad_keys, grad_values)

    start = (
        jnp.zeros((count_rows, heads, HEAD), jnp.float32),
        jnp.zeros((keys_all.shape[0], width), jnp.float32),
        jnp.zeros((keys_all.shape[0], width), jnp.float32),
    )
    grad_query, grad_keys, grad_values = lax.fori_loop(0, count, both_step, start)
    summed_keys, summed_values = (
        lax.psum_scatter(
            grad_keys.astype(jnp.bfloat16), "seq", scatter_dimension=0, tiled=True
        ).astype(jnp.float32),
        lax.psum_scatter(
            grad_values.astype(jnp.bfloat16), "seq", scatter_dimension=0, tiled=True
        ).astype(jnp.float32),
    )
    grad_query_low = grad_query.reshape(count_rows, width).astype(jnp.bfloat16)
    grad_value_low = summed_values.astype(jnp.bfloat16)
    grad_projected = jnp.concatenate(
        [grad_query_low, summed_keys.astype(jnp.bfloat16), grad_value_low], axis=1
    )
    grad_weight_qkv = cross(rows, grad_projected)
    grad_bias_query = jnp.sum(grad_query_low.astype(jnp.float32), axis=0)
    grad_bias_value = jnp.sum(grad_value_low.astype(jnp.float32), axis=0)
    grad_rows = grad_middle + against(grad_projected, back_qkv)
    ratio = full_up.shape[1] // width
    grad_small = jnp.concatenate(
        [
            jnp.stack([grad_bias_query, grad_bias_value, grad_bias_out], axis=1),
            grad_bias_up.reshape(ratio, width).T,
            jnp.stack(
                [grad_bias_down, grad_gain_one, grad_shift_one, grad_gain_two, grad_shift_two],
                axis=1,
            ),
        ],
        axis=1,
    )
    owned_qkv, owned_out, owned_up, owned_down, owned_small = (
        lax.psum_scatter(grad_weight_qkv, ("dp", "seq"), scatter_dimension=0, tiled=True),
        lax.psum_scatter(grad_weight_out, ("dp", "seq"), scatter_dimension=0, tiled=True),
        lax.psum_scatter(grad_weight_up, ("dp", "seq"), scatter_dimension=0, tiled=True),
        lax.psum_scatter(grad_weight_down, ("dp", "seq"), scatter_dimension=0, tiled=True),
        lax.psum_scatter(grad_small, ("dp", "seq"), scatter_dimension=0, tiled=True),
    )
    squares = jnp.sum(owned_qkv * owned_qkv) + jnp.sum(owned_out * owned_out)
    squares = squares + jnp.sum(owned_up * owned_up) + jnp.sum(owned_down * owned_down)
    squares = squares + jnp.sum(owned_small * owned_small)
    total = lax.psum(squares, ("dp", "seq"))
    grad_norm = jnp.sqrt(total)
    factor = jnp.minimum(1.0, CLIP_LIMIT / (grad_norm + 1e-06))
    new_qkv, new_moment_qkv, new_second_qkv = adam_update(
        weight_qkv, owned_qkv * factor, moment_qkv, second_qkv, RATE_MATRIX, WEIGHT_DECAY
    )
    new_out, new_moment_out, new_second_out = adam_update(
        weight_out, owned_out * factor, moment_out, second_out, RATE_OUTPUT, WEIGHT_DECAY
    )
    new_up, new_moment_up, new_second_up = adam_update(
        weight_up, owned_up * factor, moment_up, second_up, RATE_MATRIX, WEIGHT_DECAY
    )
    new_down, new_moment_down, new_second_down = adam_update(
        weight_down, owned_down * factor, moment_down, second_down, RATE_MATRIX, WEIGHT_DECAY
    )
    new_small, new_moment_small, new_second_small = adam_update(
        small_params, owned_small * factor, moment_small, second_small, RATE_SMALL, 0.0
    )
    return (
        output.astype(jnp.bfloat16)[None],
        grad_rows[None],
        grad_norm,
        new_qkv,
        new_out,
        new_up,
        new_down,
        new_small,
        new_moment_qkv,
        new_moment_out,
        new_moment_up,
        new_moment_down,
        new_moment_small,
        new_second_qkv,
        new_second_out,
        new_second_up,
        new_second_down,
        new_second_small,
    )


AXES = ("y", "x", "h", "l", "c")
LOW = jnp.bfloat16
WIDE = jnp.float32


def swap(value, axes):
    axes = tuple(name for name in AXES if name in axes)
    last = 2 ** len(axes) - 1
    return lax.ppermute(value, axes, [(i, i ^ last) for i in range(last + 1)])


def bit(name):
    return lax.axis_index(name)


def gather_square(value, a, b):
    half = value.shape[0] // 2
    from_a, from_b = swap(value, (a,)), swap(value, (b,))
    low_half = swap(from_a[:half], (b,))
    high_half = swap(from_b[half:], (a,))
    return [value, from_b, from_a, jnp.concatenate([low_half, high_half], axis=0)]


def gather_direct(value, a, b):
    return [value, swap(value, (b,)), swap(value, (a,)), swap(value, (a, b))]


def exchange_direct(parts, a, b):
    return [parts[0], swap(parts[1], (b,)), swap(parts[2], (a,)), swap(parts[3], (a, b))]


def scatter_square(parts, a, b):
    own, to_b, to_a, to_far = parts
    half = own.shape[0] // 2
    first = swap(to_far[:half].astype(LOW), (a,))
    second = swap(to_far[half:].astype(LOW), (b,))
    to_b = jnp.concatenate([to_b[:half] + first.astype(WIDE), to_b[half:]], axis=0)
    to_a = jnp.concatenate([to_a[:half], to_a[half:] + second.astype(WIDE)], axis=0)
    from_b = swap(to_b.astype(LOW), (b,))
    from_a = swap(to_a.astype(LOW), (a,))
    return own + from_b.astype(WIDE) + from_a.astype(WIDE)


def place(blocks, position, axis=0):
    size = blocks[0].shape[axis]
    shape = list(blocks[0].shape)
    shape[axis] = size * len(blocks)
    result = jnp.zeros(shape, blocks[0].dtype)
    for index, block in enumerate(blocks):
        result = lax.dynamic_update_slice_in_dim(result, block, (position ^ index) * size, axis)
    return result


def pick(value, position, count, axis=0):
    size = value.shape[axis] // count
    return [
        lax.dynamic_slice_in_dim(value, (position ^ index) * size, size, axis)
        for index in range(count)
    ]


def head_masks(shape, axis):
    lane = lax.broadcasted_iota(jnp.int32, shape, axis)
    return [lane < HEAD, lane >= HEAD]


def forward_kernel(q_ref, k_ref, v_ref, o_ref, lse_ref):
    queries, keys, values = q_ref[...], k_ref[...], v_ref[...]
    lanes = head_masks(queries.shape, 1)
    values_t = values.T
    zero = jnp.zeros_like(queries)
    outs = []
    for head in range(2):
        query = jnp.where(lanes[head], queries, zero)
        scores = against(keys, query) * SCORE_SCALE
        top = jnp.max(scores, axis=0, keepdims=True)
        weights = jnp.exp(scores - top)
        total = jnp.sum(weights, axis=0, keepdims=True)
        probs = (weights * (1.0 / total)).astype(LOW)
        lse_ref[head : head + 1, :] = top + jnp.log(total)
        outs.append(jnp.dot(values_t, probs, preferred_element_type=WIDE))
    rows = head_masks(outs[0].shape, 0)
    o_ref[...] = jnp.where(rows[0], outs[0], outs[1]).T.astype(LOW)


def attention(queries, keys, values, block=256):
    length, width = queries.shape
    whole = pl.BlockSpec((length, width), lambda i: (0, 0))
    part = pl.BlockSpec((block, width), lambda i: (i, 0))
    return pl.pallas_call(
        forward_kernel,
        grid=(length // block,),
        in_specs=[part, whole, whole],
        out_specs=[part, pl.BlockSpec((2, block), lambda i: (0, i))],
        out_shape=[
            jax.ShapeDtypeStruct((length, width), LOW),
            jax.ShapeDtypeStruct((2, length), WIDE),
        ],
        compiler_params=pltpu.CompilerParams(vmem_limit_bytes=40 * 2**20),
        cost_estimate=pl.CostEstimate(
            flops=16 * length * length * width, bytes_accessed=2**20, transcendentals=2 * length * length
        ),
    )(queries, keys, values)


def backward_kernel(q_ref, do_ref, k_ref, v_ref, lse_ref, dq_ref, dk_ref, dv_ref, dk_sum, dv_sum):
    step = pl.program_id(0)
    queries, douts, keys, values = q_ref[...], do_ref[...], k_ref[...], v_ref[...]
    lanes = head_masks(queries.shape, 1)
    keys_t = keys.T
    zero = jnp.zeros_like(queries)
    all_probs, all_grads, all_query, all_dout, outs = [], [], [], [], []
    for head in range(2):
        query = jnp.where(lanes[head], queries, zero)
        dout = jnp.where(lanes[head], douts, zero)
        scores = against(keys, query) * SCORE_SCALE
        probs = jnp.exp(scores - lse_ref[head : head + 1, :])
        grad_probs = against(values, dout)
        delta = jnp.sum(probs * grad_probs, axis=0, keepdims=True)
        grads = (probs * (grad_probs - delta)).astype(LOW)
        all_probs.append(probs.astype(LOW))
        all_grads.append(grads)
        all_query.append(query)
        all_dout.append(dout)
        outs.append(jnp.dot(keys_t, grads, preferred_element_type=WIDE))
    rows = head_masks(outs[0].shape, 0)
    dq_ref[...] = (jnp.where(rows[0], outs[0], outs[1]) * SCORE_SCALE).T.astype(LOW)
    part_keys = jnp.dot(
        jnp.concatenate(all_grads, axis=1),
        jnp.concatenate(all_query, axis=0),
        preferred_element_type=WIDE,
    )
    part_values = jnp.dot(
        jnp.concatenate(all_probs, axis=1),
        jnp.concatenate(all_dout, axis=0),
        preferred_element_type=WIDE,
    )

    @pl.when(step == 0)
    def _():
        dk_sum[...] = part_keys
        dv_sum[...] = part_values

    @pl.when(step > 0)
    def _():
        dk_sum[...] += part_keys
        dv_sum[...] += part_values

    @pl.when(step == pl.num_programs(0) - 1)
    def _():
        dk_ref[...] = (dk_sum[...] * SCORE_SCALE).astype(LOW)
        dv_ref[...] = dv_sum[...].astype(LOW)


def attention_back(queries, douts, keys, values, lse, block=256):
    length, width = queries.shape
    whole = pl.BlockSpec((length, width), lambda i: (0, 0))
    part = pl.BlockSpec((block, width), lambda i: (i, 0))
    return pl.pallas_call(
        backward_kernel,
        grid=(length // block,),
        in_specs=[part, part, whole, whole, pl.BlockSpec((2, block), lambda i: (0, i))],
        out_specs=[part, whole, whole],
        out_shape=[jax.ShapeDtypeStruct((length, width), LOW)] * 3,
        scratch_shapes=[pltpu.VMEM((length, width), WIDE)] * 2,
        compiler_params=pltpu.CompilerParams(vmem_limit_bytes=40 * 2**20),
        cost_estimate=pl.CostEstimate(
            flops=40 * length * length * width, bytes_accessed=2**21, transcendentals=2 * length * length
        ),
    )(queries, douts, keys, values, lse)


def on_square(
    tokens,
    cotangent,
    weight_qkv,
    weight_out,
    weight_up,
    weight_down,
    small_params,
    moment_qkv,
    moment_out,
    moment_up,
    moment_down,
    moment_small,
    second_qkv,
    second_out,
    second_up,
    second_down,
    second_small,
):
    rows = tokens[0]
    count, width = rows.shape
    own = weight_qkv.shape[0]
    ratio = weight_up.shape[1] // width
    columns = small_params.shape[1]
    part = width // 8
    units = weight_up.shape[1] // 8
    iy, ix, ih, il, ic = (bit(name) for name in AXES)
    at_seq = 4 * ih + 2 * il + ic
    at_z = 2 * ih + il
    at_dp = 2 * iy + ix
    at_yh = 2 * iy + ih

    mine = gather_direct(rows, "h", "l")
    lead = jnp.concatenate(mine, axis=0)
    tokens_all = jnp.concatenate([lead, swap(lead, ("c",))], axis=0)

    low_qkv = weight_qkv.astype(LOW).reshape(own, 3, 8, part).transpose(2, 0, 1, 3)
    low_qkv = low_qkv.reshape(8, own, 3 * part)
    low_small = small_params.astype(LOW).reshape(1, 1, own * columns)
    low_small = jnp.broadcast_to(low_small, (8, 8, own * columns))
    packed = jnp.concatenate([low_qkv, low_small], axis=1)
    packed = lax.all_to_all(packed, ("h", "l", "c"), 0, 0, tiled=True)
    packed = place(gather_square(packed, "y", "x"), at_dp)
    full_qkv = packed[:, :own].reshape(width, 3 * part)
    table = packed[:, own].astype(WIDE).reshape(width, columns)
    (
        bias_query,
        bias_value,
        bias_out,
        bias_up,
        bias_down,
        gain_one,
        shift_one,
        gain_two,
        shift_two,
    ) = unpack(table)

    full_out = lax.all_gather(weight_out.astype(LOW), AXES, axis=0, tiled=True)

    low_up = weight_up.astype(LOW).reshape(own, 2, 2, 2, 4, units // 4)
    low_up = low_up.transpose(2, 4, 0, 1, 3, 5).reshape(8, own, units)
    low_up = lax.all_to_all(low_up, ("x", "l", "c"), 0, 0, tiled=True)
    up_blocks = gather_square(low_up, "y", "h")
    full_up = jnp.zeros((2, 2, 2, 4 * own, units), LOW)
    for index, block in enumerate(up_blocks):
        block = block.reshape(1, 2, 1, 4 * own, units)
        full_up = lax.dynamic_update_slice(
            full_up, block, (iy ^ (index // 2), 0, ih ^ (index % 2), 0, 0)
        )
    full_up = full_up.reshape(width, units)
    full_down = place(gather_square(weight_down.astype(LOW), "y", "h"), at_yh)

    take = lambda vector: lax.dynamic_slice_in_dim(vector, at_seq * part, part)
    projected = jnp.dot(tokens_all, full_qkv, preferred_element_type=WIDE)
    query = (projected[:, :part] + take(bias_query)).astype(LOW)
    keys = projected[:, part : 2 * part].astype(LOW)
    values = (projected[:, 2 * part :] + take(bias_value)).astype(LOW)
    attended_mine, lse = attention(query, keys, values)

    near, far = attended_mine[: 4 * count], attended_mine[4 * count :]
    far = swap(far, ("c",))
    both = place([near, far], ic, axis=1).reshape(4, count, 2 * part)
    sources = exchange_direct([both[0], both[1], both[2], both[3]], "h", "l")
    attended = place(sources, at_z, axis=1)

    branch = jnp.dot(attended, full_out, preferred_element_type=WIDE) + bias_out
    middle = rows.astype(WIDE) + branch
    hidden, norm_one_back = jax.vjp(layer_norm, middle, gain_one, shift_one)

    def gather_group(value):
        lead = jnp.concatenate(gather_square(value, "x", "l"), axis=0)
        return jnp.concatenate([lead, swap(lead, ("c",))], axis=0)

    def scatter_group(partial):
        near = partial[: 4 * count] + swap(partial[4 * count :].astype(LOW), ("c",)).astype(WIDE)
        return scatter_square([near[i * count : (i + 1) * count] for i in range(4)], "x", "l")

    hidden_all = gather_group(hidden.astype(LOW))
    bias_units = bias_up.reshape(2, 2, 2, 4, units // 4)
    bias_units = lax.dynamic_slice(
        bias_units, (0, ix, 0, 2 * il + ic, 0), (2, 1, 2, 1, units // 4)
    ).reshape(units)
    upward = jnp.dot(hidden_all, full_up, preferred_element_type=WIDE) + bias_units
    activation, gelu_back = jax.vjp(exact_gelu, upward)
    activation_low = activation.astype(LOW)
    downward = scatter_group(jnp.dot(activation_low, full_down, preferred_element_type=WIDE))
    output, norm_two_back = jax.vjp(
        layer_norm, hidden + (downward + bias_down), gain_two, shift_two
    )

    grad_sum_two, grad_gain_two, grad_shift_two = norm_two_back(cotangent[0].astype(WIDE))
    grad_down_low = grad_sum_two.astype(LOW)
    grad_bias_down = jnp.sum(grad_down_low.astype(WIDE), axis=0)
    grad_down_all = gather_group(grad_down_low)
    grad_activation = against(grad_down_all, full_down)
    grad_up_low = gelu_back(grad_activation)[0].astype(LOW)
    grad_hidden = grad_sum_two + scatter_group(against(grad_up_low, full_up))
    part_down = cross(activation_low, grad_down_all)
    part_up = cross(hidden_all, grad_up_low)
    grad_bias_up = jnp.sum(grad_up_low.astype(WIDE), axis=0)
    owned_down = scatter_square(pick(part_down, at_yh, 4), "y", "h")
    part_up = part_up.reshape(2, 2, 2, 4 * own, units)
    up_parts = [
        lax.dynamic_slice(
            part_up, (iy ^ (i // 2), 0, ih ^ (i % 2), 0, 0), (1, 2, 1, 4 * own, units)
        ).reshape(8 * own, units)
        for i in range(4)
    ]
    owned_up = scatter_square(up_parts, "y", "h").astype(LOW).reshape(8, own, units)
    owned_up = lax.all_to_all(owned_up, ("x", "l", "c"), 0, 0, tiled=True)
    owned_up = owned_up.reshape(2, 4, own, 2, 2, units // 4).transpose(2, 3, 0, 4, 1, 5)
    owned_up = owned_up.reshape(own, 8 * units).astype(WIDE)

    grad_middle, grad_gain_one, grad_shift_one = norm_one_back(grad_hidden)
    grad_branch_low = grad_middle.astype(LOW)
    grad_bias_out = jnp.sum(grad_branch_low.astype(WIDE), axis=0)
    grad_attended = against(grad_branch_low, full_out).astype(LOW)
    sources = exchange_direct(pick(grad_attended, at_z, 4, axis=1), "h", "l")
    both = jnp.concatenate(sources, axis=0)
    near, far = pick(both, ic, 2, axis=1)
    dout = jnp.concatenate([near, swap(far, ("c",))], axis=0)

    grad_query, grad_keys, grad_values = attention_back(query, dout, keys, values, lse)
    grad_projected = jnp.concatenate([grad_query, grad_keys, grad_values], axis=1)
    part_qkv = cross(tokens_all, grad_projected)
    owned_qkv = scatter_square(pick(part_qkv, at_dp, 4), "y", "x")
    owned_qkv = owned_qkv.astype(LOW).reshape(8, own, 3 * part)
    owned_qkv = lax.all_to_all(owned_qkv, ("h", "l", "c"), 0, 0, tiled=True)
    owned_qkv = owned_qkv.reshape(8, own, 3, part).transpose(1, 2, 0, 3)
    owned_qkv = owned_qkv.reshape(own, 3 * width).astype(WIDE)

    part_out = cross(attended, grad_branch_low).reshape(16, 2, own, width)
    out_near, out_far = pick(part_out, ic, 2, axis=1)
    out_near = out_near + swap(out_far.astype(LOW), ("c",)).astype(WIDE)
    out_near = scatter_square(pick(out_near.reshape(16 * own, width), at_dp, 4), "y", "x")
    pieces = exchange_direct(
        [piece.astype(LOW) for piece in pick(out_near, at_z, 4)], "h", "l"
    )
    owned_out = sum(piece.astype(WIDE) for piece in pieces)

    part_rows = against(grad_projected, full_qkv)
    near = part_rows[: 4 * count] + swap(part_rows[4 * count :].astype(LOW), ("c",)).astype(WIDE)
    near = near.astype(LOW)
    pieces = exchange_direct([near[i * count : (i + 1) * count] for i in range(4)], "h", "l")
    grad_rows = grad_middle + sum(piece.astype(WIDE) for piece in pieces)

    blank = jnp.zeros((width,), WIDE)
    put = lambda vector: lax.dynamic_update_slice_in_dim(blank, vector, at_seq * part, 0)
    row_query = put(jnp.sum(grad_query.astype(WIDE), axis=0))
    row_value = put(jnp.sum(grad_values.astype(WIDE), axis=0))
    rows_up = lax.dynamic_update_slice(
        jnp.zeros((2, 2, 2, 4, units // 4), WIDE),
        grad_bias_up.reshape(2, 1, 2, 1, units // 4),
        (0, ix, 0, 2 * il + ic, 0),
    ).reshape(ratio, width)
    small = jnp.concatenate(
        [
            jnp.stack([row_query, row_value, grad_bias_out]),
            rows_up,
            jnp.stack([grad_bias_down, grad_gain_one, grad_shift_one, grad_gain_two, grad_shift_two]),
        ]
    )
    for name in ("c", "x", "y", "l", "h"):
        small = small + swap(small, (name,))
    at_all = 8 * at_dp + at_seq
    owned_small = lax.dynamic_slice_in_dim(small, at_all * own, own, axis=1).T

    squares = jnp.sum(owned_qkv * owned_qkv) + jnp.sum(owned_out * owned_out)
    squares = squares + jnp.sum(owned_up * owned_up) + jnp.sum(owned_down * owned_down)
    squares = squares + jnp.sum(owned_small * owned_small)
    total = jnp.broadcast_to(squares, (8, 128))
    for name in ("c", "x", "y", "l", "h"):
        total = total + swap(total, (name,))
    grad_norm = jnp.sqrt(total[0, 0])
    factor = jnp.minimum(1.0, CLIP_LIMIT / (grad_norm + 1e-06))
    new_qkv, new_moment_qkv, new_second_qkv = adam_update(
        weight_qkv, owned_qkv * factor, moment_qkv, second_qkv, RATE_MATRIX, WEIGHT_DECAY
    )
    new_out, new_moment_out, new_second_out = adam_update(
        weight_out, owned_out * factor, moment_out, second_out, RATE_OUTPUT, WEIGHT_DECAY
    )
    new_up, new_moment_up, new_second_up = adam_update(
        weight_up, owned_up * factor, moment_up, second_up, RATE_MATRIX, WEIGHT_DECAY
    )
    new_down, new_moment_down, new_second_down = adam_update(
        weight_down, owned_down * factor, moment_down, second_down, RATE_MATRIX, WEIGHT_DECAY
    )
    new_small, new_moment_small, new_second_small = adam_update(
        small_params, owned_small * factor, moment_small, second_small, RATE_SMALL, 0.0
    )
    return (
        output.astype(jnp.bfloat16)[None],
        grad_rows[None],
        grad_norm,
        new_qkv,
        new_out,
        new_up,
        new_down,
        new_small,
        new_moment_qkv,
        new_moment_out,
        new_moment_up,
        new_moment_down,
        new_moment_small,
        new_second_qkv,
        new_second_out,
        new_second_up,
        new_second_down,
        new_second_small,
    )


def solution(mesh):
    sizes = (mesh.shape["dp"], mesh.shape["seq"])
    if sizes == (4, 8):
        squares = Mesh(mesh.devices.reshape(2, 2, 2, 2, 2), AXES)
        dp, seq = ("y", "x"), ("h", "l", "c")
        body, mesh = on_square, squares
        every = P(AXES, None)
        over = P(dp, seq, None)
    else:
        body = on_device
        every = P(("dp", "seq"), None)
        over = P("dp", "seq", None)
    return jax.shard_map(
        body,
        mesh=mesh,
        in_specs=(over,) * 2 + (every,) * 15,
        out_specs=(over,) * 2 + (P(),) + (every,) * 15,
        check_vma=False,
    )
```

```python
import functools
import math

import jax
import jax.numpy as jnp
from jax import lax
from jax.experimental import pallas as pl
from jax.experimental.pallas import tpu as pltpu
from jax.sharding import Mesh
from jax.sharding import PartitionSpec as P

HEAD = 64
STEP = 5


NORM_EPSILON = 1e-05
ADAM_EPSILON = 1e-08
BETA_FIRST = 0.5
BETA_SECOND = 0.55
CLIP_LIMIT = 1.0
RATE_MATRIX = 0.04
RATE_OUTPUT = 0.5
RATE_SMALL = 0.3
WEIGHT_DECAY = 0.01
SCORE_SCALE = 0.125


def layer_norm(value, gain, shift):
    center = jnp.mean(value, axis=-1, keepdims=True)
    centered = value - center
    variance = jnp.mean(centered * centered, axis=-1, keepdims=True)
    return centered * lax.rsqrt(variance + NORM_EPSILON) * gain + shift


def exact_gelu(value):
    return jax.nn.gelu(value, approximate=False)


def unpack(table_low):
    table = table_low.astype(jnp.float32)
    ratio = table.shape[1] - 8
    bias_up = table[:, 3 : 3 + ratio].T.reshape(-1)
    return (
        table[:, 0],
        table[:, 1],
        table[:, 2],
        bias_up,
        table[:, 3 + ratio],
        table[:, 4 + ratio],
        table[:, 5 + ratio],
        table[:, 6 + ratio],
        table[:, 7 + ratio],
    )


def cross(left, right):
    return lax.dot_general(
        left, right, (((0,), (0,)), ((), ())), preferred_element_type=jnp.float32
    )


def against(left, right):
    return lax.dot_general(
        left, right, (((1,), (1,)), ((), ())), preferred_element_type=jnp.float32
    )


def take_block(source, index, block, heads):
    piece = lax.dynamic_slice_in_dim(source, index * block, block, 0)
    return piece.reshape(block, heads, HEAD)


def scores_of(query_heads, key_heads):
    return (
        jnp.einsum("qhd,khd->hqk", query_heads, key_heads, preferred_element_type=jnp.float32)
        * SCORE_SCALE
    )


def block_grads(query_heads, key_heads, value_heads, dout_heads, log_total, delta):
    scores = scores_of(query_heads, key_heads)
    probs = jnp.exp(scores - log_total[..., None])
    grad_probs = jnp.einsum(
        "qhd,khd->hqk", dout_heads, value_heads, preferred_element_type=jnp.float32
    )
    grad_scores = (probs * (grad_probs - delta[..., None])).astype(jnp.bfloat16)
    return (probs, grad_scores)


def attention_forward(query_heads, keys_all, values_all, block):
    count_rows, heads = (query_heads.shape[0], query_heads.shape[1])
    count = keys_all.shape[0] // block

    def stats_step(index, carry):
        run_top, run_total = carry
        scores = scores_of(query_heads, take_block(keys_all, index, block, heads))
        new_top = jnp.maximum(run_top, jnp.max(scores, axis=-1))
        run_total = run_total * jnp.exp(run_top - new_top) + jnp.sum(
            jnp.exp(scores - new_top[..., None]), axis=-1
        )
        return (new_top, run_total)

    start_top = jnp.full((heads, count_rows), -1e30, jnp.float32)
    start_total = jnp.zeros((heads, count_rows), jnp.float32)
    run_top, run_total = lax.fori_loop(0, count, stats_step, (start_top, start_total))
    log_total = run_top + jnp.log(run_total)

    def value_step(index, accum):
        scores = scores_of(query_heads, take_block(keys_all, index, block, heads))
        weights = jnp.exp(scores - log_total[..., None]).astype(jnp.bfloat16)
        return accum + jnp.einsum(
            "hqk,khd->qhd",
            weights,
            take_block(values_all, index, block, heads),
            preferred_element_type=jnp.float32,
        )

    accum = lax.fori_loop(0, count, value_step, jnp.zeros((count_rows, heads, HEAD), jnp.float32))
    return (accum.reshape(count_rows, heads * HEAD), log_total)


def adam_update(weight, grad, moment, second, rate, decay):
    moment_new = BETA_FIRST * moment + (1.0 - BETA_FIRST) * grad
    second_new = BETA_SECOND * second + (1.0 - BETA_SECOND) * grad * grad
    direction = (
        moment_new
        / (1.0 - BETA_FIRST**STEP)
        / (jnp.sqrt(second_new / (1.0 - BETA_SECOND**STEP)) + ADAM_EPSILON)
    )
    return (weight - rate * (direction + decay * weight), moment_new, second_new)


def on_device(
    tokens,
    cotangent,
    weight_qkv,
    weight_out,
    weight_up,
    weight_down,
    small_params,
    moment_qkv,
    moment_out,
    moment_up,
    moment_down,
    moment_small,
    second_qkv,
    second_out,
    second_up,
    second_down,
    second_small,
):
    rows = tokens[0]
    count_rows = rows.shape[0]
    width = rows.shape[1]
    heads = width // HEAD
    block = 4 * count_rows
    full_qkv, full_out, full_up, full_down, full_small = (
        lax.all_gather(weight_qkv.astype(jnp.bfloat16), ("dp", "seq"), axis=0, tiled=True),
        lax.all_gather(weight_out.astype(jnp.bfloat16), ("dp", "seq"), axis=0, tiled=True),
        lax.all_gather(weight_up.astype(jnp.bfloat16), ("dp", "seq"), axis=0, tiled=True),
        lax.all_gather(weight_down.astype(jnp.bfloat16), ("dp", "seq"), axis=0, tiled=True),
        lax.all_gather(small_params.astype(jnp.bfloat16), ("dp", "seq"), axis=0, tiled=True),
    )
    (
        bias_query,
        bias_value,
        bias_out,
        bias_up,
        bias_down,
        gain_one,
        shift_one,
        gain_two,
        shift_two,
    ) = unpack(full_small)
    projected = jnp.dot(rows, full_qkv, preferred_element_type=jnp.float32)
    query = (projected[:, :width] + bias_query).astype(jnp.bfloat16)
    key_rows = projected[:, width : 2 * width].astype(jnp.bfloat16)
    value_rows = (projected[:, 2 * width :] + bias_value).astype(jnp.bfloat16)
    keys_all, values_all = (
        lax.all_gather(key_rows, "seq", axis=0, tiled=True),
        lax.all_gather(value_rows, "seq", axis=0, tiled=True),
    )
    query_heads = query.reshape(count_rows, heads, HEAD)
    attended, log_total = attention_forward(query_heads, keys_all, values_all, block)
    attended_low = attended.astype(jnp.bfloat16)
    branch = jnp.dot(attended_low, full_out, preferred_element_type=jnp.float32) + bias_out
    middle = rows.astype(jnp.float32) + branch
    hidden, norm_one_back = jax.vjp(layer_norm, middle, gain_one, shift_one)
    hidden_low = hidden.astype(jnp.bfloat16)
    upward = jnp.dot(hidden_low, full_up, preferred_element_type=jnp.float32) + bias_up
    activation, gelu_back = jax.vjp(exact_gelu, upward)
    activation_low = activation.astype(jnp.bfloat16)
    downward = jnp.dot(activation_low, full_down, preferred_element_type=jnp.float32) + bias_down
    output, norm_two_back = jax.vjp(layer_norm, hidden + downward, gain_two, shift_two)
    back_qkv, back_out, back_up, back_down = (full_qkv, full_out, full_up, full_down)
    grad_sum_two, grad_gain_two, grad_shift_two = norm_two_back(cotangent[0].astype(jnp.float32))
    grad_down_low = grad_sum_two.astype(jnp.bfloat16)
    grad_bias_down = jnp.sum(grad_down_low.astype(jnp.float32), axis=0)
    grad_weight_down = cross(activation_low, grad_down_low)
    grad_activation = against(grad_down_low, back_down)
    grad_up_low = gelu_back(grad_activation)[0].astype(jnp.bfloat16)
    grad_bias_up = jnp.sum(grad_up_low.astype(jnp.float32), axis=0)
    grad_weight_up = cross(hidden_low, grad_up_low)
    grad_hidden = grad_sum_two + against(grad_up_low, back_up)
    grad_middle, grad_gain_one, grad_shift_one = norm_one_back(grad_hidden)
    grad_branch_low = grad_middle.astype(jnp.bfloat16)
    grad_bias_out = jnp.sum(grad_branch_low.astype(jnp.float32), axis=0)
    grad_weight_out = cross(attended_low, grad_branch_low)
    grad_attended = against(grad_branch_low, back_out).astype(jnp.bfloat16)
    delta = jnp.sum(
        (grad_attended.astype(jnp.float32) * attended).reshape(count_rows, heads, HEAD), axis=-1
    ).T
    dout_heads = grad_attended.reshape(count_rows, heads, HEAD)
    count = keys_all.shape[0] // block

    def both_step(index, carry):
        grad_query, grad_keys, grad_values = carry
        key_heads = take_block(keys_all, index, block, heads)
        value_heads = take_block(values_all, index, block, heads)
        probs, grad_scores = block_grads(
            query_heads, key_heads, value_heads, dout_heads, log_total, delta
        )
        grad_query = (
            grad_query
            + jnp.einsum("hqk,khd->qhd", grad_scores, key_heads, preferred_element_type=jnp.float32)
            * SCORE_SCALE
        )
        part_keys = (
            jnp.einsum("hqk,qhd->khd", grad_scores, query_heads, preferred_element_type=jnp.float32)
            * SCORE_SCALE
        )
        part_values = jnp.einsum(
            "hqk,qhd->khd",
            probs.astype(jnp.bfloat16),
            dout_heads,
            preferred_element_type=jnp.float32,
        )
        grad_keys = lax.dynamic_update_slice_in_dim(
            grad_keys, part_keys.reshape(block, width), index * block, 0
        )
        grad_values = lax.dynamic_update_slice_in_dim(
            grad_values, part_values.reshape(block, width), index * block, 0
        )
        return (grad_query, grad_keys, grad_values)

    start = (
        jnp.zeros((count_rows, heads, HEAD), jnp.float32),
        jnp.zeros((keys_all.shape[0], width), jnp.float32),
        jnp.zeros((keys_all.shape[0], width), jnp.float32),
    )
    grad_query, grad_keys, grad_values = lax.fori_loop(0, count, both_step, start)
    summed_keys, summed_values = (
        lax.psum_scatter(
            grad_keys.astype(jnp.bfloat16), "seq", scatter_dimension=0, tiled=True
        ).astype(jnp.float32),
        lax.psum_scatter(
            grad_values.astype(jnp.bfloat16), "seq", scatter_dimension=0, tiled=True
        ).astype(jnp.float32),
    )
    grad_query_low = grad_query.reshape(count_rows, width).astype(jnp.bfloat16)
    grad_value_low = summed_values.astype(jnp.bfloat16)
    grad_projected = jnp.concatenate(
        [grad_query_low, summed_keys.astype(jnp.bfloat16), grad_value_low], axis=1
    )
    grad_weight_qkv = cross(rows, grad_projected)
    grad_bias_query = jnp.sum(grad_query_low.astype(jnp.float32), axis=0)
    grad_bias_value = jnp.sum(grad_value_low.astype(jnp.float32), axis=0)
    grad_rows = grad_middle + against(grad_projected, back_qkv)
    ratio = full_up.shape[1] // width
    grad_small = jnp.concatenate(
        [
            jnp.stack([grad_bias_query, grad_bias_value, grad_bias_out], axis=1),
            grad_bias_up.reshape(ratio, width).T,
            jnp.stack(
                [grad_bias_down, grad_gain_one, grad_shift_one, grad_gain_two, grad_shift_two],
                axis=1,
            ),
        ],
        axis=1,
    )
    owned_qkv, owned_out, owned_up, owned_down, owned_small = (
        lax.psum_scatter(grad_weight_qkv, ("dp", "seq"), scatter_dimension=0, tiled=True),
        lax.psum_scatter(grad_weight_out, ("dp", "seq"), scatter_dimension=0, tiled=True),
        lax.psum_scatter(grad_weight_up, ("dp", "seq"), scatter_dimension=0, tiled=True),
        lax.psum_scatter(grad_weight_down, ("dp", "seq"), scatter_dimension=0, tiled=True),
        lax.psum_scatter(grad_small, ("dp", "seq"), scatter_dimension=0, tiled=True),
    )
    squares = jnp.sum(owned_qkv * owned_qkv) + jnp.sum(owned_out * owned_out)
    squares = squares + jnp.sum(owned_up * owned_up) + jnp.sum(owned_down * owned_down)
    squares = squares + jnp.sum(owned_small * owned_small)
    total = lax.psum(squares, ("dp", "seq"))
    grad_norm = jnp.sqrt(total)
    factor = jnp.minimum(1.0, CLIP_LIMIT / (grad_norm + 1e-06))
    new_qkv, new_moment_qkv, new_second_qkv = adam_update(
        weight_qkv, owned_qkv * factor, moment_qkv, second_qkv, RATE_MATRIX, WEIGHT_DECAY
    )
    new_out, new_moment_out, new_second_out = adam_update(
        weight_out, owned_out * factor, moment_out, second_out, RATE_OUTPUT, WEIGHT_DECAY
    )
    new_up, new_moment_up, new_second_up = adam_update(
        weight_up, owned_up * factor, moment_up, second_up, RATE_MATRIX, WEIGHT_DECAY
    )
    new_down, new_moment_down, new_second_down = adam_update(
        weight_down, owned_down * factor, moment_down, second_down, RATE_MATRIX, WEIGHT_DECAY
    )
    new_small, new_moment_small, new_second_small = adam_update(
        small_params, owned_small * factor, moment_small, second_small, RATE_SMALL, 0.0
    )
    return (
        output.astype(jnp.bfloat16)[None],
        grad_rows[None],
        grad_norm,
        new_qkv,
        new_out,
        new_up,
        new_down,
        new_small,
        new_moment_qkv,
        new_moment_out,
        new_moment_up,
        new_moment_down,
        new_moment_small,
        new_second_qkv,
        new_second_out,
        new_second_up,
        new_second_down,
        new_second_small,
    )


AXES = ("y", "x", "h", "l", "c")
LOW = jnp.bfloat16
WIDE = jnp.float32


def swap(value, axes):
    axes = tuple(name for name in AXES if name in axes)
    last = 2 ** len(axes) - 1
    return lax.ppermute(value, axes, [(i, i ^ last) for i in range(last + 1)])


def after(value, *events):
    return lax.optimization_barrier((value, *events))[0]


def send(value, axes, start=(), use=()):
    got = swap(after(value, *start) if start else value, axes)
    return after(got, *use) if use else got


def exchange(parts, a, b, start=(), use=()):
    ways = ((b,), (a,), (a, b))
    return [parts[0]] + [send(part, way, start, use) for part, way in zip(parts[1:], ways)]


def gather_square(value, a, b):
    half = value.shape[0] // 2
    from_a, from_b = swap(value, (a,)), swap(value, (b,))
    return [value, from_b, from_a, swap(from_a[:half], (b,)), swap(from_b[half:], (a,))]


def scatter_square(parts, a, b):
    own, to_b, to_a, far_first, far_second = parts
    half = own.shape[0] // 2
    first = swap(far_first, (a,))
    second = swap(far_second, (b,))
    to_b = jnp.concatenate([to_b[:half] + first.astype(WIDE), to_b[half:]], axis=0).astype(LOW)
    to_a = jnp.concatenate([to_a[:half], to_a[half:] + second.astype(WIDE)], axis=0).astype(LOW)
    return own, swap(to_b, (b,)), swap(to_a, (a,))


def gather_ring(value, a, b, start=(), use=()):
    from_b = send(value, (b,), start, use)
    from_a = swap(after(value, *start) if start else value, (a,))
    far = send(from_a, (b,), use=use)
    return [value, from_b, after(from_a, *use) if use else from_a, far]


def dot(left, right):
    return jnp.dot(left, right, preferred_element_type=WIDE)


def call(kernel, outs, *args, scratch=(), flops=10**9, scalars=0):
    outs = [jax.ShapeDtypeStruct(shape, kind) for shape, kind in outs]
    return pl.pallas_call(
        kernel,
        name=getattr(kernel, "func", kernel).__name__,
        in_specs=[pl.BlockSpec(memory_space=pltpu.SMEM)] * (1 + scalars)
        + [pl.BlockSpec(memory_space=pltpu.VMEM)] * (len(args) - 1 - scalars),
        out_specs=[pl.BlockSpec(memory_space=pltpu.VMEM)] * len(outs),
        out_shape=outs,
        scratch_shapes=list(scratch),
        compiler_params=pltpu.CompilerParams(vmem_limit_bytes=48 * 2**20),
        cost_estimate=pl.CostEstimate(flops=1, bytes_accessed=1, transcendentals=0),
    )(*args)


def at(start, size):
    return pl.ds(pl.multiple_of(start, size), size)


def indices(bits):
    iy, ix, ih, il, ic = (bits[i] for i in range(5))
    return 2 * iy + ix, 2 * ih + il, ic


def pack_qkv_kernel(bits, weight, small, *outs):
    _, z, _ = indices(bits)
    own = weight.shape[0]
    size = outs[0].shape[1] // 3
    for r, out in enumerate(outs):
        for kind in range(3):
            start = kind * 4 * size + (z ^ r) * size
            out[:own, kind * size : (kind + 1) * size] = weight[:, at(start, size)].astype(LOW)
        out[own:, :] = small[...]


def pack_rest_kernel(bits, out_weight, up, down, low_out, low_down, near_up, far_up):
    iy, ix, ih, il, ic = (bits[i] for i in range(5))
    own = up.shape[0]
    size = up.shape[1] // 16
    low_out[...] = out_weight[...].astype(LOW)
    low_down[...] = down[...].astype(LOW)
    for r in range(4):
        out, rows = (near_up, far_up)[r // 2], slice(r % 2 * own, (r % 2 + 1) * own)
        x, l = ix ^ (r // 2), il ^ (r % 2)
        for y in range(2):
            for h in range(2):
                start = (((y * 2 + x) * 2 + h) * 2 + l) * size
                to = (y * 2 + h) * size
                out[rows, to : to + size] = up[:, at(start, size)].astype(LOW)


def lay_rows(bits, full, pieces, own, stride, c):
    d, z, _ = indices(bits)
    for p, piece in enumerate(pieces):
        for s in range(4):
            to = (d ^ p) * 8 * own + (z ^ s) * 2 * own + c * own
            full[at(to, own), :] = piece[s * stride : s * stride + own, :]


def lay_qkv_kernel(bits, near, far, full):
    own = full.shape[0] // 32
    stride = near.shape[0] // 16
    c = bits[4]
    for ref, core in ((near, c), (far, 1 - c)):
        pieces = [ref.at[p * 4 * stride : (p + 1) * 4 * stride] for p in range(4)]
        lay_rows(bits, full, pieces, own, stride, core)


def lay_feed_kernel(bits, near, far, full_up, full_down):
    iy, ix, ih, il, ic = (bits[i] for i in range(5))
    own = full_up.shape[0] // 32
    size = full_down.shape[0] // 8
    for ref, core in ((near, ic), (far, 1 - ic)):
        for p in range(4):
            y, h = iy ^ (p // 2), ih ^ (p % 2)
            base = p * (4 * own + size)
            for q in range(4):
                x, l = ix ^ (q // 2), il ^ (q % 2)
                to = ((((y * 2 + x) * 2 + h) * 2 + l) * 2 + core) * own
                full_up[at(to, own), :] = ref[base + q * own : base + (q + 1) * own, :]
            start = base + 4 * own
            to = ((y * 2 + h) * 2 + core) * size
            full_down[at(to, size), :] = ref[start : start + size, :]


def project_kernel(bits, t0, t1, t2, t3, weight, bias, q_ref, kv_ref):
    tokens = jnp.concatenate([t0[...], t1[...], t2[...], t3[...]], axis=0)
    size = q_ref.shape[1]
    projected = dot(tokens, weight[...])
    q_ref[...] = (projected[:, :size] + bias[0:1, :]).astype(LOW)
    kv_ref[:, :size] = projected[:, size : 2 * size].astype(LOW)
    kv_ref[:, size:] = (projected[:, 2 * size :] + bias[1:2, :]).astype(LOW)


def head_mask(shape, axis, head):
    lane = lax.broadcasted_iota(jnp.int32, shape, axis)
    return (lane < HEAD) if head == 0 else (lane >= HEAD)


def forward_kernel(bits, q_ref, near, far, *outs):
    lse_ref = outs[-1]
    count = outs[0].shape[0]
    width = q_ref.shape[1]
    pair = 2 * HEAD
    for group in range(width // pair):
        cols = slice(group * pair, (group + 1) * pair)
        value_cols = slice(width + group * pair, width + (group + 1) * pair)
        keys = jnp.concatenate([near[:, cols], far[:, cols]], axis=0)
        values_t = jnp.concatenate([near[:, value_cols], far[:, value_cols]], axis=0).T
        for piece in range(2):
            rows = slice(2 * piece * count, 2 * (piece + 1) * count)
            queries = q_ref[rows, cols]
            zero = jnp.zeros_like(queries)
            halves = []
            for head in range(2):
                query = jnp.where(head_mask(queries.shape, 1, head), queries, zero)
                scores = against(keys, query) * SCORE_SCALE
                top = jnp.max(scores, axis=0, keepdims=True)
                weights = jnp.exp(scores - top)
                total = jnp.sum(weights, axis=0, keepdims=True)
                at_head = 2 * group + head
                lse_ref[at_head : at_head + 1, rows] = top + jnp.log(total)
                probs = (weights * (1.0 / total)).astype(LOW)
                halves.append(dot(values_t, probs))
            mask = head_mask(halves[0].shape, 0, 0)
            result = jnp.where(mask, halves[0], halves[1]).T.astype(LOW)
            outs[2 * piece][:, cols] = result[:count]
            outs[2 * piece + 1][:, cols] = result[count:]


def backward_kernel(
    bits, q_ref, near, far, lse_ref, d0, d1, d2, d3, dq_ref, near_ref, far_ref, sums
):
    count = d0.shape[0]
    length = 2 * near.shape[0]
    width = q_ref.shape[1]
    pair = 2 * HEAD
    for group in range(width // pair):
        cols = slice(group * pair, (group + 1) * pair)
        value_cols = slice(width + group * pair, width + (group + 1) * pair)
        keys = jnp.concatenate([near[:, cols], far[:, cols]], axis=0)
        values = jnp.concatenate([near[:, value_cols], far[:, value_cols]], axis=0)
        keys_t = keys.T
        sum_keys = jnp.zeros((length, pair), WIDE)
        sum_values = jnp.zeros((length, pair), WIDE)
        bias_query = jnp.zeros((1, pair), WIDE)
        for piece in range(2):
            rows = slice(2 * piece * count, 2 * (piece + 1) * count)
            queries = q_ref[rows, cols]
            refs = (d0, d1) if piece == 0 else (d2, d3)
            douts = jnp.concatenate([refs[0][:, cols], refs[1][:, cols]], axis=0)
            zero = jnp.zeros_like(queries)
            all_probs, all_grads, all_query, all_dout, halves = [], [], [], [], []
            for head in range(2):
                mask = head_mask(queries.shape, 1, head)
                query = jnp.where(mask, queries, zero)
                dout = jnp.where(mask, douts, zero)
                at_head = 2 * group + head
                scores = against(keys, query) * SCORE_SCALE
                probs = jnp.exp(scores - lse_ref[at_head : at_head + 1, rows])
                grad_probs = against(values, dout)
                delta = jnp.sum(probs * grad_probs, axis=0, keepdims=True)
                grads = (probs * (grad_probs - delta)).astype(LOW)
                all_probs.append(probs.astype(LOW))
                all_grads.append(grads)
                all_query.append(query)
                all_dout.append(dout)
                halves.append(dot(keys_t, grads))
            mask = head_mask(halves[0].shape, 0, 0)
            dq = jnp.where(mask, halves[0], halves[1]) * SCORE_SCALE
            dq = dq.T.astype(LOW)
            dq_ref[rows, cols] = dq
            bias_query += jnp.sum(dq.astype(WIDE), axis=0, keepdims=True)
            sum_keys += dot(jnp.concatenate(all_grads, axis=1), jnp.concatenate(all_query, axis=0))
            sum_values += dot(jnp.concatenate(all_probs, axis=1), jnp.concatenate(all_dout, axis=0))
        sum_keys = sum_keys * SCORE_SCALE
        half = length // 2
        near_ref[:, cols] = sum_keys[:half]
        far_ref[:, cols] = sum_keys[half:].astype(LOW)
        sums[0:1, cols] = bias_query
        sums[1:2, cols] = jnp.sum(sum_values, axis=0, keepdims=True)
        near_ref[:, value_cols] = sum_values[:half]
        far_ref[:, value_cols] = sum_values[half:].astype(LOW)


def row_mean(value):
    return jnp.mean(value, axis=-1, keepdims=True)


def column_sums(out, *values):
    out[...] = jnp.zeros_like(out)
    for index, value in enumerate(values):
        out[index : index + 1, :] = jnp.sum(value, axis=0, keepdims=True)


def out_kernel(bits, a0, a1, a2, a3, weight, tokens, table, hidden, low, normed, scale):
    _, z, _ = indices(bits)
    size = a0.shape[1]
    branch = jnp.zeros(hidden.shape, WIDE)
    for r, piece in enumerate((a0, a1, a2, a3)):
        branch += dot(piece[...], weight[at((z ^ r) * size, size), :])
    middle = tokens[...].astype(WIDE) + (branch + table[2:3, :])
    centered = middle - row_mean(middle)
    inverse = lax.rsqrt(row_mean(centered * centered) + NORM_EPSILON)
    unit = centered * inverse
    value = unit * table[-4:-3, :] + table[-3:-2, :]
    hidden[...] = value
    low[...] = value.astype(LOW)
    normed[...] = unit
    scale[...] = jnp.broadcast_to(inverse, scale.shape)


def store_parts(product, own, to_b, to_a, far_first, far_second):
    count = own.shape[0]
    half = count // 2
    own[...] = product[:count]
    to_b[...] = product[count : 2 * count]
    to_a[...] = product[2 * count : 3 * count]
    far_first[...] = product[3 * count : 3 * count + half].astype(LOW)
    far_second[...] = product[3 * count + half :].astype(LOW)


def feed_up_kernel(bits, h0, h1, h2, h3, h4, up, bias, act, slope):
    hidden = jnp.concatenate([ref[...] for ref in (h0, h1, h2, h3, h4)], axis=0)
    upward = dot(hidden, up[...]) + bias[...]
    half = (1.0 + lax.erf(upward * (0.5**0.5))) * 0.5
    act[...] = (upward * half).astype(LOW)
    bell = jnp.exp(upward * upward * -0.5) * (0.5 * 2.0**0.5 * math.pi**-0.5)
    slope[...] = (half + upward * bell).astype(LOW)


def feed_down_kernel(bits, act, down, *parts):
    store_parts(dot(act[...], down[...]), *parts)


def norm_two_kernel(bits, own, from_b, from_a, hidden, cot, table, output, grad, low, sums):
    downward = own[...] + from_b[...].astype(WIDE) + from_a[...].astype(WIDE)
    value = hidden[...] + (downward + table[-5:-4, :])
    centered = value - row_mean(value)
    inverse = lax.rsqrt(row_mean(centered * centered) + NORM_EPSILON)
    unit = centered * inverse
    gain = table[-2:-1, :]
    output[...] = (unit * gain + table[-1:, :]).astype(LOW)
    cotangent = cot[...].astype(WIDE)
    inner = cotangent * gain
    result = inverse * (inner - row_mean(inner) - unit * row_mean(inner * unit))
    grad[...] = result
    rounded = result.astype(LOW)
    low[...] = rounded
    column_sums(sums, rounded.astype(WIDE), cotangent * unit, cotangent)


def feed_back_kernel(bits, g0, g1, g2, g3, g4, down, up, slope, grad_up, sums, *parts):
    grads = jnp.concatenate([ref[...] for ref in (g0, g1, g2, g3, g4)], axis=0)
    upward = (against(grads, down[...]) * slope[...].astype(WIDE)).astype(LOW)
    grad_up[...] = upward
    column_sums(sums, upward.astype(WIDE))
    store_parts(against(upward, up[...]), *parts)


def feed_grad_kernel(
    bits, act, g0, g1, g2, g3, g4, h0, h1, h2, h3, h4, grad_up, near, far, down_full, up_full
):
    iy, ix, ih, il, ic = (bits[i] for i in range(5))
    grads = jnp.concatenate([ref[...] for ref in (g0, g1, g2, g3, g4)], axis=0)
    hidden = jnp.concatenate([ref[...] for ref in (h0, h1, h2, h3, h4)], axis=0)
    down_full[...] = cross(act[...], grads).astype(LOW)
    up_full[...] = cross(hidden, grad_up[...]).astype(LOW)
    own = up_full.shape[0] // 32
    size = down_full.shape[0] // 8
    for p in range(4):
        y, h = iy ^ (p // 2), ih ^ (p % 2)
        base = p * (4 * own + size)
        for q in range(4):
            x, l = ix ^ (q // 2), il ^ (q % 2)
            start = ((((y * 2 + x) * 2 + h) * 2 + l) * 2) * own
            to = base + q * own
            near[to : to + own, :] = up_full[at(start + ic * own, own), :]
            far[to : to + own, :] = up_full[at(start + (1 - ic) * own, own), :]
        start = (y * 2 + h) * 2
        to = base + 4 * own
        near[to : to + size, :] = down_full[at((start + ic) * size, size), :]
        far[to : to + size, :] = down_full[at((start + 1 - ic) * size, size), :]


def norm_one_kernel(
    bits, own, from_b, from_a, above, normed, scale, weight, table, grad, low, sums, *pieces
):
    _, z, _ = indices(bits)
    hidden = own[...] + from_b[...].astype(WIDE) + from_a[...].astype(WIDE)
    hidden = above[...] + hidden
    unit = normed[...]
    inner = hidden * table[-4:-3, :]
    result = scale[:, 0:1] * (inner - row_mean(inner) - unit * row_mean(inner * unit))
    grad[...] = result
    rounded = result.astype(LOW)
    low[...] = rounded
    column_sums(sums, rounded.astype(WIDE), hidden * unit, hidden)
    size = pieces[0].shape[1]
    for r, piece in enumerate(pieces):
        piece[...] = against(rounded, weight[at((z ^ r) * size, size), :]).astype(LOW)


def split_rows(bits, full, near, far, order=(0, 1, 2, 3)):
    d, z, c = indices(bits)
    own = full.shape[0] // 32
    for p in range(4):
        for s in range(4):
            start = (d ^ order[p]) * 8 * own + (z ^ s) * 2 * own
            to = (4 * p + s) * own
            near[to : to + own, :] = full[at(start + c * own, own), :]
            far[to : to + own, :] = full[at(start + (1 - c) * own, own), :]


def out_grad_kernel(bits, a0, a1, a2, a3, grad, near, far, full):
    _, z, _ = indices(bits)
    size = a0.shape[1]
    for r, piece in enumerate((a0, a1, a2, a3)):
        full[at((z ^ r) * size, size), :] = cross(piece[...], grad[...]).astype(LOW)
    split_rows(bits, full, near, far, order=(0, 2, 1, 3))


def qkv_grad_kernel(
    bits, t0, t1, t2, t3, dq, dkv, other, heads, one, two, up, near, far, grads, full, extra
):
    d, z, c = indices(bits)
    tokens = jnp.concatenate([t0[...], t1[...], t2[...], t3[...]], axis=0)
    size = dq.shape[1]
    both = (dkv[...] + other[...].astype(WIDE)).astype(LOW)
    grads[:, :size] = dq[...]
    grads[:, size:] = both
    full[...] = cross(tokens, grads[...]).astype(LOW)
    own = full.shape[0] // 32
    tile = full.shape[0] // 8
    lanes = full.shape[1] // tile
    tall = near.shape[0] // 16
    extra[...] = jnp.zeros_like(extra)
    ratio = up.shape[1] // size
    rows = [(one, 0)] + [None] * ratio + [(two, 0), (one, 1), (one, 2), (two, 1), (two, 2)]
    for k in range(8):
        values = []
        for row in range(2):
            value = heads[row : row + 1, k % 2 * tile : (k % 2 + 1) * tile]
            values.append(jnp.where(z == k // 2, value, 0.0))
        for index, source in enumerate(rows):
            if source is None:
                y, x = (index - 1) // 2, (index - 1) % 2
                lane = ((y * 2 + k // 4) * 2 + k % 2) * tile
                mine = jnp.logical_and(bits[1] == x, bits[3] == k // 2 % 2)
                values.append(jnp.where(mine, up[0:1, lane : lane + tile], 0.0))
            else:
                ref, row = source
                values.append(ref[row : row + 1, k * tile : (k + 1) * tile])
        for column, value in enumerate(values):
            row, lane = column // lanes, column % lanes * tile
            extra[k, row : row + 1, lane : lane + tile] = value
    for p in range(4):
        for s in range(4):
            start = (d ^ p) * 8 * own + (z ^ s) * 2 * own
            to = (4 * p + s) * tall
            near[to : to + own, :] = full[at(start + c * own, own), :]
            far[to : to + own, :] = full[at(start + (1 - c) * own, own), :]
            rows = extra[(d ^ p) * 2 + (z ^ s) // 2].astype(LOW)
            near[to + own : to + tall, :] = rows
            far[to + own : to + tall, :] = rows


def rows_grad_kernel(bits, grads, weight, above, own, *parts):
    product = against(grads[...], weight[...])
    count = own.shape[0]
    own[...] = above[...] + product[:count]
    for r, part in enumerate(parts):
        part[...] = product[(r + 1) * count : (r + 2) * count].astype(LOW)


def squares_kernel(bits, down, out, u0, u1, u2, u3, p0, p1, p2, p3, result, small):
    _, _, c = indices(bits)
    own = out.shape[0]
    values = [ref[...].astype(WIDE) for ref in (down, out, u0, u1, u2, u3)]
    values += [ref[:own, :].astype(WIDE) for ref in (p0, p1, p2, p3)]
    rows = sum(ref[own:, :].astype(WIDE) for ref in (p0, p1, p2, p3))
    small[...] = rows
    lane = lax.broadcasted_iota(jnp.int32, rows.shape, 1) % 128
    mine = (lane // own) == bits[3] * 2 + c
    values.append(jnp.where(mine, rows, 0.0))
    total = jnp.zeros((1, 1), WIDE)
    for value in values:
        total += jnp.sum(jnp.sum(value * value, axis=0, keepdims=True), axis=1, keepdims=True)
    result[...] = jnp.broadcast_to(total, result.shape)


def store_update(rate, decay, grad, refs, columns):
    weight, moment, second, new_weight, new_moment, new_second = (ref.at[:, columns] for ref in refs)
    results = adam_update(weight[...], grad, moment[...], second[...], rate, decay)
    new_weight[...], new_moment[...], new_second[...] = results


def update_whole_kernel(rate, decay, bits, factor, grad, *refs):
    store_update(rate, decay, grad[...] * factor[0], refs, slice(None))


def update_qkv_kernel(rate, decay, bits, factor, g0, g1, g2, g3, *refs):
    _, z, _ = indices(bits)
    size = g0.shape[1] // 3
    for r, piece in enumerate((g0, g1, g2, g3)):
        for kind in range(3):
            own = refs[0].shape[0]
            grad = piece[:own, kind * size : (kind + 1) * size].astype(WIDE) * factor[0]
            store_update(rate, decay, grad, refs, at(kind * 4 * size + (z ^ r) * size, size))


def update_up_kernel(rate, decay, bits, factor, g0, g1, g2, g3, *refs):
    ix, il = bits[1], bits[3]
    size = g0.shape[1] // 4
    for r, piece in enumerate((g0, g1, g2, g3)):
        x, l = ix ^ (r // 2), il ^ (r % 2)
        for y in range(2):
            for h in range(2):
                to = (y * 2 + h) * size
                grad = piece[:, to : to + size].astype(WIDE) * factor[0]
                start = (((y * 2 + x) * 2 + h) * 2 + l) * size
                store_update(rate, decay, grad, refs, at(start, size))


def on_square(
    tokens,
    cotangent,
    weight_qkv,
    weight_out,
    weight_up,
    weight_down,
    small_params,
    moment_qkv,
    moment_out,
    moment_up,
    moment_down,
    moment_small,
    second_qkv,
    second_out,
    second_up,
    second_down,
    second_small,
):
    rows = tokens[0]
    count, width = rows.shape
    own = weight_qkv.shape[0]
    down_rows = weight_down.shape[0]
    ratio = weight_up.shape[1] // width
    columns = small_params.shape[1]
    part = width // 4
    units = weight_up.shape[1] // 4
    pad = 8
    tall = own + pad
    iy, ix, ih, il, ic = (lax.axis_index(name) for name in AXES)
    bits = jnp.stack([iy, ix, ih, il, ic]).astype(jnp.int32)
    at_dp, at_z = 2 * iy + ix, 2 * ih + il
    place = 8 * at_dp + 2 * at_z + ic

    low_small = small_params.astype(LOW).T.reshape(1, own * columns)
    low_small = jnp.pad(low_small, ((0, pad - 1), (0, 3 * part - own * columns)))
    with jax.named_scope("weight_qkv"):
        pieces = call(pack_qkv_kernel, [((tall, 3 * part), LOW)] * 4, bits, weight_qkv, low_small)
    with jax.named_scope("tokens"):
        token_parts = gather_ring(rows, "h", "l")
    low_out, low_down, up_near, up_far = call(
        pack_rest_kernel,
        [((own, width), LOW), ((down_rows, width), LOW)] + [((2 * own, units), LOW)] * 2,
        bits,
        weight_out,
        weight_up,
        weight_down,
    )
    with jax.named_scope("weight_qkv"):
        near_qkv = jnp.concatenate(exchange(pieces, "h", "l"), axis=0)
        near_qkv = after(near_qkv, token_parts[1], low_out)
        blocks = [near_qkv, swap(near_qkv, ("x",)), swap(near_qkv, ("y",))]
    with jax.named_scope("weight_up"):
        up_far = send(up_far, ("x",), start=(near_qkv,))
    with jax.named_scope("weight_qkv"):
        blocks.append(swap(after(near_qkv, token_parts[2], up_far), ("y", "x")))
    with jax.named_scope("weight_up"):
        up_other = swap(jnp.concatenate([up_near[own:], up_far[own:]], axis=0), ("l",))
    with jax.named_scope("weight_qkv"):
        near_qkv = after(jnp.concatenate(blocks, axis=0), up_other, token_parts[3])
        far_qkv = swap(near_qkv, ("c",))
        (full_qkv,) = call(lay_qkv_kernel, [((width, 3 * part), LOW)], bits, near_qkv, far_qkv)
    with jax.named_scope("weight_up"):
        feed = [up_near[:own], up_other[:own], up_far[:own], up_other[own:], low_down]
        feed = jnp.concatenate(feed, axis=0)

    rows_of = lambda v: v.reshape(16, tall, 3 * part)[:, own, : own * columns]
    blocks = jnp.concatenate([rows_of(near_qkv), rows_of(far_qkv)], axis=0).astype(WIDE)
    index = jnp.arange(32)
    owner = (((index // 4) % 4) ^ at_dp) * 8 + ((index % 4) ^ at_z) * 2 + ((index // 16) ^ ic)
    chosen = (owner[None, :] == index[:, None]).astype(WIDE)
    blocks = jnp.dot(chosen, blocks)
    table = blocks.reshape(32, columns, own).transpose(1, 0, 2).reshape(columns, width)
    bias_heads = lax.dynamic_slice_in_dim(table[0:2], at_z * part, part, axis=1)
    bias_units = table[3 : 3 + ratio].reshape(2, 2, 2, 2, units // 4)
    bias_units = lax.dynamic_slice(bias_units, (0, ix, 0, il, 0), (2, 1, 2, 1, units // 4))
    bias_units = bias_units.reshape(1, units)

    with jax.named_scope("weight_out"):
        near_out = exchange([after(low_out, near_qkv)] * 4, "h", "l")
        near_out = [low_out] + [after(piece, far_qkv) for piece in near_out[1:]]
        near_out = jnp.concatenate(near_out, axis=0)
    near_out, full_qkv = lax.optimization_barrier((near_out, full_qkv))
    q, kv = call(
        project_kernel,
        [((4 * count, part), LOW), ((4 * count, 2 * part), LOW)],
        bits,
        *token_parts,
        full_qkv,
        bias_heads,
    )
    with jax.named_scope("keys_values"):
        kv_far = swap(kv, ("c",))
    with jax.named_scope("weight_feed"):
        feed_other = send(feed, ("h",), start=(near_out,))
    with jax.named_scope("weight_out"):
        out_parts = exchange([after(near_out, kv)] * 4, "y", "x")
    *attended, lse = call(
        forward_kernel,
        [((count, part), LOW)] * 4 + [((4, 4 * count), WIDE)],
        bits,
        q,
        kv,
        kv_far,
    )
    with jax.named_scope("weight_feed"):
        feed = jnp.concatenate([feed, after(feed_other, lse)], axis=0)
    *attended, feed = lax.optimization_barrier((*attended, feed))
    with jax.named_scope("weight_feed"):
        feed_other = swap(feed, ("y",))
    with jax.named_scope("attended"):
        attended = exchange(attended, "h", "l")
    with jax.named_scope("weight_out"):
        out_parts = [near_out] + [after(piece, lse) for piece in out_parts[1:]]
        near_out = jnp.concatenate(out_parts, axis=0)
        far_out = swap(near_out, ("c",))
        (full_out,) = call(lay_qkv_kernel, [((width, width), LOW)], bits, near_out, far_out)
    hidden, hidden_low, normed, scale = call(
        out_kernel,
        [((count, width), WIDE), ((count, width), LOW), ((count, width), WIDE), ((count, 128), WIDE)],
        bits,
        *attended,
        full_out,
        rows,
        table,
    )

    with jax.named_scope("hidden"):
        hidden_parts = gather_square(hidden_low, "x", "l")
    with jax.named_scope("weight_feed"):
        feed = jnp.concatenate([feed, after(feed_other, *hidden_parts[1:3])], axis=0)
        feed_far = swap(feed, ("c",))
    full_up, full_down = call(
        lay_feed_kernel,
        [((width, units), LOW), ((units, width), LOW)],
        bits,
        feed,
        after(feed_far, *hidden_parts[3:]),
    )
    parts_shape = [((count, width), WIDE)] * 3 + [((count // 2, width), LOW)] * 2
    act, slope = call(
        feed_up_kernel,
        [((4 * count, units), LOW)] * 2,
        bits,
        *hidden_parts,
        full_up,
        bias_units,
        flops=10**9,
    )
    parts = call(feed_down_kernel, parts_shape, bits, act, full_down)
    terms = scatter_square(parts, "x", "l")
    output, grad_two, grad_down, sums_two = call(
        norm_two_kernel,
        [((count, width), LOW), ((count, width), WIDE), ((count, width), LOW), ((8, width), WIDE)],
        bits,
        *terms,
        hidden,
        cotangent[0],
        table,
    )

    with jax.named_scope("grad_down"):
        grad_parts = gather_square(grad_down, "x", "l")
    grad_up, sums_up, *parts = call(
        feed_back_kernel,
        [((4 * count, units), LOW), ((8, units), WIDE)] + parts_shape,
        bits,
        *grad_parts,
        full_down,
        full_up,
        slope,
        flops=2 * 10**9,
    )
    with jax.named_scope("grad_hidden"):
        terms = scatter_square(parts, "x", "l")

    feed_near, feed_far = call(
        feed_grad_kernel,
        [((16 * own + 4 * down_rows, width), LOW)] * 2,
        bits,
        act,
        *grad_parts,
        *hidden_parts,
        grad_up,
        scratch=[pltpu.VMEM((units, width), LOW), pltpu.VMEM((width, units), LOW)],
    )

    def halve(value, axis, start=(), use=()):
        size = value.shape[0] // 2
        other = send(value[size:].astype(LOW), (axis,), start, use)
        return value[:size].astype(WIDE) + other.astype(WIDE)

    with jax.named_scope("grad_weight_feed"):
        feed_other = swap(feed_far, ("c",))
        feed_sum = (feed_near.astype(WIDE) + feed_other.astype(WIDE)).astype(LOW)
    *terms, feed_sum = lax.optimization_barrier((*terms, feed_sum))
    grad_middle, grad_branch, sums_one, *douts = call(
        norm_one_kernel,
        [((count, width), WIDE), ((count, width), LOW), ((8, width), WIDE)]
        + [((count, part), LOW)] * 4,
        bits,
        *terms,
        grad_two,
        normed,
        scale,
        full_out,
        table,
    )
    with jax.named_scope("grad_attended"):
        douts = exchange(douts, "h", "l")
    back = tuple(douts[1:])
    out_near, out_far = call(
        out_grad_kernel,
        [((16 * own, width), LOW)] * 2,
        bits,
        *attended,
        grad_branch,
        scratch=[pltpu.VMEM((width, width), LOW)],
    )
    with jax.named_scope("grad_weight_feed"):
        feed_other = send(feed_sum[feed_sum.shape[0] // 2 :], ("y",))
    with jax.named_scope("grad_weight_out"):
        out_other = send(out_far, ("c",), use=back)
        out_sum = (out_near.astype(WIDE) + out_other.astype(WIDE)).astype(LOW)
    late_lse, out_sum = lax.optimization_barrier((lse, out_sum))
    dq, dkv_near, dkv_far, sums_heads = call(
        backward_kernel,
        [
            ((4 * count, part), LOW),
            ((4 * count, 2 * part), WIDE),
            ((4 * count, 2 * part), LOW),
            ((8, part), WIDE),
        ],
        bits,
        q,
        kv,
        kv_far,
        late_lse,
        *douts,
    )
    with jax.named_scope("grad_weight_out"):
        out_sum = halve(out_sum, "x", use=(dq,)).astype(LOW)
    with jax.named_scope("grad_weight_feed"):
        half = feed_sum.shape[0] // 2
        feed_other = after(feed_other, dq)
        feed_sum = (feed_sum[:half].astype(WIDE) + feed_other.astype(WIDE)).astype(LOW)
    dkv_far, out_sum, feed_sum = lax.optimization_barrier((dkv_far, out_sum, feed_sum))
    up_size = 4 * own
    rows_of_part = lambda start, size: jnp.concatenate(
        [feed_sum[start : start + size], feed_sum[start + up_size + down_rows :][:size]], axis=0
    )
    up_sum, down_sum = rows_of_part(0, up_size), rows_of_part(up_size, down_rows)
    with jax.named_scope("grad_keys_values"):
        dkv_other = swap(dkv_far, ("c",))
    with jax.named_scope("grad_weight_up"):
        owned_up = halve(up_sum, "h", use=(dkv_other,)).astype(LOW)
    near, far, grad_projected = call(
        qkv_grad_kernel,
        [((16 * tall, 3 * part), LOW)] * 2 + [((4 * count, 3 * part), LOW)],
        bits,
        *token_parts,
        dq,
        dkv_near,
        dkv_other,
        sums_heads,
        sums_one,
        sums_two,
        sums_up,
        scratch=[pltpu.VMEM((width, 3 * part), LOW), pltpu.VMEM((8, 8, 3 * part), WIDE)],
    )
    with jax.named_scope("grad_weight_out"):
        out_sum = halve(out_sum, "y", use=(near,)).astype(LOW)
    far, owned_up = lax.optimization_barrier((far, owned_up))
    with jax.named_scope("grad_weight_up"):
        up_pieces = [owned_up[i * own : (i + 1) * own] for i in range(4)]
        up_pieces = exchange(up_pieces, "x", "l")
    with jax.named_scope("grad_weight_qkv"):
        far_other = swap(far, ("c",))
        qkv_sum = (near.astype(WIDE) + far_other.astype(WIDE)).astype(LOW)
    qkv_sum, out_sum, *up_pieces = lax.optimization_barrier((qkv_sum, out_sum, *up_pieces))
    parts = call(
        rows_grad_kernel,
        [((count, width), WIDE)] + [((count, width), LOW)] * 3,
        bits,
        after(grad_projected, far_other),
        full_qkv,
        grad_middle,
    )
    with jax.named_scope("grad_weight_qkv"):
        blocks = [qkv_sum[i * 4 * tall : (i + 1) * 4 * tall] for i in range(4)]
        blocks = exchange(blocks, "y", "x")
        owned_qkv = sum(block.astype(WIDE) for block in blocks).astype(LOW)
    late = tuple(blocks[1:])
    with jax.named_scope("grad_weight_down"):
        owned_down = halve(down_sum, "h", start=(far_other,), use=late)
    with jax.named_scope("grad_weight_out"):
        out_sum = halve(out_sum, "h", use=late).astype(LOW)
    owned_qkv, owned_down, out_sum, *parts = lax.optimization_barrier(
        (owned_qkv, owned_down, out_sum, *parts)
    )
    with jax.named_scope("grad_weight_qkv"):
        qkv_pieces = exchange([owned_qkv[i * tall : (i + 1) * tall] for i in range(4)], "h", "l")
    last = tuple(qkv_pieces[1:])
    with jax.named_scope("grad_weight_out"):
        owned_out = halve(out_sum, "l", use=last)
    with jax.named_scope("grad_tokens"):
        far_l = swap(parts[3], ("l",))
        to_h = (parts[2].astype(WIDE) + far_l.astype(WIDE)).astype(LOW)
        from_l = send(parts[1], ("l",), start=last)
    owned_out, to_h = lax.optimization_barrier((owned_out, to_h))
    with jax.named_scope("grad_tokens"):
        from_h = swap(to_h, ("h",))

    total, small_tile = call(
        squares_kernel,
        [((8, 128), WIDE), ((8, 3 * part), WIDE)],
        bits,
        owned_down,
        owned_out,
        *up_pieces,
        *qkv_pieces,
    )
    tile = width // 8
    lanes = 3 * part // tile
    small_tile = small_tile[:2].reshape(2 * lanes, tile)[:columns]
    owned_small = lax.dynamic_slice_in_dim(small_tile, (2 * il + ic) * own, own, axis=1).T
    with jax.named_scope("norm"):
        for name in ("c", "x", "y", "l"):
            total = total + swap(total, (name,))
        total = after(total, from_l)
        total = total + swap(total, ("h",))
    total, from_h = lax.optimization_barrier((total, from_h))
    grad_rows = parts[0] + from_l.astype(WIDE) + from_h.astype(WIDE)
    grad_norm = jnp.sqrt(total[0, 0])
    factor = jnp.minimum(1.0, CLIP_LIMIT / (grad_norm + 1e-06))
    held = jnp.full((1,), factor)

    def update(kernel, rate, decay, grads, weight, moment, second):
        return call(
            functools.partial(kernel, rate, decay),
            [(weight.shape, WIDE)] * 3,
            bits,
            held,
            *grads,
            weight,
            moment,
            second,
            scalars=1,
        )

    new_qkv, new_moment_qkv, new_second_qkv = update(
        update_qkv_kernel, RATE_MATRIX, WEIGHT_DECAY, qkv_pieces, weight_qkv, moment_qkv, second_qkv
    )
    new_out, new_moment_out, new_second_out = update(
        update_whole_kernel, RATE_OUTPUT, WEIGHT_DECAY, [owned_out], weight_out, moment_out, second_out
    )
    new_up, new_moment_up, new_second_up = update(
        update_up_kernel, RATE_MATRIX, WEIGHT_DECAY, up_pieces, weight_up, moment_up, second_up
    )
    new_down, new_moment_down, new_second_down = update(
        update_whole_kernel, RATE_MATRIX, WEIGHT_DECAY, [owned_down], weight_down, moment_down, second_down
    )
    new_small, new_moment_small, new_second_small = adam_update(
        small_params, owned_small * factor, moment_small, second_small, RATE_SMALL, 0.0
    )
    return (
        output[None],
        grad_rows[None],
        grad_norm,
        new_qkv,
        new_out,
        new_up,
        new_down,
        new_small,
        new_moment_qkv,
        new_moment_out,
        new_moment_up,
        new_moment_down,
        new_moment_small,
        new_second_qkv,
        new_second_out,
        new_second_up,
        new_second_down,
        new_second_small,
    )


def solution(mesh):
    sizes = (mesh.shape["dp"], mesh.shape["seq"])
    if sizes == (4, 8):
        squares = Mesh(mesh.devices.reshape(2, 2, 2, 2, 2), AXES)
        dp, seq = ("y", "x"), ("h", "l", "c")
        body, mesh = on_square, squares
        every = P(AXES, None)
        over = P(dp, seq, None)
    else:
        body = on_device
        every = P(("dp", "seq"), None)
        over = P("dp", "seq", None)
    return jax.shard_map(
        body,
        mesh=mesh,
        in_specs=(over,) * 2 + (every,) * 15,
        out_specs=(over,) * 2 + (P(),) + (every,) * 15,
        check_vma=False,
    )
```

```python
import functools
import math

import jax
import jax.numpy as jnp
from jax import lax
from jax.experimental import pallas as pl
from jax.experimental.pallas import tpu as pltpu
from jax.sharding import Mesh
from jax.sharding import PartitionSpec as P

HEAD = 64
STEP = 5


NORM_EPSILON = 1e-05
ADAM_EPSILON = 1e-08
BETA_FIRST = 0.5
BETA_SECOND = 0.55
CLIP_LIMIT = 1.0
RATE_MATRIX = 0.04
RATE_OUTPUT = 0.5
RATE_SMALL = 0.3
WEIGHT_DECAY = 0.01
SCORE_SCALE = 0.125


def layer_norm(value, gain, shift):
    center = jnp.mean(value, axis=-1, keepdims=True)
    centered = value - center
    variance = jnp.mean(centered * centered, axis=-1, keepdims=True)
    return centered * lax.rsqrt(variance + NORM_EPSILON) * gain + shift


def exact_gelu(value):
    return jax.nn.gelu(value, approximate=False)


def unpack(table_low):
    table = table_low.astype(jnp.float32)
    ratio = table.shape[1] - 8
    bias_up = table[:, 3 : 3 + ratio].T.reshape(-1)
    return (
        table[:, 0],
        table[:, 1],
        table[:, 2],
        bias_up,
        table[:, 3 + ratio],
        table[:, 4 + ratio],
        table[:, 5 + ratio],
        table[:, 6 + ratio],
        table[:, 7 + ratio],
    )


def cross(left, right):
    return lax.dot_general(
        left, right, (((0,), (0,)), ((), ())), preferred_element_type=jnp.float32
    )


def against(left, right):
    return lax.dot_general(
        left, right, (((1,), (1,)), ((), ())), preferred_element_type=jnp.float32
    )


def take_block(source, index, block, heads):
    piece = lax.dynamic_slice_in_dim(source, index * block, block, 0)
    return piece.reshape(block, heads, HEAD)


def scores_of(query_heads, key_heads):
    return (
        jnp.einsum("qhd,khd->hqk", query_heads, key_heads, preferred_element_type=jnp.float32)
        * SCORE_SCALE
    )


def block_grads(query_heads, key_heads, value_heads, dout_heads, log_total, delta):
    scores = scores_of(query_heads, key_heads)
    probs = jnp.exp(scores - log_total[..., None])
    grad_probs = jnp.einsum(
        "qhd,khd->hqk", dout_heads, value_heads, preferred_element_type=jnp.float32
    )
    grad_scores = (probs * (grad_probs - delta[..., None])).astype(jnp.bfloat16)
    return (probs, grad_scores)


def attention_forward(query_heads, keys_all, values_all, block):
    count_rows, heads = (query_heads.shape[0], query_heads.shape[1])
    count = keys_all.shape[0] // block

    def stats_step(index, carry):
        run_top, run_total = carry
        scores = scores_of(query_heads, take_block(keys_all, index, block, heads))
        new_top = jnp.maximum(run_top, jnp.max(scores, axis=-1))
        run_total = run_total * jnp.exp(run_top - new_top) + jnp.sum(
            jnp.exp(scores - new_top[..., None]), axis=-1
        )
        return (new_top, run_total)

    start_top = jnp.full((heads, count_rows), -1e30, jnp.float32)
    start_total = jnp.zeros((heads, count_rows), jnp.float32)
    run_top, run_total = lax.fori_loop(0, count, stats_step, (start_top, start_total))
    log_total = run_top + jnp.log(run_total)

    def value_step(index, accum):
        scores = scores_of(query_heads, take_block(keys_all, index, block, heads))
        weights = jnp.exp(scores - log_total[..., None]).astype(jnp.bfloat16)
        return accum + jnp.einsum(
            "hqk,khd->qhd",
            weights,
            take_block(values_all, index, block, heads),
            preferred_element_type=jnp.float32,
        )

    accum = lax.fori_loop(0, count, value_step, jnp.zeros((count_rows, heads, HEAD), jnp.float32))
    return (accum.reshape(count_rows, heads * HEAD), log_total)


def adam_update(weight, grad, moment, second, rate, decay):
    moment_new = BETA_FIRST * moment + (1.0 - BETA_FIRST) * grad
    second_new = BETA_SECOND * second + (1.0 - BETA_SECOND) * grad * grad
    direction = (
        moment_new
        / (1.0 - BETA_FIRST**STEP)
        / (jnp.sqrt(second_new / (1.0 - BETA_SECOND**STEP)) + ADAM_EPSILON)
    )
    return (weight - rate * (direction + decay * weight), moment_new, second_new)


def on_device(
    tokens,
    cotangent,
    weight_qkv,
    weight_out,
    weight_up,
    weight_down,
    small_params,
    moment_qkv,
    moment_out,
    moment_up,
    moment_down,
    moment_small,
    second_qkv,
    second_out,
    second_up,
    second_down,
    second_small,
):
    rows = tokens[0]
    count_rows = rows.shape[0]
    width = rows.shape[1]
    heads = width // HEAD
    block = 4 * count_rows
    full_qkv, full_out, full_up, full_down, full_small = (
        lax.all_gather(weight_qkv.astype(jnp.bfloat16), ("dp", "seq"), axis=0, tiled=True),
        lax.all_gather(weight_out.astype(jnp.bfloat16), ("dp", "seq"), axis=0, tiled=True),
        lax.all_gather(weight_up.astype(jnp.bfloat16), ("dp", "seq"), axis=0, tiled=True),
        lax.all_gather(weight_down.astype(jnp.bfloat16), ("dp", "seq"), axis=0, tiled=True),
        lax.all_gather(small_params.astype(jnp.bfloat16), ("dp", "seq"), axis=0, tiled=True),
    )
    (
        bias_query,
        bias_value,
        bias_out,
        bias_up,
        bias_down,
        gain_one,
        shift_one,
        gain_two,
        shift_two,
    ) = unpack(full_small)
    projected = jnp.dot(rows, full_qkv, preferred_element_type=jnp.float32)
    query = (projected[:, :width] + bias_query).astype(jnp.bfloat16)
    key_rows = projected[:, width : 2 * width].astype(jnp.bfloat16)
    value_rows = (projected[:, 2 * width :] + bias_value).astype(jnp.bfloat16)
    keys_all, values_all = (
        lax.all_gather(key_rows, "seq", axis=0, tiled=True),
        lax.all_gather(value_rows, "seq", axis=0, tiled=True),
    )
    query_heads = query.reshape(count_rows, heads, HEAD)
    attended, log_total = attention_forward(query_heads, keys_all, values_all, block)
    attended_low = attended.astype(jnp.bfloat16)
    branch = jnp.dot(attended_low, full_out, preferred_element_type=jnp.float32) + bias_out
    middle = rows.astype(jnp.float32) + branch
    hidden, norm_one_back = jax.vjp(layer_norm, middle, gain_one, shift_one)
    hidden_low = hidden.astype(jnp.bfloat16)
    upward = jnp.dot(hidden_low, full_up, preferred_element_type=jnp.float32) + bias_up
    activation, gelu_back = jax.vjp(exact_gelu, upward)
    activation_low = activation.astype(jnp.bfloat16)
    downward = jnp.dot(activation_low, full_down, preferred_element_type=jnp.float32) + bias_down
    output, norm_two_back = jax.vjp(layer_norm, hidden + downward, gain_two, shift_two)
    back_qkv, back_out, back_up, back_down = (full_qkv, full_out, full_up, full_down)
    grad_sum_two, grad_gain_two, grad_shift_two = norm_two_back(cotangent[0].astype(jnp.float32))
    grad_down_low = grad_sum_two.astype(jnp.bfloat16)
    grad_bias_down = jnp.sum(grad_down_low.astype(jnp.float32), axis=0)
    grad_weight_down = cross(activation_low, grad_down_low)
    grad_activation = against(grad_down_low, back_down)
    grad_up_low = gelu_back(grad_activation)[0].astype(jnp.bfloat16)
    grad_bias_up = jnp.sum(grad_up_low.astype(jnp.float32), axis=0)
    grad_weight_up = cross(hidden_low, grad_up_low)
    grad_hidden = grad_sum_two + against(grad_up_low, back_up)
    grad_middle, grad_gain_one, grad_shift_one = norm_one_back(grad_hidden)
    grad_branch_low = grad_middle.astype(jnp.bfloat16)
    grad_bias_out = jnp.sum(grad_branch_low.astype(jnp.float32), axis=0)
    grad_weight_out = cross(attended_low, grad_branch_low)
    grad_attended = against(grad_branch_low, back_out).astype(jnp.bfloat16)
    delta = jnp.sum(
        (grad_attended.astype(jnp.float32) * attended).reshape(count_rows, heads, HEAD), axis=-1
    ).T
    dout_heads = grad_attended.reshape(count_rows, heads, HEAD)
    count = keys_all.shape[0] // block

    def both_step(index, carry):
        grad_query, grad_keys, grad_values = carry
        key_heads = take_block(keys_all, index, block, heads)
        value_heads = take_block(values_all, index, block, heads)
        probs, grad_scores = block_grads(
            query_heads, key_heads, value_heads, dout_heads, log_total, delta
        )
        grad_query = (
            grad_query
            + jnp.einsum("hqk,khd->qhd", grad_scores, key_heads, preferred_element_type=jnp.float32)
            * SCORE_SCALE
        )
        part_keys = (
            jnp.einsum("hqk,qhd->khd", grad_scores, query_heads, preferred_element_type=jnp.float32)
            * SCORE_SCALE
        )
        part_values = jnp.einsum(
            "hqk,qhd->khd",
            probs.astype(jnp.bfloat16),
            dout_heads,
            preferred_element_type=jnp.float32,
        )
        grad_keys = lax.dynamic_update_slice_in_dim(
            grad_keys, part_keys.reshape(block, width), index * block, 0
        )
        grad_values = lax.dynamic_update_slice_in_dim(
            grad_values, part_values.reshape(block, width), index * block, 0
        )
        return (grad_query, grad_keys, grad_values)

    start = (
        jnp.zeros((count_rows, heads, HEAD), jnp.float32),
        jnp.zeros((keys_all.shape[0], width), jnp.float32),
        jnp.zeros((keys_all.shape[0], width), jnp.float32),
    )
    grad_query, grad_keys, grad_values = lax.fori_loop(0, count, both_step, start)
    summed_keys, summed_values = (
        lax.psum_scatter(
            grad_keys.astype(jnp.bfloat16), "seq", scatter_dimension=0, tiled=True
        ).astype(jnp.float32),
        lax.psum_scatter(
            grad_values.astype(jnp.bfloat16), "seq", scatter_dimension=0, tiled=True
        ).astype(jnp.float32),
    )
    grad_query_low = grad_query.reshape(count_rows, width).astype(jnp.bfloat16)
    grad_value_low = summed_values.astype(jnp.bfloat16)
    grad_projected = jnp.concatenate(
        [grad_query_low, summed_keys.astype(jnp.bfloat16), grad_value_low], axis=1
    )
    grad_weight_qkv = cross(rows, grad_projected)
    grad_bias_query = jnp.sum(grad_query_low.astype(jnp.float32), axis=0)
    grad_bias_value = jnp.sum(grad_value_low.astype(jnp.float32), axis=0)
    grad_rows = grad_middle + against(grad_projected, back_qkv)
    ratio = full_up.shape[1] // width
    grad_small = jnp.concatenate(
        [
            jnp.stack([grad_bias_query, grad_bias_value, grad_bias_out], axis=1),
            grad_bias_up.reshape(ratio, width).T,
            jnp.stack(
                [grad_bias_down, grad_gain_one, grad_shift_one, grad_gain_two, grad_shift_two],
                axis=1,
            ),
        ],
        axis=1,
    )
    owned_qkv, owned_out, owned_up, owned_down, owned_small = (
        lax.psum_scatter(grad_weight_qkv, ("dp", "seq"), scatter_dimension=0, tiled=True),
        lax.psum_scatter(grad_weight_out, ("dp", "seq"), scatter_dimension=0, tiled=True),
        lax.psum_scatter(grad_weight_up, ("dp", "seq"), scatter_dimension=0, tiled=True),
        lax.psum_scatter(grad_weight_down, ("dp", "seq"), scatter_dimension=0, tiled=True),
        lax.psum_scatter(grad_small, ("dp", "seq"), scatter_dimension=0, tiled=True),
    )
    squares = jnp.sum(owned_qkv * owned_qkv) + jnp.sum(owned_out * owned_out)
    squares = squares + jnp.sum(owned_up * owned_up) + jnp.sum(owned_down * owned_down)
    squares = squares + jnp.sum(owned_small * owned_small)
    total = lax.psum(squares, ("dp", "seq"))
    grad_norm = jnp.sqrt(total)
    factor = jnp.minimum(1.0, CLIP_LIMIT / (grad_norm + 1e-06))
    new_qkv, new_moment_qkv, new_second_qkv = adam_update(
        weight_qkv, owned_qkv * factor, moment_qkv, second_qkv, RATE_MATRIX, WEIGHT_DECAY
    )
    new_out, new_moment_out, new_second_out = adam_update(
        weight_out, owned_out * factor, moment_out, second_out, RATE_OUTPUT, WEIGHT_DECAY
    )
    new_up, new_moment_up, new_second_up = adam_update(
        weight_up, owned_up * factor, moment_up, second_up, RATE_MATRIX, WEIGHT_DECAY
    )
    new_down, new_moment_down, new_second_down = adam_update(
        weight_down, owned_down * factor, moment_down, second_down, RATE_MATRIX, WEIGHT_DECAY
    )
    new_small, new_moment_small, new_second_small = adam_update(
        small_params, owned_small * factor, moment_small, second_small, RATE_SMALL, 0.0
    )
    return (
        output.astype(jnp.bfloat16)[None],
        grad_rows[None],
        grad_norm,
        new_qkv,
        new_out,
        new_up,
        new_down,
        new_small,
        new_moment_qkv,
        new_moment_out,
        new_moment_up,
        new_moment_down,
        new_moment_small,
        new_second_qkv,
        new_second_out,
        new_second_up,
        new_second_down,
        new_second_small,
    )


AXES = ("y", "x", "h", "l", "c")
LOW = jnp.bfloat16
WIDE = jnp.float32


def swap(value, axes):
    axes = tuple(name for name in AXES if name in axes)
    last = 2 ** len(axes) - 1
    return lax.ppermute(value, axes, [(i, i ^ last) for i in range(last + 1)])


def after(value, *events):
    return lax.optimization_barrier((value, *events))[0]


def tie(*values):
    return lax.optimization_barrier(values)


def send(value, axes, start=(), use=()):
    got = swap(after(value, *start) if start else value, axes)
    return after(got, *use) if use else got


def exchange(parts, a, b, start=(), use=()):
    ways = ((b,), (a,), (a, b))
    return [parts[0]] + [send(part, way, start, use) for part, way in zip(parts[1:], ways)]


def gather_square(value, a, b):
    half = value.shape[0] // 2
    from_a, from_b = swap(value, (a,)), swap(value, (b,))
    return [value, from_b, from_a, swap(from_a[:half], (b,)), swap(from_b[half:], (a,))]


def scatter_square(parts, a, b):
    own, to_b, to_a, far_first, far_second = parts
    half = own.shape[0] // 2
    first = swap(far_first, (a,))
    second = swap(far_second, (b,))
    to_b = jnp.concatenate([to_b[:half] + first.astype(WIDE), to_b[half:]], axis=0).astype(LOW)
    to_a = jnp.concatenate([to_a[:half], to_a[half:] + second.astype(WIDE)], axis=0).astype(LOW)
    return own, swap(to_b, (b,)), swap(to_a, (a,))


def gather_ring(value, a, b, start=(), use=()):
    from_b = send(value, (b,), start, use)
    from_a = swap(after(value, *start) if start else value, (a,))
    far = send(from_a, (b,), use=use)
    return [value, from_b, after(from_a, *use) if use else from_a, far]


def dot(left, right):
    return jnp.dot(left, right, preferred_element_type=WIDE)


def call(kernel, outs, *args, scratch=(), flops=10**9, scalars=0):
    outs = [jax.ShapeDtypeStruct(shape, kind) for shape, kind in outs]
    return pl.pallas_call(
        kernel,
        name=getattr(kernel, "func", kernel).__name__,
        in_specs=[pl.BlockSpec(memory_space=pltpu.SMEM)] * (1 + scalars)
        + [pl.BlockSpec(memory_space=pltpu.VMEM)] * (len(args) - 1 - scalars),
        out_specs=[pl.BlockSpec(memory_space=pltpu.VMEM)] * len(outs),
        out_shape=outs,
        scratch_shapes=list(scratch),
        compiler_params=pltpu.CompilerParams(vmem_limit_bytes=48 * 2**20),
        cost_estimate=pl.CostEstimate(flops=1, bytes_accessed=1, transcendentals=0),
    )(*args)


def at(start, size):
    return pl.ds(pl.multiple_of(start, size), size)


def indices(bits):
    iy, ix, ih, il, ic = (bits[i] for i in range(5))
    return 2 * iy + ix, 2 * ih + il, ic


def pack_qkv_kernel(bits, weight, small, *outs):
    _, z, _ = indices(bits)
    own = weight.shape[0]
    size = outs[0].shape[1] // 3
    for r, out in enumerate(outs):
        for kind in range(3):
            start = kind * 4 * size + (z ^ r) * size
            out[:own, kind * size : (kind + 1) * size] = weight[:, at(start, size)].astype(LOW)
        out[own:, :] = small[...]


def pack_rest_kernel(bits, out_weight, up, down, low_out, low_down, near_up, far_up):
    iy, ix, ih, il, ic = (bits[i] for i in range(5))
    own = up.shape[0]
    size = up.shape[1] // 16
    low_out[...] = out_weight[...].astype(LOW)
    low_down[...] = down[...].astype(LOW)
    for r in range(4):
        out, rows = (near_up, far_up)[r // 2], slice(r % 2 * own, (r % 2 + 1) * own)
        x, l = ix ^ (r // 2), il ^ (r % 2)
        for y in range(2):
            for h in range(2):
                start = (((y * 2 + x) * 2 + h) * 2 + l) * size
                to = (y * 2 + h) * size
                out[rows, to : to + size] = up[:, at(start, size)].astype(LOW)


def lay_rows(bits, full, pieces, own, stride, c):
    d, z, _ = indices(bits)
    for p, piece in enumerate(pieces):
        for s in range(4):
            to = (d ^ p) * 8 * own + (z ^ s) * 2 * own + c * own
            full[at(to, own), :] = piece[s * stride : s * stride + own, :]


def lay_qkv_kernel(bits, near, far, full):
    own = full.shape[0] // 32
    stride = near.shape[0] // 16
    c = bits[4]
    for ref, core in ((near, c), (far, 1 - c)):
        pieces = [ref.at[p * 4 * stride : (p + 1) * 4 * stride] for p in range(4)]
        lay_rows(bits, full, pieces, own, stride, core)


def lay_up_kernel(bits, near, far, full):
    iy, ix, ih, il, ic = (bits[i] for i in range(5))
    own = full.shape[0] // 32
    for ref, core in ((near, ic), (far, 1 - ic)):
        for p in range(4):
            y, h = iy ^ (p // 2), ih ^ (p % 2)
            for q in range(4):
                x, l = ix ^ (q // 2), il ^ (q % 2)
                to = ((((y * 2 + x) * 2 + h) * 2 + l) * 2 + core) * own
                full[at(to, own), :] = ref[(4 * p + q) * own : (4 * p + q + 1) * own, :]


def lay_down_kernel(bits, near, far, full):
    iy, _, ih, _, ic = (bits[i] for i in range(5))
    size = full.shape[0] // 8
    for ref, core in ((near, ic), (far, 1 - ic)):
        for p in range(4):
            to = (((iy ^ (p // 2)) * 2 + (ih ^ (p % 2))) * 2 + core) * size
            full[at(to, size), :] = ref[p * size : (p + 1) * size, :]


def project_kernel(
    bits, bias, near_ref, far_ref, t0, t1, t2, t3, q_ref, kv_ref, full_ref, near, far, rows, sems
):
    d, z, c = indices(bits)
    count = t0.shape[0]
    own = full_ref.shape[0] // 32
    tall = near.shape[0] // 16
    size = q_ref.shape[1]
    pairs = [(near_ref, near), (far_ref, far)]
    pairs += [(ref, rows.at[i * count : (i + 1) * count]) for i, ref in enumerate((t0, t1, t2, t3))]
    copies = [pltpu.make_async_copy(*pair, sems.at[i]) for i, pair in enumerate(pairs)]
    for copy in copies:
        copy.start()
    for copy in copies[:2]:
        copy.wait()
    for ref, core in ((near, c), (far, 1 - c)):
        for p in range(4):
            for s in range(4):
                to = (d ^ p) * 8 * own + (z ^ s) * 2 * own + core * own
                full_ref[at(to, own), :] = ref[(4 * p + s) * tall : (4 * p + s) * tall + own, :]
    for copy in copies[2:]:
        copy.wait()
    projected = dot(rows[...], full_ref[...])
    q_ref[...] = (projected[:, :size] + bias[0:1, :]).astype(LOW)
    kv_ref[:, :size] = projected[:, size : 2 * size].astype(LOW)
    kv_ref[:, size:] = (projected[:, 2 * size :] + bias[1:2, :]).astype(LOW)


def head_mask(shape, axis, head):
    lane = lax.broadcasted_iota(jnp.int32, shape, axis)
    return (lane < HEAD) if head == 0 else (lane >= HEAD)


def forward_kernel(bits, q_ref, near, far, *outs):
    lse_ref = outs[-1]
    count = outs[0].shape[0]
    width = q_ref.shape[1]
    pair = 2 * HEAD
    for group in range(width // pair):
        cols = slice(group * pair, (group + 1) * pair)
        value_cols = slice(width + group * pair, width + (group + 1) * pair)
        keys = jnp.concatenate([near[:, cols], far[:, cols]], axis=0)
        values_t = jnp.concatenate([near[:, value_cols], far[:, value_cols]], axis=0).T
        for piece in range(2):
            rows = slice(2 * piece * count, 2 * (piece + 1) * count)
            queries = q_ref[rows, cols]
            zero = jnp.zeros_like(queries)
            halves = []
            for head in range(2):
                query = jnp.where(head_mask(queries.shape, 1, head), queries, zero)
                scores = against(keys, query) * SCORE_SCALE
                top = jnp.max(scores, axis=0, keepdims=True)
                weights = jnp.exp(scores - top)
                total = jnp.sum(weights, axis=0, keepdims=True)
                at_head = 2 * group + head
                lse_ref[at_head : at_head + 1, rows] = top + jnp.log(total)
                probs = (weights * (1.0 / total)).astype(LOW)
                halves.append(dot(values_t, probs))
            mask = head_mask(halves[0].shape, 0, 0)
            result = jnp.where(mask, halves[0], halves[1]).T.astype(LOW)
            outs[2 * piece][:, cols] = result[:count]
            outs[2 * piece + 1][:, cols] = result[count:]


def backward_kernel(
    bits, q_ref, near, far, lse_ref, d0, d1, d2, d3, dq_ref, near_ref, far_ref, sums
):
    count = d0.shape[0]
    length = 2 * near.shape[0]
    width = q_ref.shape[1]
    pair = 2 * HEAD
    for group in range(width // pair):
        cols = slice(group * pair, (group + 1) * pair)
        value_cols = slice(width + group * pair, width + (group + 1) * pair)
        keys = jnp.concatenate([near[:, cols], far[:, cols]], axis=0)
        values = jnp.concatenate([near[:, value_cols], far[:, value_cols]], axis=0)
        keys_t = keys.T
        sum_keys = jnp.zeros((length, pair), WIDE)
        sum_values = jnp.zeros((length, pair), WIDE)
        bias_query = jnp.zeros((1, pair), WIDE)
        for piece in range(2):
            rows = slice(2 * piece * count, 2 * (piece + 1) * count)
            queries = q_ref[rows, cols]
            refs = (d0, d1) if piece == 0 else (d2, d3)
            douts = jnp.concatenate([refs[0][:, cols], refs[1][:, cols]], axis=0)
            zero = jnp.zeros_like(queries)
            all_probs, all_grads, all_query, all_dout, halves = [], [], [], [], []
            for head in range(2):
                mask = head_mask(queries.shape, 1, head)
                query = jnp.where(mask, queries, zero)
                dout = jnp.where(mask, douts, zero)
                at_head = 2 * group + head
                scores = against(keys, query) * SCORE_SCALE
                probs = jnp.exp(scores - lse_ref[at_head : at_head + 1, rows])
                grad_probs = against(values, dout)
                delta = jnp.sum(probs * grad_probs, axis=0, keepdims=True)
                grads = (probs * (grad_probs - delta)).astype(LOW)
                all_probs.append(probs.astype(LOW))
                all_grads.append(grads)
                all_query.append(query)
                all_dout.append(dout)
                halves.append(dot(keys_t, grads))
            mask = head_mask(halves[0].shape, 0, 0)
            dq = jnp.where(mask, halves[0], halves[1]) * SCORE_SCALE
            dq = dq.T.astype(LOW)
            dq_ref[rows, cols] = dq
            bias_query += jnp.sum(dq.astype(WIDE), axis=0, keepdims=True)
            sum_keys += dot(jnp.concatenate(all_grads, axis=1), jnp.concatenate(all_query, axis=0))
            sum_values += dot(jnp.concatenate(all_probs, axis=1), jnp.concatenate(all_dout, axis=0))
        sum_keys = sum_keys * SCORE_SCALE
        half = length // 2
        near_ref[:, cols] = sum_keys[:half]
        far_ref[:, cols] = sum_keys[half:].astype(LOW)
        sums[0:1, cols] = bias_query
        sums[1:2, cols] = jnp.sum(sum_values, axis=0, keepdims=True)
        near_ref[:, value_cols] = sum_values[:half]
        far_ref[:, value_cols] = sum_values[half:].astype(LOW)


def row_mean(value):
    return jnp.mean(value, axis=-1, keepdims=True)


def column_sums(out, *values):
    out[...] = jnp.zeros_like(out)
    for index, value in enumerate(values):
        out[index : index + 1, :] = jnp.sum(value, axis=0, keepdims=True)


def out_kernel(bits, a0, a1, a2, a3, weight, tokens, table, hidden, low, normed, scale):
    _, z, _ = indices(bits)
    size = a0.shape[1]
    branch = jnp.zeros(hidden.shape, WIDE)
    for r, piece in enumerate((a0, a1, a2, a3)):
        branch += dot(piece[...], weight[at((z ^ r) * size, size), :])
    middle = tokens[...].astype(WIDE) + (branch + table[2:3, :])
    centered = middle - row_mean(middle)
    inverse = lax.rsqrt(row_mean(centered * centered) + NORM_EPSILON)
    unit = centered * inverse
    value = unit * table[-4:-3, :] + table[-3:-2, :]
    hidden[...] = value
    low[...] = value.astype(LOW)
    normed[...] = unit
    scale[...] = jnp.broadcast_to(inverse, scale.shape)


def store_parts(product, own, to_b, to_a, far_first, far_second):
    count = own.shape[0]
    half = count // 2
    own[...] = product[:count]
    to_b[...] = product[count : 2 * count]
    to_a[...] = product[2 * count : 3 * count]
    far_first[...] = product[3 * count : 3 * count + half].astype(LOW)
    far_second[...] = product[3 * count + half :].astype(LOW)


def feed_up_kernel(bits, h0, h1, h2, h3, h4, up, bias, act, slope):
    hidden = jnp.concatenate([ref[...] for ref in (h0, h1, h2, h3, h4)], axis=0)
    upward = dot(hidden, up[...]) + bias[...]
    half = (1.0 + lax.erf(upward * (0.5**0.5))) * 0.5
    act[...] = (upward * half).astype(LOW)
    bell = jnp.exp(upward * upward * -0.5) * (0.5 * 2.0**0.5 * math.pi**-0.5)
    slope[...] = (half + upward * bell).astype(LOW)


def feed_down_kernel(bits, act, down, *parts):
    store_parts(dot(act[...], down[...]), *parts)


def norm_two_kernel(bits, own, from_b, from_a, hidden, cot, table, output, grad, low, sums):
    downward = own[...] + from_b[...].astype(WIDE) + from_a[...].astype(WIDE)
    value = hidden[...] + (downward + table[-5:-4, :])
    centered = value - row_mean(value)
    inverse = lax.rsqrt(row_mean(centered * centered) + NORM_EPSILON)
    unit = centered * inverse
    gain = table[-2:-1, :]
    output[...] = (unit * gain + table[-1:, :]).astype(LOW)
    cotangent = cot[...].astype(WIDE)
    inner = cotangent * gain
    result = inverse * (inner - row_mean(inner) - unit * row_mean(inner * unit))
    grad[...] = result
    rounded = result.astype(LOW)
    low[...] = rounded
    column_sums(sums, rounded.astype(WIDE), cotangent * unit, cotangent)


def feed_back_kernel(bits, g0, g1, g2, g3, g4, down, up, slope, grad_up, sums, *parts):
    grads = jnp.concatenate([ref[...] for ref in (g0, g1, g2, g3, g4)], axis=0)
    upward = (against(grads, down[...]) * slope[...].astype(WIDE)).astype(LOW)
    grad_up[...] = upward
    column_sums(sums, upward.astype(WIDE))
    store_parts(against(upward, up[...]), *parts)


def feed_grad_kernel(
    bits, act, g0, g1, g2, g3, g4, h0, h1, h2, h3, h4, grad_up, near, far, down_full, up_full
):
    iy, ix, ih, il, ic = (bits[i] for i in range(5))
    grads = jnp.concatenate([ref[...] for ref in (g0, g1, g2, g3, g4)], axis=0)
    hidden = jnp.concatenate([ref[...] for ref in (h0, h1, h2, h3, h4)], axis=0)
    down_full[...] = cross(act[...], grads).astype(LOW)
    up_full[...] = cross(hidden, grad_up[...]).astype(LOW)
    own = up_full.shape[0] // 32
    size = down_full.shape[0] // 8
    for p in range(4):
        y, h = iy ^ (p // 2), ih ^ (p % 2)
        base = p * (4 * own + size)
        for q in range(4):
            x, l = ix ^ (q // 2), il ^ (q % 2)
            start = ((((y * 2 + x) * 2 + h) * 2 + l) * 2) * own
            to = base + q * own
            near[to : to + own, :] = up_full[at(start + ic * own, own), :]
            far[to : to + own, :] = up_full[at(start + (1 - ic) * own, own), :]
        start = (y * 2 + h) * 2
        to = base + 4 * own
        near[to : to + size, :] = down_full[at((start + ic) * size, size), :]
        far[to : to + size, :] = down_full[at((start + 1 - ic) * size, size), :]


def norm_one_kernel(
    bits, own, from_b, from_a, above, normed, scale, weight, table, grad, low, sums, *pieces
):
    _, z, _ = indices(bits)
    hidden = own[...] + from_b[...].astype(WIDE) + from_a[...].astype(WIDE)
    hidden = above[...] + hidden
    unit = normed[...]
    inner = hidden * table[-4:-3, :]
    result = scale[:, 0:1] * (inner - row_mean(inner) - unit * row_mean(inner * unit))
    grad[...] = result
    rounded = result.astype(LOW)
    low[...] = rounded
    column_sums(sums, rounded.astype(WIDE), hidden * unit, hidden)
    size = pieces[0].shape[1]
    for r, piece in enumerate(pieces):
        piece[...] = against(rounded, weight[at((z ^ r) * size, size), :]).astype(LOW)


def split_rows(bits, full, near, far, order=(0, 1, 2, 3)):
    d, z, c = indices(bits)
    own = full.shape[0] // 32
    for p in range(4):
        for s in range(4):
            start = (d ^ order[p]) * 8 * own + (z ^ order[s]) * 2 * own
            to = (4 * p + s) * own
            near[to : to + own, :] = full[at(start + c * own, own), :]
            far[to : to + own, :] = full[at(start + (1 - c) * own, own), :]


def out_grad_kernel(bits, a0, a1, a2, a3, grad, near, far, full):
    _, z, _ = indices(bits)
    size = a0.shape[1]
    for r, piece in enumerate((a0, a1, a2, a3)):
        full[at((z ^ r) * size, size), :] = cross(piece[...], grad[...]).astype(LOW)
    split_rows(bits, full, near, far, order=(0, 2, 1, 3))


def qkv_grad_kernel(
    bits, t0, t1, t2, t3, dq, dkv, other, heads, one, two, up, near, far, grads, full, extra
):
    d, z, c = indices(bits)
    tokens = jnp.concatenate([t0[...], t1[...], t2[...], t3[...]], axis=0)
    size = dq.shape[1]
    both = (dkv[...] + other[...].astype(WIDE)).astype(LOW)
    grads[:, :size] = dq[...]
    grads[:, size:] = both
    full[...] = cross(tokens, grads[...]).astype(LOW)
    own = full.shape[0] // 32
    tile = full.shape[0] // 8
    lanes = full.shape[1] // tile
    tall = near.shape[0] // 16
    extra[...] = jnp.zeros_like(extra)
    ratio = up.shape[1] // size
    rows = [(one, 0)] + [None] * ratio + [(two, 0), (one, 1), (one, 2), (two, 1), (two, 2)]
    for k in range(8):
        values = []
        for row in range(2):
            value = heads[row : row + 1, k % 2 * tile : (k % 2 + 1) * tile]
            values.append(jnp.where(z == k // 2, value, 0.0))
        for index, source in enumerate(rows):
            if source is None:
                y, x = (index - 1) // 2, (index - 1) % 2
                lane = ((y * 2 + k // 4) * 2 + k % 2) * tile
                mine = jnp.logical_and(bits[1] == x, bits[3] == k // 2 % 2)
                values.append(jnp.where(mine, up[0:1, lane : lane + tile], 0.0))
            else:
                ref, row = source
                values.append(ref[row : row + 1, k * tile : (k + 1) * tile])
        for column, value in enumerate(values):
            row, lane = column // lanes, column % lanes * tile
            extra[k, row : row + 1, lane : lane + tile] = value
    for p in range(4):
        for s in range(4):
            start = (d ^ p) * 8 * own + (z ^ s) * 2 * own
            to = (4 * p + s) * tall
            near[to : to + own, :] = full[at(start + c * own, own), :]
            far[to : to + own, :] = full[at(start + (1 - c) * own, own), :]
            rows = extra[(d ^ p) * 2 + (z ^ s) // 2].astype(LOW)
            near[to + own : to + tall, :] = rows
            far[to + own : to + tall, :] = rows


def rows_grad_kernel(bits, grads, weight, above, own, *parts):
    product = against(grads[...], weight[...])
    count = own.shape[0]
    own[...] = above[...] + product[:count]
    for r, part in enumerate(parts):
        part[...] = product[(r + 1) * count : (r + 2) * count].astype(LOW)


def squares_kernel(bits, down, out, u0, u1, u2, u3, p0, p1, p2, p3, result, small):
    _, _, c = indices(bits)
    own = out.shape[0]
    values = [ref[...].astype(WIDE) for ref in (down, out, u0, u1, u2, u3)]
    values += [ref[:own, :].astype(WIDE) for ref in (p0, p1, p2, p3)]
    rows = sum(ref[own:, :].astype(WIDE) for ref in (p0, p1, p2, p3))
    small[...] = rows
    lane = lax.broadcasted_iota(jnp.int32, rows.shape, 1) % 128
    mine = (lane // own) == bits[3] * 2 + c
    values.append(jnp.where(mine, rows, 0.0))
    total = jnp.zeros((1, 1), WIDE)
    for value in values:
        total += jnp.sum(jnp.sum(value * value, axis=0, keepdims=True), axis=1, keepdims=True)
    result[...] = jnp.broadcast_to(total, result.shape)


def update_kernel(plans, bits, factor, *refs):
    count = len(plans)
    total = sum(plan[2] for plan in plans)
    sources, refs = refs[:total], refs[total:]
    grads, refs = refs[6 * count : 6 * count + total], refs[: 6 * count] + refs[6 * count + total :]
    brought = refs[-3]
    fetches = [
        pltpu.make_async_copy(sources[i], grads[i], brought.at[i]) for i in range(total)
    ]
    for fetch in fetches:
        fetch.start()
    states, results = refs[: 3 * count], refs[3 * count : 6 * count]
    held, made = refs[6 * count : 9 * count], refs[9 * count : 12 * count]
    arrive, leave = refs[-2:]
    loads = [
        pltpu.make_async_copy(states[i], held[i], arrive.at[i]) for i in range(3 * count)
    ]
    stores = [
        pltpu.make_async_copy(made[i], results[i], leave.at[i]) for i in range(3 * count)
    ]
    for load in loads:
        load.start()
    _, z, _ = indices(bits)
    first = 0
    for index, (rate, places, pieces) in enumerate(plans):
        mine = slice(3 * index, 3 * index + 3)
        for load in loads[mine] + fetches[first : first + pieces]:
            load.wait()
        own = held[3 * index].shape[0]
        for r in range(pieces):
            piece = grads[first + r]
            for source, target in places(bits, z, r, piece.shape[1]):
                grad = piece[:own, source].astype(WIDE) * factor[0]
                weight, moment, second = (ref[:, target] for ref in held[mine])
                values = adam_update(weight, grad, moment, second, rate, WEIGHT_DECAY)
                for ref, value in zip(made[mine], values):
                    ref[:, target] = value
        for store in stores[mine]:
            store.start()
        first += pieces
    for store in stores:
        store.wait()


def whole_places(bits, z, r, columns):
    return [(slice(None), slice(None))]


def qkv_places(bits, z, r, columns):
    size = columns // 3
    return [
        (slice(kind * size, (kind + 1) * size), at(kind * 4 * size + (z ^ r) * size, size))
        for kind in range(3)
    ]


def up_places(bits, z, r, columns):
    size = columns // 4
    x, l = bits[1] ^ (r // 2), bits[3] ^ (r % 2)
    return [
        (
            slice((2 * y + h) * size, (2 * y + h + 1) * size),
            at((((y * 2 + x) * 2 + h) * 2 + l) * size, size),
        )
        for y in range(2)
        for h in range(2)
    ]


def on_square(
    tokens,
    cotangent,
    weight_qkv,
    weight_out,
    weight_up,
    weight_down,
    small_params,
    moment_qkv,
    moment_out,
    moment_up,
    moment_down,
    moment_small,
    second_qkv,
    second_out,
    second_up,
    second_down,
    second_small,
):
    rows = tokens[0]
    count, width = rows.shape
    own = weight_qkv.shape[0]
    down_rows = weight_down.shape[0]
    ratio = weight_up.shape[1] // width
    columns = small_params.shape[1]
    part = width // 4
    units = weight_up.shape[1] // 4
    pad = 8
    tall = own + pad
    iy, ix, ih, il, ic = (lax.axis_index(name) for name in AXES)
    bits = jnp.stack([iy, ix, ih, il, ic]).astype(jnp.int32)
    at_dp, at_z = 2 * iy + ix, 2 * ih + il
    place = 8 * at_dp + 2 * at_z + ic

    low_small = small_params.astype(LOW).T.reshape(1, own * columns)
    low_small = jnp.pad(low_small, ((0, pad - 1), (0, 3 * part - own * columns)))
    with jax.named_scope("weight_qkv"):
        pieces = call(pack_qkv_kernel, [((tall, 3 * part), LOW)] * 4, bits, weight_qkv, low_small)
    with jax.named_scope("tokens"):
        token_l, token_h = swap(rows, ("l",)), swap(rows, ("h",))
    low_out, low_down, up_near, up_far = call(
        pack_rest_kernel,
        [((own, width), LOW), ((down_rows, width), LOW)] + [((2 * own, units), LOW)] * 2,
        bits,
        weight_out,
        weight_up,
        weight_down,
    )
    with jax.named_scope("weight_qkv"):
        near_qkv = jnp.concatenate(exchange(pieces, "h", "l"), axis=0)
        near_qkv = after(near_qkv, token_l, low_out)
    with jax.named_scope("weight_up"):
        up_far = send(up_far, ("x",), start=(near_qkv,))
        up_last = swap(jnp.concatenate([up_near[own:], up_far[own:]], axis=0), ("l",))
        near_up = [up_near[:own], up_last[:own], up_far[:own], up_last[own:]]
        near_up = jnp.concatenate(near_up, axis=0)
    with jax.named_scope("weight_out"):
        out_other = send(low_out, ("l",), start=(near_qkv,))
    with jax.named_scope("weight_qkv"):
        near_qkv = jnp.concatenate(exchange([near_qkv] * 4, "y", "x"), axis=0)
    near_qkv, token_h, near_up, out_other = tie(near_qkv, token_h, near_up, out_other)
    with jax.named_scope("weight_qkv"):
        far_qkv = swap(near_qkv, ("c",))
    with jax.named_scope("tokens"):
        token_parts = [rows, token_l, token_h, swap(token_h, ("l",))]
    with jax.named_scope("weight_up"):
        up_other = swap(near_up, ("h",))
    far_qkv, token_parts[3] = tie(far_qkv, token_parts[3])
    with jax.named_scope("weight_out"):
        near_out = jnp.concatenate([low_out, after(out_other, token_parts[3])], axis=0)
        out_other = swap(near_out, ("h",))
    far_qkv, up_other = tie(far_qkv, after(up_other, far_qkv))

    rows_of = lambda v: v.reshape(16, tall, 3 * part)[:, own, : own * columns]
    blocks = jnp.concatenate([rows_of(near_qkv), rows_of(far_qkv)], axis=0).astype(WIDE)
    index = jnp.arange(32)
    owner = (((index // 4) % 4) ^ at_dp) * 8 + ((index % 4) ^ at_z) * 2 + ((index // 16) ^ ic)
    chosen = (owner[None, :] == index[:, None]).astype(WIDE)
    blocks = jnp.dot(chosen, blocks)
    table = blocks.reshape(32, columns, own).transpose(1, 0, 2).reshape(columns, width)
    bias_heads = lax.dynamic_slice_in_dim(table[0:2], at_z * part, part, axis=1)
    bias_units = table[3 : 3 + ratio].reshape(2, 2, 2, 2, units // 4)
    bias_units = lax.dynamic_slice(bias_units, (0, ix, 0, il, 0), (2, 1, 2, 1, units // 4))
    bias_units = bias_units.reshape(1, units)

    vmem, hbm = pl.BlockSpec(memory_space=pltpu.VMEM), pl.BlockSpec(memory_space=pltpu.HBM)
    q, kv, full_qkv = pl.pallas_call(
        project_kernel,
        name="project_kernel",
        in_specs=[pl.BlockSpec(memory_space=pltpu.SMEM), vmem] + [hbm] * 6,
        out_specs=[vmem] * 3,
        out_shape=[
            jax.ShapeDtypeStruct((4 * count, part), LOW),
            jax.ShapeDtypeStruct((4 * count, 2 * part), LOW),
            jax.ShapeDtypeStruct((width, 3 * part), LOW),
        ],
        scratch_shapes=[
            pltpu.VMEM(near_qkv.shape, LOW),
            pltpu.VMEM(far_qkv.shape, LOW),
            pltpu.VMEM((4 * count, width), LOW),
            pltpu.SemaphoreType.DMA((6,)),
        ],
        compiler_params=pltpu.CompilerParams(vmem_limit_bytes=48 * 2**20),
        cost_estimate=pl.CostEstimate(flops=1, bytes_accessed=1, transcendentals=0),
    )(bits, bias_heads, near_qkv, far_qkv, *token_parts)
    kv, out_other = tie(kv, out_other)
    with jax.named_scope("keys_values"):
        kv_far = swap(kv, ("c",))
    with jax.named_scope("weight_out"):
        near_out = jnp.concatenate([near_out, out_other], axis=0)
        out_parts = exchange([near_out] * 4, "y", "x")
    late_q, late_down, late_up = tie(q, after(low_down, kv_far), near_up)
    with jax.named_scope("weight_up"):
        near_up = jnp.concatenate([late_up, up_other], axis=0)
        up_other = swap(near_up, ("y",))
    with jax.named_scope("weight_down"):
        down_other = swap(late_down, ("h",))
    *attended, lse = call(
        forward_kernel,
        [((count, part), LOW)] * 4 + [((4, 4 * count), WIDE)],
        bits,
        late_q,
        kv,
        kv_far,
    )
    out_parts = [near_out] + [after(piece, lse) for piece in out_parts[1:]]
    near_out = jnp.concatenate(out_parts, axis=0)
    *attended, down_other, near_out = tie(*attended, after(down_other, lse), near_out)
    with jax.named_scope("attended"):
        attended = exchange(attended, "h", "l")
    with jax.named_scope("weight_out"):
        far_out = swap(near_out, ("c",))
        (full_out,) = call(lay_qkv_kernel, [((width, width), LOW)], bits, near_out, far_out)
    attended[1:3], up_other, down_other = lax.optimization_barrier(
        (attended[1:3], up_other, down_other)
    )
    with jax.named_scope("weight_up"):
        near_up = jnp.concatenate([near_up, up_other], axis=0)
        far_up = swap(near_up, ("c",))
    with jax.named_scope("weight_down"):
        near_down = jnp.concatenate([low_down, down_other], axis=0)
        down_other = swap(near_down, ("y",))
    hidden, hidden_low, normed, scale = call(
        out_kernel,
        [((count, width), WIDE), ((count, width), LOW), ((count, width), WIDE), ((count, 128), WIDE)],
        bits,
        *attended,
        full_out,
        rows,
        table,
    )

    half = count // 2
    with jax.named_scope("hidden"):
        from_l, from_x = swap(hidden_low, ("l",)), swap(hidden_low, ("x",))
    from_l, from_x, far_up, down_other = tie(
        from_l, from_x, after(far_up, from_l, from_x), after(down_other, from_l, from_x)
    )
    with jax.named_scope("hidden"):
        hidden_parts = [hidden_low, from_l, from_x]
        hidden_parts += [swap(from_x[:half], ("l",)), swap(from_l[half:], ("x",))]
    with jax.named_scope("weight_down"):
        near_down = jnp.concatenate([near_down, down_other], axis=0)
        far_down = swap(near_down, ("c",))
    (full_up,) = call(lay_up_kernel, [((width, units), LOW)], bits, near_up, far_up)
    (full_down,) = call(lay_down_kernel, [((units, width), LOW)], bits, near_down, far_down)
    parts_shape = [((count, width), WIDE)] * 3 + [((count // 2, width), LOW)] * 2
    act, slope = call(
        feed_up_kernel,
        [((4 * count, units), LOW)] * 2,
        bits,
        *hidden_parts,
        full_up,
        bias_units,
        flops=10**9,
    )
    parts = call(feed_down_kernel, parts_shape, bits, act, full_down)
    terms = scatter_square(parts, "x", "l")
    output, grad_two, grad_down, sums_two = call(
        norm_two_kernel,
        [((count, width), LOW), ((count, width), WIDE), ((count, width), LOW), ((8, width), WIDE)],
        bits,
        *terms,
        hidden,
        cotangent[0],
        table,
    )

    with jax.named_scope("grad_down"):
        grad_parts = gather_square(grad_down, "x", "l")
    grad_up, sums_up, *parts = call(
        feed_back_kernel,
        [((4 * count, units), LOW), ((8, units), WIDE)] + parts_shape,
        bits,
        *grad_parts,
        full_down,
        full_up,
        slope,
        flops=2 * 10**9,
    )
    with jax.named_scope("grad_hidden"):
        terms = scatter_square(parts, "x", "l")

    feed_near, feed_far = call(
        feed_grad_kernel,
        [((16 * own + 4 * down_rows, width), LOW)] * 2,
        bits,
        act,
        *grad_parts,
        *hidden_parts,
        grad_up,
        scratch=[pltpu.VMEM((units, width), LOW), pltpu.VMEM((width, units), LOW)],
    )

    def halve(value, axis, start=(), use=()):
        size = value.shape[0] // 2
        other = send(value[size:].astype(LOW), (axis,), start, use)
        return value[:size].astype(WIDE) + other.astype(WIDE)

    with jax.named_scope("grad_weight_feed"):
        feed_other = swap(feed_far, ("c",))
        feed_sum = (feed_near.astype(WIDE) + feed_other.astype(WIDE)).astype(LOW)
    *terms, feed_sum = lax.optimization_barrier((*terms, feed_sum))
    grad_middle, grad_branch, sums_one, *douts = call(
        norm_one_kernel,
        [((count, width), WIDE), ((count, width), LOW), ((8, width), WIDE)]
        + [((count, part), LOW)] * 4,
        bits,
        *terms,
        grad_two,
        normed,
        scale,
        full_out,
        table,
    )
    with jax.named_scope("grad_attended"):
        douts = exchange(douts, "h", "l")
    back = tuple(douts[1:])
    out_near, out_far = call(
        out_grad_kernel,
        [((16 * own, width), LOW)] * 2,
        bits,
        *attended,
        grad_branch,
        scratch=[pltpu.VMEM((width, width), LOW)],
    )
    with jax.named_scope("grad_weight_feed"):
        feed_other = send(feed_sum[feed_sum.shape[0] // 2 :], ("y",))
    with jax.named_scope("grad_weight_out"):
        out_other = send(out_far, ("c",), use=back)
        out_sum = (out_near.astype(WIDE) + out_other.astype(WIDE)).astype(LOW)
    late_lse, out_sum = lax.optimization_barrier((lse, out_sum))
    dq, dkv_near, dkv_far, sums_heads = call(
        backward_kernel,
        [
            ((4 * count, part), LOW),
            ((4 * count, 2 * part), WIDE),
            ((4 * count, 2 * part), LOW),
            ((8, part), WIDE),
        ],
        bits,
        q,
        kv,
        kv_far,
        late_lse,
        *douts,
    )
    with jax.named_scope("grad_weight_out"):
        out_sum = halve(out_sum, "x", use=(dq,)).astype(LOW)
    with jax.named_scope("grad_weight_feed"):
        half = feed_sum.shape[0] // 2
        feed_other = after(feed_other, dq)
        feed_sum = (feed_sum[:half].astype(WIDE) + feed_other.astype(WIDE)).astype(LOW)
    dkv_far, out_sum, feed_sum = lax.optimization_barrier((dkv_far, out_sum, feed_sum))
    up_size = 4 * own
    rows_of_part = lambda start, size: jnp.concatenate(
        [feed_sum[start : start + size], feed_sum[start + up_size + down_rows :][:size]], axis=0
    )
    up_sum, down_sum = rows_of_part(0, up_size), rows_of_part(up_size, down_rows)
    with jax.named_scope("grad_keys_values"):
        dkv_other = swap(dkv_far, ("c",))
    with jax.named_scope("grad_weight_out"):
        out_other = swap(out_sum[out_sum.shape[0] // 2 :], ("y",))
    with jax.named_scope("grad_weight_up"):
        up_other = swap(up_sum[up_size:], ("h",))
    near, far, grad_projected = call(
        qkv_grad_kernel,
        [((16 * tall, 3 * part), LOW)] * 2 + [((4 * count, 3 * part), LOW)],
        bits,
        *token_parts,
        dq,
        dkv_near,
        dkv_other,
        sums_heads,
        sums_one,
        sums_two,
        sums_up,
        scratch=[pltpu.VMEM((width, 3 * part), LOW), pltpu.VMEM((8, 8, 3 * part), WIDE)],
    )
    def add_first(value, other):
        return value[: other.shape[0]].astype(WIDE) + other.astype(WIDE)

    out_sum = add_first(out_sum, after(out_other, near)).astype(LOW)
    owned_up = add_first(up_sum, after(up_other, near)).astype(LOW)
    far, out_sum, owned_up = tie(far, out_sum, owned_up)
    with jax.named_scope("grad_weight_qkv"):
        far_other = swap(far, ("c",))
        qkv_sum = (near.astype(WIDE) + far_other.astype(WIDE)).astype(LOW)
    with jax.named_scope("grad_weight_out"):
        out_other = swap(out_sum[2 * own :], ("l",))
    with jax.named_scope("grad_weight_down"):
        down_other = send(down_sum[down_rows:], ("h",), start=(far,))
    parts = call(
        rows_grad_kernel,
        [((count, width), WIDE)] + [((count, width), LOW)] * 3,
        bits,
        after(grad_projected, far_other),
        full_qkv,
        grad_middle,
    )
    with jax.named_scope("grad_weight_qkv"):
        blocks = [qkv_sum[i * 4 * tall : (i + 1) * 4 * tall] for i in range(4)]
        blocks = exchange(blocks, "y", "x")
        owned_qkv = sum(block.astype(WIDE) for block in blocks).astype(LOW)
    late = tuple(blocks[1:])
    with jax.named_scope("grad_weight_up"):
        up_other = send(owned_up[2 * own :], ("x",), use=late)
    owned_down = add_first(down_sum, after(down_other, *late))
    out_sum = add_first(out_sum, after(out_other, *late)).astype(LOW)
    owned_qkv, up_other, owned_down, out_sum, *parts = tie(
        owned_qkv, up_other, owned_down, out_sum, *parts
    )
    with jax.named_scope("grad_weight_qkv"):
        qkv_pieces = exchange([owned_qkv[i * tall : (i + 1) * tall] for i in range(4)], "h", "l")
    last = tuple(qkv_pieces[1:])
    with jax.named_scope("grad_weight_up"):
        up_last = swap(jnp.concatenate([owned_up[own : 2 * own], up_other[own:]], axis=0), ("l",))
        up_last = after(up_last, *last)
        up_pieces = [owned_up[:own], up_last[:own], up_other[:own], up_last[own:]]
    with jax.named_scope("grad_weight_out"):
        owned_out = add_first(out_sum, send(out_sum[own:], ("h",), use=last))

    total, small_tile = call(
        squares_kernel,
        [((8, 128), WIDE), ((8, 3 * part), WIDE)],
        bits,
        owned_down,
        owned_out,
        *up_pieces,
        *qkv_pieces,
    )
    tile = width // 8
    lanes = 3 * part // tile
    small_tile = small_tile[:2].reshape(2 * lanes, tile)[:columns]
    owned_small = lax.dynamic_slice_in_dim(small_tile, (2 * il + ic) * own, own, axis=1).T
    def sum_square(value, a, b):
        terms = exchange([value] * 4, a, b)
        return (terms[0] + terms[1]) + (terms[2] + terms[3])

    with jax.named_scope("norm"):
        total = total + swap(total, ("c",))
        total = sum_square(total, "h", "l")
    with jax.named_scope("grad_tokens"):
        far_l = send(parts[3], ("l",), start=(total,))
        from_l = send(parts[1], ("l",), start=(total,))
        to_h = (parts[2].astype(WIDE) + far_l.astype(WIDE)).astype(LOW)
    with jax.named_scope("norm"):
        total = sum_square(total, "y", "x")
    total, to_h = tie(total, to_h)
    with jax.named_scope("grad_tokens"):
        from_h = swap(to_h, ("h",))
    grad_rows = parts[0] + from_l.astype(WIDE) + from_h.astype(WIDE)
    grad_norm = jnp.sqrt(total[0, 0])
    factor = jnp.minimum(1.0, CLIP_LIMIT / (grad_norm + 1e-06))
    held = jnp.full((1,), factor)

    states = [
        (weight_down, moment_down, second_down),
        (weight_out, moment_out, second_out),
        (weight_up, moment_up, second_up),
        (weight_qkv, moment_qkv, second_qkv),
    ]
    plans = [
        (RATE_MATRIX, whole_places, 1),
        (RATE_OUTPUT, whole_places, 1),
        (RATE_MATRIX, up_places, 4),
        (RATE_MATRIX, qkv_places, 4),
    ]
    grads = [owned_down, owned_out, *up_pieces, *qkv_pieces]
    flat = [array for group in states for array in group]
    results = pl.pallas_call(
        functools.partial(update_kernel, plans),
        name="update_kernel",
        in_specs=[pl.BlockSpec(memory_space=pltpu.SMEM)] * 2
        + [pl.BlockSpec(memory_space=pltpu.HBM)] * (len(grads) + 12),
        out_specs=[pl.BlockSpec(memory_space=pltpu.HBM)] * 12,
        out_shape=[jax.ShapeDtypeStruct(array.shape, WIDE) for array in flat],
        scratch_shapes=[pltpu.VMEM(grad.shape, grad.dtype) for grad in grads]
        + [pltpu.VMEM(array.shape, WIDE) for array in flat * 2]
        + [pltpu.SemaphoreType.DMA((len(grads),))]
        + [pltpu.SemaphoreType.DMA((12,))] * 2,
        compiler_params=pltpu.CompilerParams(vmem_limit_bytes=60 * 2**20),
        cost_estimate=pl.CostEstimate(flops=1, bytes_accessed=1, transcendentals=0),
    )(bits, held, *grads, *flat)
    new_down, new_moment_down, new_second_down = results[0:3]
    new_out, new_moment_out, new_second_out = results[3:6]
    new_up, new_moment_up, new_second_up = results[6:9]
    new_qkv, new_moment_qkv, new_second_qkv = results[9:12]
    new_small, new_moment_small, new_second_small = adam_update(
        small_params, owned_small * factor, moment_small, second_small, RATE_SMALL, 0.0
    )
    return (
        output[None],
        grad_rows[None],
        grad_norm,
        new_qkv,
        new_out,
        new_up,
        new_down,
        new_small,
        new_moment_qkv,
        new_moment_out,
        new_moment_up,
        new_moment_down,
        new_moment_small,
        new_second_qkv,
        new_second_out,
        new_second_up,
        new_second_down,
        new_second_small,
    )


def solution(mesh):
    sizes = (mesh.shape["dp"], mesh.shape["seq"])
    if sizes == (4, 8):
        squares = Mesh(mesh.devices.reshape(2, 2, 2, 2, 2), AXES)
        dp, seq = ("y", "x"), ("h", "l", "c")
        body, mesh = on_square, squares
        every = P(AXES, None)
        over = P(dp, seq, None)
    else:
        body = on_device
        every = P(("dp", "seq"), None)
        over = P("dp", "seq", None)
    return jax.shard_map(
        body,
        mesh=mesh,
        in_specs=(over,) * 2 + (every,) * 15,
        out_specs=(over,) * 2 + (P(),) + (every,) * 15,
        check_vma=False,
    )
```

```python
import functools
import math

import jax
import jax.numpy as jnp
from jax import lax
from jax.experimental import pallas as pl
from jax.experimental.pallas import tpu as pltpu
from jax.sharding import Mesh
from jax.sharding import PartitionSpec as P

HEAD = 64
STEP = 5


NORM_EPSILON = 1e-05
ADAM_EPSILON = 1e-08
BETA_FIRST = 0.5
BETA_SECOND = 0.55
CLIP_LIMIT = 1.0
RATE_MATRIX = 0.04
RATE_OUTPUT = 0.5
RATE_SMALL = 0.3
WEIGHT_DECAY = 0.01
SCORE_SCALE = 0.125


def layer_norm(value, gain, shift):
    center = jnp.mean(value, axis=-1, keepdims=True)
    centered = value - center
    variance = jnp.mean(centered * centered, axis=-1, keepdims=True)
    return centered * lax.rsqrt(variance + NORM_EPSILON) * gain + shift


def exact_gelu(value):
    return jax.nn.gelu(value, approximate=False)


def unpack(table_low):
    table = table_low.astype(jnp.float32)
    ratio = table.shape[1] - 8
    bias_up = table[:, 3 : 3 + ratio].T.reshape(-1)
    return (
        table[:, 0],
        table[:, 1],
        table[:, 2],
        bias_up,
        table[:, 3 + ratio],
        table[:, 4 + ratio],
        table[:, 5 + ratio],
        table[:, 6 + ratio],
        table[:, 7 + ratio],
    )


def cross(left, right):
    return lax.dot_general(
        left, right, (((0,), (0,)), ((), ())), preferred_element_type=jnp.float32
    )


def against(left, right):
    return lax.dot_general(
        left, right, (((1,), (1,)), ((), ())), preferred_element_type=jnp.float32
    )


def take_block(source, index, block, heads):
    piece = lax.dynamic_slice_in_dim(source, index * block, block, 0)
    return piece.reshape(block, heads, HEAD)


def scores_of(query_heads, key_heads):
    return (
        jnp.einsum("qhd,khd->hqk", query_heads, key_heads, preferred_element_type=jnp.float32)
        * SCORE_SCALE
    )


def block_grads(query_heads, key_heads, value_heads, dout_heads, log_total, delta):
    scores = scores_of(query_heads, key_heads)
    probs = jnp.exp(scores - log_total[..., None])
    grad_probs = jnp.einsum(
        "qhd,khd->hqk", dout_heads, value_heads, preferred_element_type=jnp.float32
    )
    grad_scores = (probs * (grad_probs - delta[..., None])).astype(jnp.bfloat16)
    return (probs, grad_scores)


def attention_forward(query_heads, keys_all, values_all, block):
    count_rows, heads = (query_heads.shape[0], query_heads.shape[1])
    count = keys_all.shape[0] // block

    def stats_step(index, carry):
        run_top, run_total = carry
        scores = scores_of(query_heads, take_block(keys_all, index, block, heads))
        new_top = jnp.maximum(run_top, jnp.max(scores, axis=-1))
        run_total = run_total * jnp.exp(run_top - new_top) + jnp.sum(
            jnp.exp(scores - new_top[..., None]), axis=-1
        )
        return (new_top, run_total)

    start_top = jnp.full((heads, count_rows), -1e30, jnp.float32)
    start_total = jnp.zeros((heads, count_rows), jnp.float32)
    run_top, run_total = lax.fori_loop(0, count, stats_step, (start_top, start_total))
    log_total = run_top + jnp.log(run_total)

    def value_step(index, accum):
        scores = scores_of(query_heads, take_block(keys_all, index, block, heads))
        weights = jnp.exp(scores - log_total[..., None]).astype(jnp.bfloat16)
        return accum + jnp.einsum(
            "hqk,khd->qhd",
            weights,
            take_block(values_all, index, block, heads),
            preferred_element_type=jnp.float32,
        )

    accum = lax.fori_loop(0, count, value_step, jnp.zeros((count_rows, heads, HEAD), jnp.float32))
    return (accum.reshape(count_rows, heads * HEAD), log_total)


def adam_update(weight, grad, moment, second, rate, decay):
    moment_new = BETA_FIRST * moment + (1.0 - BETA_FIRST) * grad
    second_new = BETA_SECOND * second + (1.0 - BETA_SECOND) * grad * grad
    direction = (
        moment_new
        / (1.0 - BETA_FIRST**STEP)
        / (jnp.sqrt(second_new / (1.0 - BETA_SECOND**STEP)) + ADAM_EPSILON)
    )
    return (weight - rate * (direction + decay * weight), moment_new, second_new)


def on_device(
    tokens,
    cotangent,
    weight_qkv,
    weight_out,
    weight_up,
    weight_down,
    small_params,
    moment_qkv,
    moment_out,
    moment_up,
    moment_down,
    moment_small,
    second_qkv,
    second_out,
    second_up,
    second_down,
    second_small,
):
    rows = tokens[0]
    count_rows = rows.shape[0]
    width = rows.shape[1]
    heads = width // HEAD
    block = 4 * count_rows
    full_qkv, full_out, full_up, full_down, full_small = (
        lax.all_gather(weight_qkv.astype(jnp.bfloat16), ("dp", "seq"), axis=0, tiled=True),
        lax.all_gather(weight_out.astype(jnp.bfloat16), ("dp", "seq"), axis=0, tiled=True),
        lax.all_gather(weight_up.astype(jnp.bfloat16), ("dp", "seq"), axis=0, tiled=True),
        lax.all_gather(weight_down.astype(jnp.bfloat16), ("dp", "seq"), axis=0, tiled=True),
        lax.all_gather(small_params.astype(jnp.bfloat16), ("dp", "seq"), axis=0, tiled=True),
    )
    (
        bias_query,
        bias_value,
        bias_out,
        bias_up,
        bias_down,
        gain_one,
        shift_one,
        gain_two,
        shift_two,
    ) = unpack(full_small)
    projected = jnp.dot(rows, full_qkv, preferred_element_type=jnp.float32)
    query = (projected[:, :width] + bias_query).astype(jnp.bfloat16)
    key_rows = projected[:, width : 2 * width].astype(jnp.bfloat16)
    value_rows = (projected[:, 2 * width :] + bias_value).astype(jnp.bfloat16)
    keys_all, values_all = (
        lax.all_gather(key_rows, "seq", axis=0, tiled=True),
        lax.all_gather(value_rows, "seq", axis=0, tiled=True),
    )
    query_heads = query.reshape(count_rows, heads, HEAD)
    attended, log_total = attention_forward(query_heads, keys_all, values_all, block)
    attended_low = attended.astype(jnp.bfloat16)
    branch = jnp.dot(attended_low, full_out, preferred_element_type=jnp.float32) + bias_out
    middle = rows.astype(jnp.float32) + branch
    hidden, norm_one_back = jax.vjp(layer_norm, middle, gain_one, shift_one)
    hidden_low = hidden.astype(jnp.bfloat16)
    upward = jnp.dot(hidden_low, full_up, preferred_element_type=jnp.float32) + bias_up
    activation, gelu_back = jax.vjp(exact_gelu, upward)
    activation_low = activation.astype(jnp.bfloat16)
    downward = jnp.dot(activation_low, full_down, preferred_element_type=jnp.float32) + bias_down
    output, norm_two_back = jax.vjp(layer_norm, hidden + downward, gain_two, shift_two)
    back_qkv, back_out, back_up, back_down = (full_qkv, full_out, full_up, full_down)
    grad_sum_two, grad_gain_two, grad_shift_two = norm_two_back(cotangent[0].astype(jnp.float32))
    grad_down_low = grad_sum_two.astype(jnp.bfloat16)
    grad_bias_down = jnp.sum(grad_down_low.astype(jnp.float32), axis=0)
    grad_weight_down = cross(activation_low, grad_down_low)
    grad_activation = against(grad_down_low, back_down)
    grad_up_low = gelu_back(grad_activation)[0].astype(jnp.bfloat16)
    grad_bias_up = jnp.sum(grad_up_low.astype(jnp.float32), axis=0)
    grad_weight_up = cross(hidden_low, grad_up_low)
    grad_hidden = grad_sum_two + against(grad_up_low, back_up)
    grad_middle, grad_gain_one, grad_shift_one = norm_one_back(grad_hidden)
    grad_branch_low = grad_middle.astype(jnp.bfloat16)
    grad_bias_out = jnp.sum(grad_branch_low.astype(jnp.float32), axis=0)
    grad_weight_out = cross(attended_low, grad_branch_low)
    grad_attended = against(grad_branch_low, back_out).astype(jnp.bfloat16)
    delta = jnp.sum(
        (grad_attended.astype(jnp.float32) * attended).reshape(count_rows, heads, HEAD), axis=-1
    ).T
    dout_heads = grad_attended.reshape(count_rows, heads, HEAD)
    count = keys_all.shape[0] // block

    def both_step(index, carry):
        grad_query, grad_keys, grad_values = carry
        key_heads = take_block(keys_all, index, block, heads)
        value_heads = take_block(values_all, index, block, heads)
        probs, grad_scores = block_grads(
            query_heads, key_heads, value_heads, dout_heads, log_total, delta
        )
        grad_query = (
            grad_query
            + jnp.einsum("hqk,khd->qhd", grad_scores, key_heads, preferred_element_type=jnp.float32)
            * SCORE_SCALE
        )
        part_keys = (
            jnp.einsum("hqk,qhd->khd", grad_scores, query_heads, preferred_element_type=jnp.float32)
            * SCORE_SCALE
        )
        part_values = jnp.einsum(
            "hqk,qhd->khd",
            probs.astype(jnp.bfloat16),
            dout_heads,
            preferred_element_type=jnp.float32,
        )
        grad_keys = lax.dynamic_update_slice_in_dim(
            grad_keys, part_keys.reshape(block, width), index * block, 0
        )
        grad_values = lax.dynamic_update_slice_in_dim(
            grad_values, part_values.reshape(block, width), index * block, 0
        )
        return (grad_query, grad_keys, grad_values)

    start = (
        jnp.zeros((count_rows, heads, HEAD), jnp.float32),
        jnp.zeros((keys_all.shape[0], width), jnp.float32),
        jnp.zeros((keys_all.shape[0], width), jnp.float32),
    )
    grad_query, grad_keys, grad_values = lax.fori_loop(0, count, both_step, start)
    summed_keys, summed_values = (
        lax.psum_scatter(
            grad_keys.astype(jnp.bfloat16), "seq", scatter_dimension=0, tiled=True
        ).astype(jnp.float32),
        lax.psum_scatter(
            grad_values.astype(jnp.bfloat16), "seq", scatter_dimension=0, tiled=True
        ).astype(jnp.float32),
    )
    grad_query_low = grad_query.reshape(count_rows, width).astype(jnp.bfloat16)
    grad_value_low = summed_values.astype(jnp.bfloat16)
    grad_projected = jnp.concatenate(
        [grad_query_low, summed_keys.astype(jnp.bfloat16), grad_value_low], axis=1
    )
    grad_weight_qkv = cross(rows, grad_projected)
    grad_bias_query = jnp.sum(grad_query_low.astype(jnp.float32), axis=0)
    grad_bias_value = jnp.sum(grad_value_low.astype(jnp.float32), axis=0)
    grad_rows = grad_middle + against(grad_projected, back_qkv)
    ratio = full_up.shape[1] // width
    grad_small = jnp.concatenate(
        [
            jnp.stack([grad_bias_query, grad_bias_value, grad_bias_out], axis=1),
            grad_bias_up.reshape(ratio, width).T,
            jnp.stack(
                [grad_bias_down, grad_gain_one, grad_shift_one, grad_gain_two, grad_shift_two],
                axis=1,
            ),
        ],
        axis=1,
    )
    owned_qkv, owned_out, owned_up, owned_down, owned_small = (
        lax.psum_scatter(grad_weight_qkv, ("dp", "seq"), scatter_dimension=0, tiled=True),
        lax.psum_scatter(grad_weight_out, ("dp", "seq"), scatter_dimension=0, tiled=True),
        lax.psum_scatter(grad_weight_up, ("dp", "seq"), scatter_dimension=0, tiled=True),
        lax.psum_scatter(grad_weight_down, ("dp", "seq"), scatter_dimension=0, tiled=True),
        lax.psum_scatter(grad_small, ("dp", "seq"), scatter_dimension=0, tiled=True),
    )
    squares = jnp.sum(owned_qkv * owned_qkv) + jnp.sum(owned_out * owned_out)
    squares = squares + jnp.sum(owned_up * owned_up) + jnp.sum(owned_down * owned_down)
    squares = squares + jnp.sum(owned_small * owned_small)
    total = lax.psum(squares, ("dp", "seq"))
    grad_norm = jnp.sqrt(total)
    factor = jnp.minimum(1.0, CLIP_LIMIT / (grad_norm + 1e-06))
    new_qkv, new_moment_qkv, new_second_qkv = adam_update(
        weight_qkv, owned_qkv * factor, moment_qkv, second_qkv, RATE_MATRIX, WEIGHT_DECAY
    )
    new_out, new_moment_out, new_second_out = adam_update(
        weight_out, owned_out * factor, moment_out, second_out, RATE_OUTPUT, WEIGHT_DECAY
    )
    new_up, new_moment_up, new_second_up = adam_update(
        weight_up, owned_up * factor, moment_up, second_up, RATE_MATRIX, WEIGHT_DECAY
    )
    new_down, new_moment_down, new_second_down = adam_update(
        weight_down, owned_down * factor, moment_down, second_down, RATE_MATRIX, WEIGHT_DECAY
    )
    new_small, new_moment_small, new_second_small = adam_update(
        small_params, owned_small * factor, moment_small, second_small, RATE_SMALL, 0.0
    )
    return (
        output.astype(jnp.bfloat16)[None],
        grad_rows[None],
        grad_norm,
        new_qkv,
        new_out,
        new_up,
        new_down,
        new_small,
        new_moment_qkv,
        new_moment_out,
        new_moment_up,
        new_moment_down,
        new_moment_small,
        new_second_qkv,
        new_second_out,
        new_second_up,
        new_second_down,
        new_second_small,
    )


AXES = ("y", "x", "h", "l", "c")
LOW = jnp.bfloat16
WIDE = jnp.float32


def swap(value, axes):
    axes = tuple(name for name in AXES if name in axes)
    last = 2 ** len(axes) - 1
    return lax.ppermute(value, axes, [(i, i ^ last) for i in range(last + 1)])


def after(value, *events):
    return lax.optimization_barrier((value, *events))[0]


def tie(*values):
    return lax.optimization_barrier(values)


def send(value, axes, start=(), use=()):
    got = swap(after(value, *start) if start else value, axes)
    return after(got, *use) if use else got


def exchange(parts, a, b, start=(), use=()):
    ways = ((b,), (a,), (a, b))
    return [parts[0]] + [send(part, way, start, use) for part, way in zip(parts[1:], ways)]


def gather_square(value, a, b):
    half = value.shape[0] // 2
    from_a, from_b = swap(value, (a,)), swap(value, (b,))
    return [value, from_b, from_a, swap(from_a[:half], (b,)), swap(from_b[half:], (a,))]


def scatter_square(parts, a, b):
    own, to_b, to_a, far_first, far_second = parts
    half = own.shape[0] // 2
    first = swap(far_first, (a,))
    second = swap(far_second, (b,))
    to_b = jnp.concatenate([to_b[:half] + first.astype(WIDE), to_b[half:]], axis=0).astype(LOW)
    to_a = jnp.concatenate([to_a[:half], to_a[half:] + second.astype(WIDE)], axis=0).astype(LOW)
    return own, swap(to_b, (b,)), swap(to_a, (a,))


def gather_ring(value, a, b, start=(), use=()):
    from_b = send(value, (b,), start, use)
    from_a = swap(after(value, *start) if start else value, (a,))
    far = send(from_a, (b,), use=use)
    return [value, from_b, after(from_a, *use) if use else from_a, far]


def dot(left, right):
    return jnp.dot(left, right, preferred_element_type=WIDE)


def call(kernel, outs, *args, scratch=(), flops=10**9, scalars=0):
    outs = [jax.ShapeDtypeStruct(shape, kind) for shape, kind in outs]
    return pl.pallas_call(
        kernel,
        name=getattr(kernel, "func", kernel).__name__,
        in_specs=[pl.BlockSpec(memory_space=pltpu.SMEM)] * (1 + scalars)
        + [pl.BlockSpec(memory_space=pltpu.VMEM)] * (len(args) - 1 - scalars),
        out_specs=[pl.BlockSpec(memory_space=pltpu.VMEM)] * len(outs),
        out_shape=outs,
        scratch_shapes=list(scratch),
        compiler_params=pltpu.CompilerParams(vmem_limit_bytes=48 * 2**20),
        cost_estimate=pl.CostEstimate(flops=1, bytes_accessed=1, transcendentals=0),
    )(*args)


def at(start, size):
    return pl.ds(pl.multiple_of(start, size), size)


def indices(bits):
    iy, ix, ih, il, ic = (bits[i] for i in range(5))
    return 2 * iy + ix, 2 * ih + il, ic


def pack_qkv_kernel(bits, weight, small, *outs):
    _, z, _ = indices(bits)
    own = weight.shape[0]
    size = outs[0].shape[1] // 3
    for r, out in enumerate(outs):
        for kind in range(3):
            start = kind * 4 * size + (z ^ r) * size
            out[:own, kind * size : (kind + 1) * size] = weight[:, at(start, size)].astype(LOW)
        out[own:, :] = small[...]


def pack_rest_kernel(bits, out_weight, up, down, low_out, low_down, near_up, far_up):
    iy, ix, ih, il, ic = (bits[i] for i in range(5))
    own = up.shape[0]
    size = up.shape[1] // 16
    low_out[...] = out_weight[...].astype(LOW)
    low_down[...] = down[...].astype(LOW)
    for r in range(4):
        out, rows = (near_up, far_up)[r // 2], slice(r % 2 * own, (r % 2 + 1) * own)
        x, l = ix ^ (r // 2), il ^ (r % 2)
        for y in range(2):
            for h in range(2):
                start = (((y * 2 + x) * 2 + h) * 2 + l) * size
                to = (y * 2 + h) * size
                out[rows, to : to + size] = up[:, at(start, size)].astype(LOW)


def lay_rows(bits, full, pieces, own, stride, c):
    d, z, _ = indices(bits)
    for p, piece in enumerate(pieces):
        for s in range(4):
            to = (d ^ p) * 8 * own + (z ^ s) * 2 * own + c * own
            full[at(to, own), :] = piece[s * stride : s * stride + own, :]


def lay_qkv_kernel(bits, near, far, full):
    own = full.shape[0] // 32
    stride = near.shape[0] // 16
    c = bits[4]
    for ref, core in ((near, c), (far, 1 - c)):
        pieces = [ref.at[p * 4 * stride : (p + 1) * 4 * stride] for p in range(4)]
        lay_rows(bits, full, pieces, own, stride, core)


def lay_up_kernel(bits, near, far, full):
    iy, ix, ih, il, ic = (bits[i] for i in range(5))
    own = full.shape[0] // 32
    for ref, core in ((near, ic), (far, 1 - ic)):
        for p in range(4):
            y, h = iy ^ (p // 2), ih ^ (p % 2)
            for q in range(4):
                x, l = ix ^ (q // 2), il ^ (q % 2)
                to = ((((y * 2 + x) * 2 + h) * 2 + l) * 2 + core) * own
                full[at(to, own), :] = ref[(4 * p + q) * own : (4 * p + q + 1) * own, :]


def lay_down_kernel(bits, near, far, full):
    iy, _, ih, _, ic = (bits[i] for i in range(5))
    size = full.shape[0] // 8
    for ref, core in ((near, ic), (far, 1 - ic)):
        for p in range(4):
            to = (((iy ^ (p // 2)) * 2 + (ih ^ (p % 2))) * 2 + core) * size
            full[at(to, size), :] = ref[p * size : (p + 1) * size, :]


def project_kernel(
    bits, bias, near_ref, far_ref, t0, t1, t2, t3, q_ref, kv_ref, full_ref, near, far, rows, sems
):
    d, z, c = indices(bits)
    count = t0.shape[0]
    own = full_ref.shape[0] // 32
    tall = near.shape[0] // 16
    size = q_ref.shape[1]
    pairs = [(near_ref, near), (far_ref, far)]
    pairs += [(ref, rows.at[i * count : (i + 1) * count]) for i, ref in enumerate((t0, t1, t2, t3))]
    copies = [pltpu.make_async_copy(*pair, sems.at[i]) for i, pair in enumerate(pairs)]
    for copy in copies:
        copy.start()
    for copy in copies[:2]:
        copy.wait()
    for ref, core in ((near, c), (far, 1 - c)):
        for p in range(4):
            for s in range(4):
                to = (d ^ p) * 8 * own + (z ^ s) * 2 * own + core * own
                full_ref[at(to, own), :] = ref[(4 * p + s) * tall : (4 * p + s) * tall + own, :]
    for copy in copies[2:]:
        copy.wait()
    projected = dot(rows[...], full_ref[...])
    q_ref[...] = (projected[:, :size] + bias[0:1, :]).astype(LOW)
    kv_ref[:, :size] = projected[:, size : 2 * size].astype(LOW)
    kv_ref[:, size:] = (projected[:, 2 * size :] + bias[1:2, :]).astype(LOW)


def head_mask(shape, axis, head):
    lane = lax.broadcasted_iota(jnp.int32, shape, axis)
    return (lane < HEAD) if head == 0 else (lane >= HEAD)


def forward_kernel(bits, q_ref, near, far, *outs):
    lse_ref = outs[-1]
    count = outs[0].shape[0]
    width = q_ref.shape[1]
    pair = 2 * HEAD
    for group in range(width // pair):
        cols = slice(group * pair, (group + 1) * pair)
        value_cols = slice(width + group * pair, width + (group + 1) * pair)
        keys = jnp.concatenate([near[:, cols], far[:, cols]], axis=0)
        values_t = jnp.concatenate([near[:, value_cols], far[:, value_cols]], axis=0).T
        for piece in range(2):
            rows = slice(2 * piece * count, 2 * (piece + 1) * count)
            queries = q_ref[rows, cols]
            zero = jnp.zeros_like(queries)
            halves = []
            for head in range(2):
                query = jnp.where(head_mask(queries.shape, 1, head), queries, zero)
                scores = against(keys, query) * SCORE_SCALE
                top = jnp.max(scores, axis=0, keepdims=True)
                weights = jnp.exp(scores - top)
                total = jnp.sum(weights, axis=0, keepdims=True)
                at_head = 2 * group + head
                lse_ref[at_head : at_head + 1, rows] = top + jnp.log(total)
                probs = (weights * (1.0 / total)).astype(LOW)
                halves.append(dot(values_t, probs))
            mask = head_mask(halves[0].shape, 0, 0)
            result = jnp.where(mask, halves[0], halves[1]).T.astype(LOW)
            outs[2 * piece][:, cols] = result[:count]
            outs[2 * piece + 1][:, cols] = result[count:]


def backward_kernel(
    bits, q_ref, near, far, lse_ref, d0, d1, d2, d3, dq_ref, near_ref, far_ref, sums
):
    count = d0.shape[0]
    length = 2 * near.shape[0]
    width = q_ref.shape[1]
    pair = 2 * HEAD
    for group in range(width // pair):
        cols = slice(group * pair, (group + 1) * pair)
        value_cols = slice(width + group * pair, width + (group + 1) * pair)
        keys = jnp.concatenate([near[:, cols], far[:, cols]], axis=0)
        values = jnp.concatenate([near[:, value_cols], far[:, value_cols]], axis=0)
        keys_t = keys.T
        sum_keys = jnp.zeros((length, pair), WIDE)
        sum_values = jnp.zeros((length, pair), WIDE)
        bias_query = jnp.zeros((1, pair), WIDE)
        for piece in range(2):
            rows = slice(2 * piece * count, 2 * (piece + 1) * count)
            queries = q_ref[rows, cols]
            refs = (d0, d1) if piece == 0 else (d2, d3)
            douts = jnp.concatenate([refs[0][:, cols], refs[1][:, cols]], axis=0)
            zero = jnp.zeros_like(queries)
            all_probs, all_grads, all_query, all_dout, halves = [], [], [], [], []
            for head in range(2):
                mask = head_mask(queries.shape, 1, head)
                query = jnp.where(mask, queries, zero)
                dout = jnp.where(mask, douts, zero)
                at_head = 2 * group + head
                scores = against(keys, query) * SCORE_SCALE
                probs = jnp.exp(scores - lse_ref[at_head : at_head + 1, rows])
                grad_probs = against(values, dout)
                delta = jnp.sum(probs * grad_probs, axis=0, keepdims=True)
                grads = (probs * (grad_probs - delta)).astype(LOW)
                all_probs.append(probs.astype(LOW))
                all_grads.append(grads)
                all_query.append(query)
                all_dout.append(dout)
                halves.append(dot(keys_t, grads))
            mask = head_mask(halves[0].shape, 0, 0)
            dq = jnp.where(mask, halves[0], halves[1]) * SCORE_SCALE
            dq = dq.T.astype(LOW)
            dq_ref[rows, cols] = dq
            bias_query += jnp.sum(dq.astype(WIDE), axis=0, keepdims=True)
            sum_keys += dot(jnp.concatenate(all_grads, axis=1), jnp.concatenate(all_query, axis=0))
            sum_values += dot(jnp.concatenate(all_probs, axis=1), jnp.concatenate(all_dout, axis=0))
        sum_keys = sum_keys * SCORE_SCALE
        half = length // 2
        near_ref[:, cols] = sum_keys[:half]
        far_ref[:, cols] = sum_keys[half:].astype(LOW)
        sums[0:1, cols] = bias_query
        sums[1:2, cols] = jnp.sum(sum_values, axis=0, keepdims=True)
        near_ref[:, value_cols] = sum_values[:half]
        far_ref[:, value_cols] = sum_values[half:].astype(LOW)


def row_mean(value):
    return jnp.mean(value, axis=-1, keepdims=True)


def column_sums(out, *values):
    out[...] = jnp.zeros_like(out)
    for index, value in enumerate(values):
        out[index : index + 1, :] = jnp.sum(value, axis=0, keepdims=True)


def out_kernel(bits, a0, a1, a2, a3, weight, tokens, table, hidden, low, normed, scale):
    _, z, _ = indices(bits)
    size = a0.shape[1]
    branch = jnp.zeros(hidden.shape, WIDE)
    for r, piece in enumerate((a0, a1, a2, a3)):
        branch += dot(piece[...], weight[at((z ^ r) * size, size), :])
    middle = tokens[...].astype(WIDE) + (branch + table[2:3, :])
    centered = middle - row_mean(middle)
    inverse = lax.rsqrt(row_mean(centered * centered) + NORM_EPSILON)
    unit = centered * inverse
    value = unit * table[-4:-3, :] + table[-3:-2, :]
    hidden[...] = value
    low[...] = value.astype(LOW)
    normed[...] = unit
    scale[...] = jnp.broadcast_to(inverse, scale.shape)


def store_parts(product, own, to_b, to_a, far_first, far_second):
    count = own.shape[0]
    half = count // 2
    own[...] = product[:count]
    to_b[...] = product[count : 2 * count]
    to_a[...] = product[2 * count : 3 * count]
    far_first[...] = product[3 * count : 3 * count + half].astype(LOW)
    far_second[...] = product[3 * count + half :].astype(LOW)


def feed_up_kernel(bits, h0, h1, h2, h3, h4, up, bias, act, slope):
    hidden = jnp.concatenate([ref[...] for ref in (h0, h1, h2, h3, h4)], axis=0)
    upward = dot(hidden, up[...]) + bias[...]
    half = (1.0 + lax.erf(upward * (0.5**0.5))) * 0.5
    act[...] = (upward * half).astype(LOW)
    bell = jnp.exp(upward * upward * -0.5) * (0.5 * 2.0**0.5 * math.pi**-0.5)
    slope[...] = (half + upward * bell).astype(LOW)


def feed_down_kernel(bits, act, down, *parts):
    store_parts(dot(act[...], down[...]), *parts)


def norm_two_kernel(bits, own, from_b, from_a, hidden, cot, table, output, grad, low, sums):
    downward = own[...] + from_b[...].astype(WIDE) + from_a[...].astype(WIDE)
    value = hidden[...] + (downward + table[-5:-4, :])
    centered = value - row_mean(value)
    inverse = lax.rsqrt(row_mean(centered * centered) + NORM_EPSILON)
    unit = centered * inverse
    gain = table[-2:-1, :]
    output[...] = (unit * gain + table[-1:, :]).astype(LOW)
    cotangent = cot[...].astype(WIDE)
    inner = cotangent * gain
    result = inverse * (inner - row_mean(inner) - unit * row_mean(inner * unit))
    grad[...] = result
    rounded = result.astype(LOW)
    low[...] = rounded
    column_sums(sums, rounded.astype(WIDE), cotangent * unit, cotangent)


def feed_back_kernel(bits, g0, g1, g2, g3, g4, down, up, slope, grad_up, sums, *parts):
    grads = jnp.concatenate([ref[...] for ref in (g0, g1, g2, g3, g4)], axis=0)
    upward = (against(grads, down[...]) * slope[...].astype(WIDE)).astype(LOW)
    grad_up[...] = upward
    column_sums(sums, upward.astype(WIDE))
    store_parts(against(upward, up[...]), *parts)


def feed_grad_kernel(
    bits, act, g0, g1, g2, g3, g4, h0, h1, h2, h3, h4, grad_up, near, far, down_full, up_full
):
    iy, ix, ih, il, ic = (bits[i] for i in range(5))
    grads = jnp.concatenate([ref[...] for ref in (g0, g1, g2, g3, g4)], axis=0)
    hidden = jnp.concatenate([ref[...] for ref in (h0, h1, h2, h3, h4)], axis=0)
    down_full[...] = cross(act[...], grads).astype(LOW)
    up_full[...] = cross(hidden, grad_up[...]).astype(LOW)
    own = up_full.shape[0] // 32
    size = down_full.shape[0] // 8
    for p in range(4):
        y, h = iy ^ (p // 2), ih ^ (p % 2)
        base = p * (4 * own + size)
        for q in range(4):
            x, l = ix ^ (q // 2), il ^ (q % 2)
            start = ((((y * 2 + x) * 2 + h) * 2 + l) * 2) * own
            to = base + q * own
            near[to : to + own, :] = up_full[at(start + ic * own, own), :]
            far[to : to + own, :] = up_full[at(start + (1 - ic) * own, own), :]
        start = (y * 2 + h) * 2
        to = base + 4 * own
        near[to : to + size, :] = down_full[at((start + ic) * size, size), :]
        far[to : to + size, :] = down_full[at((start + 1 - ic) * size, size), :]


def norm_one_kernel(
    bits, own, from_b, from_a, above, normed, scale, weight, table, grad, low, sums, *pieces
):
    _, z, _ = indices(bits)
    hidden = own[...] + from_b[...].astype(WIDE) + from_a[...].astype(WIDE)
    hidden = above[...] + hidden
    unit = normed[...]
    inner = hidden * table[-4:-3, :]
    result = scale[:, 0:1] * (inner - row_mean(inner) - unit * row_mean(inner * unit))
    grad[...] = result
    rounded = result.astype(LOW)
    low[...] = rounded
    column_sums(sums, rounded.astype(WIDE), hidden * unit, hidden)
    size = pieces[0].shape[1]
    for r, piece in enumerate(pieces):
        piece[...] = against(rounded, weight[at((z ^ r) * size, size), :]).astype(LOW)


def split_rows(bits, full, near, far, order=(0, 1, 2, 3)):
    d, z, c = indices(bits)
    own = full.shape[0] // 32
    for p in range(4):
        for s in range(4):
            start = (d ^ order[p]) * 8 * own + (z ^ order[s]) * 2 * own
            to = (4 * p + s) * own
            near[to : to + own, :] = full[at(start + c * own, own), :]
            far[to : to + own, :] = full[at(start + (1 - c) * own, own), :]


def out_grad_kernel(bits, a0, a1, a2, a3, grad, near, far, full):
    _, z, _ = indices(bits)
    size = a0.shape[1]
    for r, piece in enumerate((a0, a1, a2, a3)):
        full[at((z ^ r) * size, size), :] = cross(piece[...], grad[...]).astype(LOW)
    split_rows(bits, full, near, far, order=(0, 2, 1, 3))


def qkv_grad_kernel(
    bits, t0, t1, t2, t3, dq, dkv, other, heads, one, two, up, near, far, grads, full, extra
):
    d, z, c = indices(bits)
    tokens = jnp.concatenate([t0[...], t1[...], t2[...], t3[...]], axis=0)
    size = dq.shape[1]
    both = (dkv[...] + other[...].astype(WIDE)).astype(LOW)
    grads[:, :size] = dq[...]
    grads[:, size:] = both
    full[...] = cross(tokens, grads[...]).astype(LOW)
    own = full.shape[0] // 32
    tile = full.shape[0] // 8
    lanes = full.shape[1] // tile
    tall = near.shape[0] // 16
    extra[...] = jnp.zeros_like(extra)
    ratio = up.shape[1] // size
    rows = [(one, 0)] + [None] * ratio + [(two, 0), (one, 1), (one, 2), (two, 1), (two, 2)]
    for k in range(8):
        values = []
        for row in range(2):
            value = heads[row : row + 1, k % 2 * tile : (k % 2 + 1) * tile]
            values.append(jnp.where(z == k // 2, value, 0.0))
        for index, source in enumerate(rows):
            if source is None:
                y, x = (index - 1) // 2, (index - 1) % 2
                lane = ((y * 2 + k // 4) * 2 + k % 2) * tile
                mine = jnp.logical_and(bits[1] == x, bits[3] == k // 2 % 2)
                values.append(jnp.where(mine, up[0:1, lane : lane + tile], 0.0))
            else:
                ref, row = source
                values.append(ref[row : row + 1, k * tile : (k + 1) * tile])
        for column, value in enumerate(values):
            row, lane = column // lanes, column % lanes * tile
            extra[k, row : row + 1, lane : lane + tile] = value
    for p in range(4):
        for s in range(4):
            start = (d ^ p) * 8 * own + (z ^ s) * 2 * own
            to = (4 * p + s) * tall
            near[to : to + own, :] = full[at(start + c * own, own), :]
            far[to : to + own, :] = full[at(start + (1 - c) * own, own), :]
            rows = extra[(d ^ p) * 2 + (z ^ s) // 2].astype(LOW)
            near[to + own : to + tall, :] = rows
            far[to + own : to + tall, :] = rows


def rows_grad_kernel(bits, grads, weight, above, own, *parts):
    product = against(grads[...], weight[...])
    count = own.shape[0]
    own[...] = above[...] + product[:count]
    for r, part in enumerate(parts):
        part[...] = product[(r + 1) * count : (r + 2) * count].astype(LOW)


def squares_kernel(bits, down, out, u0, u1, u2, u3, p0, p1, p2, p3, result, small):
    _, _, c = indices(bits)
    own = out.shape[0]
    values = [ref[...].astype(WIDE) for ref in (down, out, u0, u1, u2, u3)]
    values += [ref[:own, :].astype(WIDE) for ref in (p0, p1, p2, p3)]
    rows = sum(ref[own:, :].astype(WIDE) for ref in (p0, p1, p2, p3))
    small[...] = rows
    lane = lax.broadcasted_iota(jnp.int32, rows.shape, 1) % 128
    mine = (lane // own) == bits[3] * 2 + c
    values.append(jnp.where(mine, rows, 0.0))
    total = jnp.zeros((1, 1), WIDE)
    for value in values:
        total += jnp.sum(jnp.sum(value * value, axis=0, keepdims=True), axis=1, keepdims=True)
    result[...] = jnp.broadcast_to(total, result.shape)


def update_kernel(plans, bits, factor, *refs):
    count = len(plans)
    total = sum(plan[2] for plan in plans)
    sources, refs = refs[:total], refs[total:]
    grads, refs = refs[6 * count : 6 * count + total], refs[: 6 * count] + refs[6 * count + total :]
    brought = refs[-3]
    fetches = [
        pltpu.make_async_copy(sources[i], grads[i], brought.at[i]) for i in range(total)
    ]
    for fetch in fetches:
        fetch.start()
    states, results = refs[: 3 * count], refs[3 * count : 6 * count]
    held, made = refs[6 * count : 9 * count], refs[9 * count : 12 * count]
    arrive, leave = refs[-2:]
    loads = [
        pltpu.make_async_copy(states[i], held[i], arrive.at[i]) for i in range(3 * count)
    ]
    stores = [
        pltpu.make_async_copy(made[i], results[i], leave.at[i]) for i in range(3 * count)
    ]
    for load in loads:
        load.start()
    _, z, _ = indices(bits)
    first = 0
    for index, (rate, places, pieces) in enumerate(plans):
        mine = slice(3 * index, 3 * index + 3)
        for load in loads[mine] + fetches[first : first + pieces]:
            load.wait()
        own = held[3 * index].shape[0]
        for r in range(pieces):
            piece = grads[first + r]
            for source, target in places(bits, z, r, piece.shape[1]):
                grad = piece[:own, source].astype(WIDE) * factor[0]
                weight, moment, second = (ref[:, target] for ref in held[mine])
                values = adam_update(weight, grad, moment, second, rate, WEIGHT_DECAY)
                for ref, value in zip(made[mine], values):
                    ref[:, target] = value
        for store in stores[mine]:
            store.start()
        first += pieces
    for store in stores:
        store.wait()


def whole_places(bits, z, r, columns):
    return [(slice(None), slice(None))]


def qkv_places(bits, z, r, columns):
    size = columns // 3
    return [
        (slice(kind * size, (kind + 1) * size), at(kind * 4 * size + (z ^ r) * size, size))
        for kind in range(3)
    ]


def up_places(bits, z, r, columns):
    size = columns // 4
    x, l = bits[1] ^ (r // 2), bits[3] ^ (r % 2)
    return [
        (
            slice((2 * y + h) * size, (2 * y + h + 1) * size),
            at((((y * 2 + x) * 2 + h) * 2 + l) * size, size),
        )
        for y in range(2)
        for h in range(2)
    ]


def on_square(
    tokens,
    cotangent,
    weight_qkv,
    weight_out,
    weight_up,
    weight_down,
    small_params,
    moment_qkv,
    moment_out,
    moment_up,
    moment_down,
    moment_small,
    second_qkv,
    second_out,
    second_up,
    second_down,
    second_small,
):
    rows = tokens[0]
    count, width = rows.shape
    own = weight_qkv.shape[0]
    down_rows = weight_down.shape[0]
    ratio = weight_up.shape[1] // width
    columns = small_params.shape[1]
    part = width // 4
    units = weight_up.shape[1] // 4
    pad = 8
    tall = own + pad
    iy, ix, ih, il, ic = (lax.axis_index(name) for name in AXES)
    bits = jnp.stack([iy, ix, ih, il, ic]).astype(jnp.int32)
    at_dp, at_z = 2 * iy + ix, 2 * ih + il
    place = 8 * at_dp + 2 * at_z + ic

    low_small = small_params.astype(LOW).T.reshape(1, own * columns)
    low_small = jnp.pad(low_small, ((0, pad - 1), (0, 3 * part - own * columns)))
    with jax.named_scope("weight_qkv"):
        pieces = call(pack_qkv_kernel, [((tall, 3 * part), LOW)] * 4, bits, weight_qkv, low_small)
    with jax.named_scope("tokens"):
        token_l, token_h = swap(rows, ("l",)), swap(rows, ("h",))
    low_out, low_down, up_near, up_far = call(
        pack_rest_kernel,
        [((own, width), LOW), ((down_rows, width), LOW)] + [((2 * own, units), LOW)] * 2,
        bits,
        weight_out,
        weight_up,
        weight_down,
    )
    with jax.named_scope("weight_qkv"):
        near_qkv = jnp.concatenate(exchange(pieces, "h", "l"), axis=0)
        near_qkv = after(near_qkv, token_l, low_out)
    with jax.named_scope("weight_up"):
        up_far = send(up_far, ("x",), start=(near_qkv,))
        up_last = swap(jnp.concatenate([up_near[own:], up_far[own:]], axis=0), ("l",))
        near_up = [up_near[:own], up_last[:own], up_far[:own], up_last[own:]]
        near_up = jnp.concatenate(near_up, axis=0)
    with jax.named_scope("weight_out"):
        out_other = send(low_out, ("l",), start=(near_qkv,))
    with jax.named_scope("weight_qkv"):
        near_qkv = jnp.concatenate(exchange([near_qkv] * 4, "y", "x"), axis=0)
    near_qkv, token_h, near_up, out_other = tie(near_qkv, token_h, near_up, out_other)
    with jax.named_scope("weight_qkv"):
        far_qkv = swap(near_qkv, ("c",))
    with jax.named_scope("tokens"):
        token_parts = [rows, token_l, token_h, swap(token_h, ("l",))]
    with jax.named_scope("weight_up"):
        up_other = swap(near_up, ("h",))
    rows_of = lambda v: v.reshape(16, tall, 3 * part)[:, own, : own * columns]
    blocks = jnp.concatenate([rows_of(near_qkv), rows_of(far_qkv)], axis=0).astype(WIDE)
    index = jnp.arange(32)
    owner = (((index // 4) % 4) ^ at_dp) * 8 + ((index % 4) ^ at_z) * 2 + ((index // 16) ^ ic)
    chosen = (owner[None, :] == index[:, None]).astype(WIDE)
    blocks = jnp.dot(chosen, blocks)
    table = blocks.reshape(32, columns, own).transpose(1, 0, 2).reshape(columns, width)
    bias_heads = lax.dynamic_slice_in_dim(table[0:2], at_z * part, part, axis=1)
    bias_units = table[3 : 3 + ratio].reshape(2, 2, 2, 2, units // 4)
    bias_units = lax.dynamic_slice(bias_units, (0, ix, 0, il, 0), (2, 1, 2, 1, units // 4))
    bias_units = bias_units.reshape(1, units)

    far_qkv, token_parts[3], table, bias_heads, bias_units = tie(
        far_qkv, token_parts[3], table, bias_heads, bias_units
    )
    with jax.named_scope("weight_out"):
        near_out = jnp.concatenate([low_out, after(out_other, token_parts[3])], axis=0)
        out_other = swap(near_out, ("h",))
    far_qkv, up_other = tie(far_qkv, after(up_other, far_qkv))

    vmem, hbm = pl.BlockSpec(memory_space=pltpu.VMEM), pl.BlockSpec(memory_space=pltpu.HBM)
    q, kv, full_qkv = pl.pallas_call(
        project_kernel,
        name="project_kernel",
        in_specs=[pl.BlockSpec(memory_space=pltpu.SMEM), vmem] + [hbm] * 6,
        out_specs=[vmem] * 3,
        out_shape=[
            jax.ShapeDtypeStruct((4 * count, part), LOW),
            jax.ShapeDtypeStruct((4 * count, 2 * part), LOW),
            jax.ShapeDtypeStruct((width, 3 * part), LOW),
        ],
        scratch_shapes=[
            pltpu.VMEM(near_qkv.shape, LOW),
            pltpu.VMEM(far_qkv.shape, LOW),
            pltpu.VMEM((4 * count, width), LOW),
            pltpu.SemaphoreType.DMA((6,)),
        ],
        compiler_params=pltpu.CompilerParams(vmem_limit_bytes=48 * 2**20),
        cost_estimate=pl.CostEstimate(flops=1, bytes_accessed=1, transcendentals=0),
    )(bits, bias_heads, near_qkv, far_qkv, *token_parts)
    kv, out_other = tie(kv, out_other)
    with jax.named_scope("keys_values"):
        kv_far = swap(kv, ("c",))
    with jax.named_scope("weight_out"):
        near_out = jnp.concatenate([near_out, out_other], axis=0)
        out_parts = exchange([near_out] * 4, "y", "x")
    late_q, late_down, late_up = tie(q, after(low_down, kv_far), near_up)
    with jax.named_scope("weight_up"):
        near_up = jnp.concatenate([late_up, up_other], axis=0)
        up_other = swap(near_up, ("y",))
    with jax.named_scope("weight_down"):
        down_other = swap(late_down, ("h",))
    *attended, lse = call(
        forward_kernel,
        [((count, part), LOW)] * 4 + [((4, 4 * count), WIDE)],
        bits,
        late_q,
        kv,
        kv_far,
    )
    out_parts = [near_out] + [after(piece, lse) for piece in out_parts[1:]]
    near_out = jnp.concatenate(out_parts, axis=0)
    *attended, down_other, near_out = tie(*attended, after(down_other, lse), near_out)
    with jax.named_scope("attended"):
        attended = exchange(attended, "h", "l")
    with jax.named_scope("weight_out"):
        far_out = swap(near_out, ("c",))
        (full_out,) = call(lay_qkv_kernel, [((width, width), LOW)], bits, near_out, far_out)
    attended[1:], up_other, down_other = lax.optimization_barrier(
        (attended[1:], up_other, down_other)
    )
    with jax.named_scope("weight_up"):
        near_up = jnp.concatenate([near_up, up_other], axis=0)
        far_up = swap(near_up, ("c",))
    with jax.named_scope("weight_down"):
        near_down = jnp.concatenate([low_down, down_other], axis=0)
        down_other = swap(near_down, ("y",))
    hidden, hidden_low, normed, scale = call(
        out_kernel,
        [((count, width), WIDE), ((count, width), LOW), ((count, width), WIDE), ((count, 128), WIDE)],
        bits,
        *attended,
        full_out,
        rows,
        table,
    )

    half = count // 2
    with jax.named_scope("hidden"):
        from_l, from_x = swap(hidden_low, ("l",)), swap(hidden_low, ("x",))
    from_l, from_x, far_up, down_other = tie(
        from_l, from_x, after(far_up, from_l, from_x), after(down_other, from_l, from_x)
    )
    with jax.named_scope("hidden"):
        hidden_parts = [hidden_low, from_l, from_x]
        hidden_parts += [swap(from_x[:half], ("l",)), swap(from_l[half:], ("x",))]
    with jax.named_scope("weight_down"):
        near_down = jnp.concatenate([near_down, down_other], axis=0)
        far_down = swap(near_down, ("c",))
    (full_up,) = call(lay_up_kernel, [((width, units), LOW)], bits, near_up, far_up)
    (full_down,) = call(lay_down_kernel, [((units, width), LOW)], bits, near_down, far_down)
    parts_shape = [((count, width), WIDE)] * 3 + [((count // 2, width), LOW)] * 2
    hidden_parts[3], full_down = tie(hidden_parts[3], full_down)
    act, slope = call(
        feed_up_kernel,
        [((4 * count, units), LOW)] * 2,
        bits,
        *hidden_parts,
        full_up,
        bias_units,
        flops=10**9,
    )
    parts = call(feed_down_kernel, parts_shape, bits, act, full_down)
    terms = scatter_square(parts, "x", "l")
    output, grad_two, grad_down, sums_two = call(
        norm_two_kernel,
        [((count, width), LOW), ((count, width), WIDE), ((count, width), LOW), ((8, width), WIDE)],
        bits,
        *terms,
        hidden,
        cotangent[0],
        table,
    )

    with jax.named_scope("grad_down"):
        grad_parts = gather_square(grad_down, "x", "l")
    grad_up, sums_up, *parts = call(
        feed_back_kernel,
        [((4 * count, units), LOW), ((8, units), WIDE)] + parts_shape,
        bits,
        *grad_parts,
        full_down,
        full_up,
        slope,
        flops=2 * 10**9,
    )
    with jax.named_scope("grad_hidden"):
        terms = scatter_square(parts, "x", "l")

    feed_near, feed_far = call(
        feed_grad_kernel,
        [((16 * own + 4 * down_rows, width), LOW)] * 2,
        bits,
        act,
        *grad_parts,
        *hidden_parts,
        grad_up,
        scratch=[pltpu.VMEM((units, width), LOW), pltpu.VMEM((width, units), LOW)],
    )

    def halve(value, axis, start=(), use=()):
        size = value.shape[0] // 2
        other = send(value[size:].astype(LOW), (axis,), start, use)
        return value[:size].astype(WIDE) + other.astype(WIDE)

    with jax.named_scope("grad_weight_feed"):
        feed_other = swap(feed_far, ("c",))
        feed_sum = (feed_near.astype(WIDE) + feed_other.astype(WIDE)).astype(LOW)
    *terms, feed_sum = lax.optimization_barrier((*terms, feed_sum))
    grad_middle, grad_branch, sums_one, *douts = call(
        norm_one_kernel,
        [((count, width), WIDE), ((count, width), LOW), ((8, width), WIDE)]
        + [((count, part), LOW)] * 4,
        bits,
        *terms,
        grad_two,
        normed,
        scale,
        full_out,
        table,
    )
    with jax.named_scope("grad_attended"):
        douts = exchange(douts, "h", "l")
    back = tuple(douts[1:])
    out_near, out_far = call(
        out_grad_kernel,
        [((16 * own, width), LOW)] * 2,
        bits,
        *attended,
        grad_branch,
        scratch=[pltpu.VMEM((width, width), LOW)],
    )
    with jax.named_scope("grad_weight_feed"):
        feed_other = swap(feed_sum[feed_sum.shape[0] // 2 :], ("y",))
    with jax.named_scope("grad_weight_out"):
        out_other = send(out_far, ("c",), use=back)
        out_sum = (out_near.astype(WIDE) + out_other.astype(WIDE)).astype(LOW)
    late_lse, out_sum = tie(lse, out_sum)
    dq, dkv_near, dkv_far, sums_heads = call(
        backward_kernel,
        [
            ((4 * count, part), LOW),
            ((4 * count, 2 * part), WIDE),
            ((4 * count, 2 * part), LOW),
            ((8, part), WIDE),
        ],
        bits,
        q,
        kv,
        kv_far,
        late_lse,
        *douts,
    )
    with jax.named_scope("grad_weight_out"):
        out_sum = halve(out_sum, "x", use=(dq,)).astype(LOW)
    def add_first(value, other):
        return value[: other.shape[0]].astype(WIDE) + other.astype(WIDE)

    feed_sum = add_first(feed_sum, after(feed_other, dq)).astype(LOW)
    dkv_far, out_sum, feed_sum = tie(dkv_far, out_sum, feed_sum)
    up_size = 4 * own
    rows_of_part = lambda start, size: jnp.concatenate(
        [feed_sum[start : start + size], feed_sum[start + up_size + down_rows :][:size]], axis=0
    )
    up_sum, down_sum = rows_of_part(0, up_size), rows_of_part(up_size, down_rows)
    with jax.named_scope("grad_keys_values"):
        dkv_other = swap(dkv_far, ("c",))
    with jax.named_scope("grad_weight_up"):
        up_other = swap(up_sum[up_size:], ("h",))
    with jax.named_scope("grad_weight_out"):
        out_other = swap(out_sum[out_sum.shape[0] // 2 :], ("y",))
    near, far, grad_projected = call(
        qkv_grad_kernel,
        [((16 * tall, 3 * part), LOW)] * 2 + [((4 * count, 3 * part), LOW)],
        bits,
        *token_parts,
        dq,
        dkv_near,
        dkv_other,
        sums_heads,
        sums_one,
        sums_two,
        sums_up,
        scratch=[pltpu.VMEM((width, 3 * part), LOW), pltpu.VMEM((8, 8, 3 * part), WIDE)],
    )
    out_sum = add_first(out_sum, after(out_other, near)).astype(LOW)
    owned_up = add_first(up_sum, after(up_other, near)).astype(LOW)
    far, out_sum, owned_up, down_sum = tie(far, out_sum, owned_up, down_sum)
    with jax.named_scope("grad_weight_qkv"):
        far_other = swap(far, ("c",))
        qkv_sum = (near.astype(WIDE) + far_other.astype(WIDE)).astype(LOW)
    with jax.named_scope("grad_weight_out"):
        out_other = swap(out_sum[2 * own :], ("l",))
    with jax.named_scope("grad_weight_up"):
        up_other = swap(owned_up[2 * own :], ("x",))
    with jax.named_scope("grad_weight_down"):
        down_other = swap(down_sum[down_rows:], ("h",))
    qkv_sum, up_other = tie(qkv_sum, after(up_other, far_other))
    with jax.named_scope("grad_weight_up"):
        up_last = swap(jnp.concatenate([owned_up[own : 2 * own], up_other[own:]], axis=0), ("l",))
    parts = call(
        rows_grad_kernel,
        [((count, width), WIDE)] + [((count, width), LOW)] * 3,
        bits,
        after(grad_projected, far_other),
        full_qkv,
        grad_middle,
    )
    with jax.named_scope("grad_weight_qkv"):
        blocks = [qkv_sum[i * 4 * tall : (i + 1) * 4 * tall] for i in range(4)]
        blocks = exchange(blocks, "y", "x")
        owned_qkv = sum(block.astype(WIDE) for block in blocks).astype(LOW)
    late = tuple(blocks[1:])
    out_sum = add_first(out_sum, after(out_other, *late)).astype(LOW)
    owned_down = add_first(down_sum, after(down_other, *late))
    owned_qkv, owned_down, up_last, out_sum, *parts = tie(
        owned_qkv, owned_down, after(up_last, *late), out_sum, *parts
    )
    up_pieces = [owned_up[:own], up_last[:own], up_other[:own], up_last[own:]]
    with jax.named_scope("grad_weight_qkv"):
        qkv_pieces = exchange([owned_qkv[i * tall : (i + 1) * tall] for i in range(4)], "h", "l")
    with jax.named_scope("grad_weight_out"):
        owned_out = add_first(out_sum, send(out_sum[own:], ("h",), use=(qkv_pieces[1],)))

    total, small_tile = call(
        squares_kernel,
        [((8, 128), WIDE), ((8, 3 * part), WIDE)],
        bits,
        owned_down,
        owned_out,
        *up_pieces,
        *qkv_pieces,
    )
    tile = width // 8
    lanes = 3 * part // tile
    small_tile = small_tile[:2].reshape(2 * lanes, tile)[:columns]
    owned_small = lax.dynamic_slice_in_dim(small_tile, (2 * il + ic) * own, own, axis=1).T
    def sum_square(value, a, b):
        terms = exchange([value] * 4, a, b)
        return (terms[0] + terms[1]) + (terms[2] + terms[3])

    with jax.named_scope("norm"):
        total = total + swap(total, ("c",))
        total = sum_square(total, "h", "l")
    with jax.named_scope("grad_tokens"):
        far_l = send(parts[3], ("l",), start=(total,))
        from_l = send(parts[1], ("l",), start=(total,))
        to_h = (parts[2].astype(WIDE) + far_l.astype(WIDE)).astype(LOW)
    with jax.named_scope("norm"):
        total = sum_square(total, "y", "x")
    total, to_h = tie(total, to_h)
    with jax.named_scope("grad_tokens"):
        from_h = swap(to_h, ("h",))
    grad_rows = parts[0] + from_l.astype(WIDE) + from_h.astype(WIDE)
    grad_norm = jnp.sqrt(total[0, 0])
    factor = jnp.minimum(1.0, CLIP_LIMIT / (grad_norm + 1e-06))
    held = jnp.full((1,), factor)

    states = [
        (weight_down, moment_down, second_down),
        (weight_out, moment_out, second_out),
        (weight_up, moment_up, second_up),
        (weight_qkv, moment_qkv, second_qkv),
    ]
    plans = [
        (RATE_MATRIX, whole_places, 1),
        (RATE_OUTPUT, whole_places, 1),
        (RATE_MATRIX, up_places, 4),
        (RATE_MATRIX, qkv_places, 4),
    ]
    grads = [owned_down, owned_out, *up_pieces, *qkv_pieces]
    flat = [array for group in states for array in group]
    results = pl.pallas_call(
        functools.partial(update_kernel, plans),
        name="update_kernel",
        in_specs=[pl.BlockSpec(memory_space=pltpu.SMEM)] * 2
        + [pl.BlockSpec(memory_space=pltpu.HBM)] * (len(grads) + 12),
        out_specs=[pl.BlockSpec(memory_space=pltpu.HBM)] * 12,
        out_shape=[jax.ShapeDtypeStruct(array.shape, WIDE) for array in flat],
        scratch_shapes=[pltpu.VMEM(grad.shape, grad.dtype) for grad in grads]
        + [pltpu.VMEM(array.shape, WIDE) for array in flat * 2]
        + [pltpu.SemaphoreType.DMA((len(grads),))]
        + [pltpu.SemaphoreType.DMA((12,))] * 2,
        compiler_params=pltpu.CompilerParams(vmem_limit_bytes=60 * 2**20),
        cost_estimate=pl.CostEstimate(flops=1, bytes_accessed=1, transcendentals=0),
    )(bits, held, *grads, *flat)
    new_down, new_moment_down, new_second_down = results[0:3]
    new_out, new_moment_out, new_second_out = results[3:6]
    new_up, new_moment_up, new_second_up = results[6:9]
    new_qkv, new_moment_qkv, new_second_qkv = results[9:12]
    new_small, new_moment_small, new_second_small = adam_update(
        small_params, owned_small * factor, moment_small, second_small, RATE_SMALL, 0.0
    )
    return (
        output[None],
        grad_rows[None],
        grad_norm,
        new_qkv,
        new_out,
        new_up,
        new_down,
        new_small,
        new_moment_qkv,
        new_moment_out,
        new_moment_up,
        new_moment_down,
        new_moment_small,
        new_second_qkv,
        new_second_out,
        new_second_up,
        new_second_down,
        new_second_small,
    )


def solution(mesh):
    sizes = (mesh.shape["dp"], mesh.shape["seq"])
    if sizes == (4, 8):
        squares = Mesh(mesh.devices.reshape(2, 2, 2, 2, 2), AXES)
        dp, seq = ("y", "x"), ("h", "l", "c")
        body, mesh = on_square, squares
        every = P(AXES, None)
        over = P(dp, seq, None)
    else:
        body = on_device
        every = P(("dp", "seq"), None)
        over = P("dp", "seq", None)
    return jax.shard_map(
        body,
        mesh=mesh,
        in_specs=(over,) * 2 + (every,) * 15,
        out_specs=(over,) * 2 + (P(),) + (every,) * 15,
        check_vma=False,
    )
```

```python
import functools
import math

import jax
import jax.numpy as jnp
from jax import lax
from jax.experimental import pallas as pl
from jax.experimental.pallas import tpu as pltpu
from jax.sharding import Mesh
from jax.sharding import PartitionSpec as P

HEAD = 64
STEP = 5


NORM_EPSILON = 1e-05
ADAM_EPSILON = 1e-08
BETA_FIRST = 0.5
BETA_SECOND = 0.55
CLIP_LIMIT = 1.0
RATE_MATRIX = 0.04
RATE_OUTPUT = 0.5
RATE_SMALL = 0.3
WEIGHT_DECAY = 0.01
SCORE_SCALE = 0.125


def layer_norm(value, gain, shift):
    center = jnp.mean(value, axis=-1, keepdims=True)
    centered = value - center
    variance = jnp.mean(centered * centered, axis=-1, keepdims=True)
    return centered * lax.rsqrt(variance + NORM_EPSILON) * gain + shift


def exact_gelu(value):
    return jax.nn.gelu(value, approximate=False)


def unpack(table_low):
    table = table_low.astype(jnp.float32)
    ratio = table.shape[1] - 8
    bias_up = table[:, 3 : 3 + ratio].T.reshape(-1)
    return (
        table[:, 0],
        table[:, 1],
        table[:, 2],
        bias_up,
        table[:, 3 + ratio],
        table[:, 4 + ratio],
        table[:, 5 + ratio],
        table[:, 6 + ratio],
        table[:, 7 + ratio],
    )


def cross(left, right):
    return lax.dot_general(
        left, right, (((0,), (0,)), ((), ())), preferred_element_type=jnp.float32
    )


def against(left, right):
    return lax.dot_general(
        left, right, (((1,), (1,)), ((), ())), preferred_element_type=jnp.float32
    )


def take_block(source, index, block, heads):
    piece = lax.dynamic_slice_in_dim(source, index * block, block, 0)
    return piece.reshape(block, heads, HEAD)


def scores_of(query_heads, key_heads):
    return (
        jnp.einsum("qhd,khd->hqk", query_heads, key_heads, preferred_element_type=jnp.float32)
        * SCORE_SCALE
    )


def block_grads(query_heads, key_heads, value_heads, dout_heads, log_total, delta):
    scores = scores_of(query_heads, key_heads)
    probs = jnp.exp(scores - log_total[..., None])
    grad_probs = jnp.einsum(
        "qhd,khd->hqk", dout_heads, value_heads, preferred_element_type=jnp.float32
    )
    grad_scores = (probs * (grad_probs - delta[..., None])).astype(jnp.bfloat16)
    return (probs, grad_scores)


def attention_forward(query_heads, keys_all, values_all, block):
    count_rows, heads = (query_heads.shape[0], query_heads.shape[1])
    count = keys_all.shape[0] // block

    def stats_step(index, carry):
        run_top, run_total = carry
        scores = scores_of(query_heads, take_block(keys_all, index, block, heads))
        new_top = jnp.maximum(run_top, jnp.max(scores, axis=-1))
        run_total = run_total * jnp.exp(run_top - new_top) + jnp.sum(
            jnp.exp(scores - new_top[..., None]), axis=-1
        )
        return (new_top, run_total)

    start_top = jnp.full((heads, count_rows), -1e30, jnp.float32)
    start_total = jnp.zeros((heads, count_rows), jnp.float32)
    run_top, run_total = lax.fori_loop(0, count, stats_step, (start_top, start_total))
    log_total = run_top + jnp.log(run_total)

    def value_step(index, accum):
        scores = scores_of(query_heads, take_block(keys_all, index, block, heads))
        weights = jnp.exp(scores - log_total[..., None]).astype(jnp.bfloat16)
        return accum + jnp.einsum(
            "hqk,khd->qhd",
            weights,
            take_block(values_all, index, block, heads),
            preferred_element_type=jnp.float32,
        )

    accum = lax.fori_loop(0, count, value_step, jnp.zeros((count_rows, heads, HEAD), jnp.float32))
    return (accum.reshape(count_rows, heads * HEAD), log_total)


def adam_update(weight, grad, moment, second, rate, decay):
    moment_new = BETA_FIRST * moment + (1.0 - BETA_FIRST) * grad
    second_new = BETA_SECOND * second + (1.0 - BETA_SECOND) * grad * grad
    direction = (
        moment_new
        / (1.0 - BETA_FIRST**STEP)
        / (jnp.sqrt(second_new / (1.0 - BETA_SECOND**STEP)) + ADAM_EPSILON)
    )
    return (weight - rate * (direction + decay * weight), moment_new, second_new)


def on_device(
    tokens,
    cotangent,
    weight_qkv,
    weight_out,
    weight_up,
    weight_down,
    small_params,
    moment_qkv,
    moment_out,
    moment_up,
    moment_down,
    moment_small,
    second_qkv,
    second_out,
    second_up,
    second_down,
    second_small,
):
    rows = tokens[0]
    count_rows = rows.shape[0]
    width = rows.shape[1]
    heads = width // HEAD
    block = 4 * count_rows
    full_qkv, full_out, full_up, full_down, full_small = (
        lax.all_gather(weight_qkv.astype(jnp.bfloat16), ("dp", "seq"), axis=0, tiled=True),
        lax.all_gather(weight_out.astype(jnp.bfloat16), ("dp", "seq"), axis=0, tiled=True),
        lax.all_gather(weight_up.astype(jnp.bfloat16), ("dp", "seq"), axis=0, tiled=True),
        lax.all_gather(weight_down.astype(jnp.bfloat16), ("dp", "seq"), axis=0, tiled=True),
        lax.all_gather(small_params.astype(jnp.bfloat16), ("dp", "seq"), axis=0, tiled=True),
    )
    (
        bias_query,
        bias_value,
        bias_out,
        bias_up,
        bias_down,
        gain_one,
        shift_one,
        gain_two,
        shift_two,
    ) = unpack(full_small)
    projected = jnp.dot(rows, full_qkv, preferred_element_type=jnp.float32)
    query = (projected[:, :width] + bias_query).astype(jnp.bfloat16)
    key_rows = projected[:, width : 2 * width].astype(jnp.bfloat16)
    value_rows = (projected[:, 2 * width :] + bias_value).astype(jnp.bfloat16)
    keys_all, values_all = (
        lax.all_gather(key_rows, "seq", axis=0, tiled=True),
        lax.all_gather(value_rows, "seq", axis=0, tiled=True),
    )
    query_heads = query.reshape(count_rows, heads, HEAD)
    attended, log_total = attention_forward(query_heads, keys_all, values_all, block)
    attended_low = attended.astype(jnp.bfloat16)
    branch = jnp.dot(attended_low, full_out, preferred_element_type=jnp.float32) + bias_out
    middle = rows.astype(jnp.float32) + branch
    hidden, norm_one_back = jax.vjp(layer_norm, middle, gain_one, shift_one)
    hidden_low = hidden.astype(jnp.bfloat16)
    upward = jnp.dot(hidden_low, full_up, preferred_element_type=jnp.float32) + bias_up
    activation, gelu_back = jax.vjp(exact_gelu, upward)
    activation_low = activation.astype(jnp.bfloat16)
    downward = jnp.dot(activation_low, full_down, preferred_element_type=jnp.float32) + bias_down
    output, norm_two_back = jax.vjp(layer_norm, hidden + downward, gain_two, shift_two)
    back_qkv, back_out, back_up, back_down = (full_qkv, full_out, full_up, full_down)
    grad_sum_two, grad_gain_two, grad_shift_two = norm_two_back(cotangent[0].astype(jnp.float32))
    grad_down_low = grad_sum_two.astype(jnp.bfloat16)
    grad_bias_down = jnp.sum(grad_down_low.astype(jnp.float32), axis=0)
    grad_weight_down = cross(activation_low, grad_down_low)
    grad_activation = against(grad_down_low, back_down)
    grad_up_low = gelu_back(grad_activation)[0].astype(jnp.bfloat16)
    grad_bias_up = jnp.sum(grad_up_low.astype(jnp.float32), axis=0)
    grad_weight_up = cross(hidden_low, grad_up_low)
    grad_hidden = grad_sum_two + against(grad_up_low, back_up)
    grad_middle, grad_gain_one, grad_shift_one = norm_one_back(grad_hidden)
    grad_branch_low = grad_middle.astype(jnp.bfloat16)
    grad_bias_out = jnp.sum(grad_branch_low.astype(jnp.float32), axis=0)
    grad_weight_out = cross(attended_low, grad_branch_low)
    grad_attended = against(grad_branch_low, back_out).astype(jnp.bfloat16)
    delta = jnp.sum(
        (grad_attended.astype(jnp.float32) * attended).reshape(count_rows, heads, HEAD), axis=-1
    ).T
    dout_heads = grad_attended.reshape(count_rows, heads, HEAD)
    count = keys_all.shape[0] // block

    def both_step(index, carry):
        grad_query, grad_keys, grad_values = carry
        key_heads = take_block(keys_all, index, block, heads)
        value_heads = take_block(values_all, index, block, heads)
        probs, grad_scores = block_grads(
            query_heads, key_heads, value_heads, dout_heads, log_total, delta
        )
        grad_query = (
            grad_query
            + jnp.einsum("hqk,khd->qhd", grad_scores, key_heads, preferred_element_type=jnp.float32)
            * SCORE_SCALE
        )
        part_keys = (
            jnp.einsum("hqk,qhd->khd", grad_scores, query_heads, preferred_element_type=jnp.float32)
            * SCORE_SCALE
        )
        part_values = jnp.einsum(
            "hqk,qhd->khd",
            probs.astype(jnp.bfloat16),
            dout_heads,
            preferred_element_type=jnp.float32,
        )
        grad_keys = lax.dynamic_update_slice_in_dim(
            grad_keys, part_keys.reshape(block, width), index * block, 0
        )
        grad_values = lax.dynamic_update_slice_in_dim(
            grad_values, part_values.reshape(block, width), index * block, 0
        )
        return (grad_query, grad_keys, grad_values)

    start = (
        jnp.zeros((count_rows, heads, HEAD), jnp.float32),
        jnp.zeros((keys_all.shape[0], width), jnp.float32),
        jnp.zeros((keys_all.shape[0], width), jnp.float32),
    )
    grad_query, grad_keys, grad_values = lax.fori_loop(0, count, both_step, start)
    summed_keys, summed_values = (
        lax.psum_scatter(
            grad_keys.astype(jnp.bfloat16), "seq", scatter_dimension=0, tiled=True
        ).astype(jnp.float32),
        lax.psum_scatter(
            grad_values.astype(jnp.bfloat16), "seq", scatter_dimension=0, tiled=True
        ).astype(jnp.float32),
    )
    grad_query_low = grad_query.reshape(count_rows, width).astype(jnp.bfloat16)
    grad_value_low = summed_values.astype(jnp.bfloat16)
    grad_projected = jnp.concatenate(
        [grad_query_low, summed_keys.astype(jnp.bfloat16), grad_value_low], axis=1
    )
    grad_weight_qkv = cross(rows, grad_projected)
    grad_bias_query = jnp.sum(grad_query_low.astype(jnp.float32), axis=0)
    grad_bias_value = jnp.sum(grad_value_low.astype(jnp.float32), axis=0)
    grad_rows = grad_middle + against(grad_projected, back_qkv)
    ratio = full_up.shape[1] // width
    grad_small = jnp.concatenate(
        [
            jnp.stack([grad_bias_query, grad_bias_value, grad_bias_out], axis=1),
            grad_bias_up.reshape(ratio, width).T,
            jnp.stack(
                [grad_bias_down, grad_gain_one, grad_shift_one, grad_gain_two, grad_shift_two],
                axis=1,
            ),
        ],
        axis=1,
    )
    owned_qkv, owned_out, owned_up, owned_down, owned_small = (
        lax.psum_scatter(grad_weight_qkv, ("dp", "seq"), scatter_dimension=0, tiled=True),
        lax.psum_scatter(grad_weight_out, ("dp", "seq"), scatter_dimension=0, tiled=True),
        lax.psum_scatter(grad_weight_up, ("dp", "seq"), scatter_dimension=0, tiled=True),
        lax.psum_scatter(grad_weight_down, ("dp", "seq"), scatter_dimension=0, tiled=True),
        lax.psum_scatter(grad_small, ("dp", "seq"), scatter_dimension=0, tiled=True),
    )
    squares = jnp.sum(owned_qkv * owned_qkv) + jnp.sum(owned_out * owned_out)
    squares = squares + jnp.sum(owned_up * owned_up) + jnp.sum(owned_down * owned_down)
    squares = squares + jnp.sum(owned_small * owned_small)
    total = lax.psum(squares, ("dp", "seq"))
    grad_norm = jnp.sqrt(total)
    factor = jnp.minimum(1.0, CLIP_LIMIT / (grad_norm + 1e-06))
    new_qkv, new_moment_qkv, new_second_qkv = adam_update(
        weight_qkv, owned_qkv * factor, moment_qkv, second_qkv, RATE_MATRIX, WEIGHT_DECAY
    )
    new_out, new_moment_out, new_second_out = adam_update(
        weight_out, owned_out * factor, moment_out, second_out, RATE_OUTPUT, WEIGHT_DECAY
    )
    new_up, new_moment_up, new_second_up = adam_update(
        weight_up, owned_up * factor, moment_up, second_up, RATE_MATRIX, WEIGHT_DECAY
    )
    new_down, new_moment_down, new_second_down = adam_update(
        weight_down, owned_down * factor, moment_down, second_down, RATE_MATRIX, WEIGHT_DECAY
    )
    new_small, new_moment_small, new_second_small = adam_update(
        small_params, owned_small * factor, moment_small, second_small, RATE_SMALL, 0.0
    )
    return (
        output.astype(jnp.bfloat16)[None],
        grad_rows[None],
        grad_norm,
        new_qkv,
        new_out,
        new_up,
        new_down,
        new_small,
        new_moment_qkv,
        new_moment_out,
        new_moment_up,
        new_moment_down,
        new_moment_small,
        new_second_qkv,
        new_second_out,
        new_second_up,
        new_second_down,
        new_second_small,
    )


AXES = ("y", "x", "h", "l", "c")
LOW = jnp.bfloat16
WIDE = jnp.float32


def swap(value, axes):
    axes = tuple(name for name in AXES if name in axes)
    last = 2 ** len(axes) - 1
    return lax.ppermute(value, axes, [(i, i ^ last) for i in range(last + 1)])


def after(value, *events):
    return lax.optimization_barrier((value, *events))[0]


def tie(*values):
    return lax.optimization_barrier(values)


def send(value, axes, start=(), use=()):
    got = swap(after(value, *start) if start else value, axes)
    return after(got, *use) if use else got


def exchange(parts, a, b, start=(), use=()):
    ways = ((b,), (a,), (a, b))
    return [parts[0]] + [send(part, way, start, use) for part, way in zip(parts[1:], ways)]


def gather_square(value, a, b):
    half = value.shape[0] // 2
    from_a, from_b = swap(value, (a,)), swap(value, (b,))
    return [value, from_b, from_a, swap(from_a[:half], (b,)), swap(from_b[half:], (a,))]


def scatter_square(parts, a, b):
    own, to_b, to_a, far_first, far_second = parts
    half = own.shape[0] // 2
    first = swap(far_first, (a,))
    second = swap(far_second, (b,))
    to_b = jnp.concatenate([to_b[:half] + first.astype(WIDE), to_b[half:]], axis=0).astype(LOW)
    to_a = jnp.concatenate([to_a[:half], to_a[half:] + second.astype(WIDE)], axis=0).astype(LOW)
    return own, swap(to_b, (b,)), swap(to_a, (a,))


def gather_ring(value, a, b, start=(), use=()):
    from_b = send(value, (b,), start, use)
    from_a = swap(after(value, *start) if start else value, (a,))
    far = send(from_a, (b,), use=use)
    return [value, from_b, after(from_a, *use) if use else from_a, far]


def dot(left, right):
    return jnp.dot(left, right, preferred_element_type=WIDE)


def call(kernel, outs, *args, scratch=(), flops=10**9, scalars=0):
    outs = [jax.ShapeDtypeStruct(shape, kind) for shape, kind in outs]
    return pl.pallas_call(
        kernel,
        name=getattr(kernel, "func", kernel).__name__,
        in_specs=[pl.BlockSpec(memory_space=pltpu.SMEM)] * (1 + scalars)
        + [pl.BlockSpec(memory_space=pltpu.VMEM)] * (len(args) - 1 - scalars),
        out_specs=[pl.BlockSpec(memory_space=pltpu.VMEM)] * len(outs),
        out_shape=outs,
        scratch_shapes=list(scratch),
        compiler_params=pltpu.CompilerParams(vmem_limit_bytes=48 * 2**20),
        cost_estimate=pl.CostEstimate(flops=1, bytes_accessed=1, transcendentals=0),
    )(*args)


def at(start, size):
    return pl.ds(pl.multiple_of(start, size), size)


def indices(bits):
    iy, ix, ih, il, ic = (bits[i] for i in range(5))
    return 2 * iy + ix, 2 * ih + il, ic


def pack_qkv_kernel(bits, weight, small, *outs):
    _, z, _ = indices(bits)
    own = weight.shape[0]
    size = outs[0].shape[1] // 3
    for r, out in enumerate(outs):
        for kind in range(3):
            start = kind * 4 * size + (z ^ r) * size
            out[:own, kind * size : (kind + 1) * size] = weight[:, at(start, size)].astype(LOW)
        out[own:, :] = small[...]


def pack_rest_kernel(bits, out_weight, up, down, low_out, low_down, near_up, far_up):
    iy, ix, ih, il, ic = (bits[i] for i in range(5))
    own = up.shape[0]
    size = up.shape[1] // 16
    low_out[...] = out_weight[...].astype(LOW)
    low_down[...] = down[...].astype(LOW)
    for r in range(4):
        out, rows = (near_up, far_up)[r // 2], slice(r % 2 * own, (r % 2 + 1) * own)
        x, l = ix ^ (r // 2), il ^ (r % 2)
        for y in range(2):
            for h in range(2):
                start = (((y * 2 + x) * 2 + h) * 2 + l) * size
                to = (y * 2 + h) * size
                out[rows, to : to + size] = up[:, at(start, size)].astype(LOW)


def lay_rows(bits, full, pieces, own, stride, c):
    d, z, _ = indices(bits)
    for p, piece in enumerate(pieces):
        for s in range(4):
            to = (d ^ p) * 8 * own + (z ^ s) * 2 * own + c * own
            full[at(to, own), :] = piece[s * stride : s * stride + own, :]


def lay_qkv_kernel(bits, near, far, full):
    own = full.shape[0] // 32
    stride = near.shape[0] // 16
    c = bits[4]
    for ref, core in ((near, c), (far, 1 - c)):
        pieces = [ref.at[p * 4 * stride : (p + 1) * 4 * stride] for p in range(4)]
        lay_rows(bits, full, pieces, own, stride, core)


def lay_up_kernel(bits, near, far, full):
    iy, ix, ih, il, ic = (bits[i] for i in range(5))
    own = full.shape[0] // 32
    for ref, core in ((near, ic), (far, 1 - ic)):
        for p in range(4):
            y, h = iy ^ (p // 2), ih ^ (p % 2)
            for q in range(4):
                x, l = ix ^ (q // 2), il ^ (q % 2)
                to = ((((y * 2 + x) * 2 + h) * 2 + l) * 2 + core) * own
                full[at(to, own), :] = ref[(4 * p + q) * own : (4 * p + q + 1) * own, :]


def lay_down_kernel(bits, near, far, full):
    iy, _, ih, _, ic = (bits[i] for i in range(5))
    size = full.shape[0] // 8
    for ref, core in ((near, ic), (far, 1 - ic)):
        for p in range(4):
            to = (((iy ^ (p // 2)) * 2 + (ih ^ (p % 2))) * 2 + core) * size
            full[at(to, size), :] = ref[p * size : (p + 1) * size, :]


def project_kernel(
    bits, bias, near_ref, far_ref, t0, t1, t2, t3, q_ref, kv_ref, full_ref, near, far, rows, sems
):
    d, z, c = indices(bits)
    count = t0.shape[0]
    own = full_ref.shape[0] // 32
    tall = near.shape[0] // 16
    size = q_ref.shape[1]
    pairs = [(near_ref, near), (far_ref, far)]
    pairs += [(ref, rows.at[i * count : (i + 1) * count]) for i, ref in enumerate((t0, t1, t2, t3))]
    copies = [pltpu.make_async_copy(*pair, sems.at[i]) for i, pair in enumerate(pairs)]
    for copy in copies:
        copy.start()
    for copy in copies[:2]:
        copy.wait()
    for ref, core in ((near, c), (far, 1 - c)):
        for p in range(4):
            for s in range(4):
                to = (d ^ p) * 8 * own + (z ^ s) * 2 * own + core * own
                full_ref[at(to, own), :] = ref[(4 * p + s) * tall : (4 * p + s) * tall + own, :]
    for copy in copies[2:]:
        copy.wait()
    projected = dot(rows[...], full_ref[...])
    query = (projected[:, :size] + bias[0:1, :]).astype(LOW)
    q_ref[...] = (query.astype(WIDE) * SCORE_SCALE).astype(LOW)
    kv_ref[:, :size] = projected[:, size : 2 * size].astype(LOW)
    kv_ref[:, size:] = (projected[:, 2 * size :] + bias[1:2, :]).astype(LOW)


def head_mask(shape, axis, head):
    lane = lax.broadcasted_iota(jnp.int32, shape, axis)
    return (lane < HEAD) if head == 0 else (lane >= HEAD)


def forward_kernel(bits, q_ref, near, far, *outs):
    lse_ref = outs[-1]
    count = outs[0].shape[0]
    width = q_ref.shape[1]
    pair = 2 * HEAD
    for group in range(width // pair):
        cols = slice(group * pair, (group + 1) * pair)
        value_cols = slice(width + group * pair, width + (group + 1) * pair)
        keys = jnp.concatenate([near[:, cols], far[:, cols]], axis=0)
        values_t = jnp.concatenate([near[:, value_cols], far[:, value_cols]], axis=0).T
        for piece in range(2):
            rows = slice(2 * piece * count, 2 * (piece + 1) * count)
            queries = q_ref[rows, cols]
            zero = jnp.zeros_like(queries)
            halves = []
            for head in range(2):
                query = jnp.where(head_mask(queries.shape, 1, head), queries, zero)
                scores = against(keys, query)
                top = jnp.max(scores, axis=0, keepdims=True)
                weights = jnp.exp(scores - top)
                total = jnp.sum(weights, axis=0, keepdims=True)
                at_head = 2 * group + head
                lse_ref[at_head : at_head + 1, rows] = top + jnp.log(total)
                halves.append(dot(values_t, weights.astype(LOW)) * (1.0 / total))
            mask = head_mask(halves[0].shape, 0, 0)
            result = jnp.where(mask, halves[0], halves[1]).T.astype(LOW)
            outs[2 * piece][:, cols] = result[:count]
            outs[2 * piece + 1][:, cols] = result[count:]


def backward_kernel(
    bits, q_ref, near, far, lse_ref, d0, d1, d2, d3, dq_ref, near_ref, far_ref, sums
):
    count = d0.shape[0]
    length = 2 * near.shape[0]
    width = q_ref.shape[1]
    pair = 2 * HEAD
    for group in range(width // pair):
        cols = slice(group * pair, (group + 1) * pair)
        value_cols = slice(width + group * pair, width + (group + 1) * pair)
        keys = jnp.concatenate([near[:, cols], far[:, cols]], axis=0)
        values = jnp.concatenate([near[:, value_cols], far[:, value_cols]], axis=0)
        keys_t = keys.T
        sum_keys = jnp.zeros((length, pair), WIDE)
        sum_values = jnp.zeros((length, pair), WIDE)
        bias_query = jnp.zeros((1, pair), WIDE)
        for piece in range(2):
            rows = slice(2 * piece * count, 2 * (piece + 1) * count)
            queries = q_ref[rows, cols]
            refs = (d0, d1) if piece == 0 else (d2, d3)
            douts = jnp.concatenate([refs[0][:, cols], refs[1][:, cols]], axis=0)
            zero = jnp.zeros_like(queries)
            all_probs, all_grads, all_query, all_dout, halves = [], [], [], [], []
            for head in range(2):
                mask = head_mask(queries.shape, 1, head)
                query = jnp.where(mask, queries, zero)
                dout = jnp.where(mask, douts, zero)
                at_head = 2 * group + head
                scores = against(keys, query)
                probs = jnp.exp(scores - lse_ref[at_head : at_head + 1, rows])
                grad_probs = against(values, dout)
                delta = jnp.sum(probs * grad_probs, axis=0, keepdims=True)
                grads = (probs * (grad_probs - delta)).astype(LOW)
                all_probs.append(probs.astype(LOW))
                all_grads.append(grads)
                all_query.append(query)
                all_dout.append(dout)
                halves.append(dot(keys_t, grads))
            mask = head_mask(halves[0].shape, 0, 0)
            dq = jnp.where(mask, halves[0], halves[1]) * SCORE_SCALE
            dq = dq.T.astype(LOW)
            dq_ref[rows, cols] = dq
            bias_query += jnp.sum(dq.astype(WIDE), axis=0, keepdims=True)
            sum_keys += dot(jnp.concatenate(all_grads, axis=1), jnp.concatenate(all_query, axis=0))
            sum_values += dot(jnp.concatenate(all_probs, axis=1), jnp.concatenate(all_dout, axis=0))
        half = length // 2
        near_ref[:, cols] = sum_keys[:half]
        far_ref[:, cols] = sum_keys[half:].astype(LOW)
        sums[0:1, cols] = bias_query
        sums[1:2, cols] = jnp.sum(sum_values, axis=0, keepdims=True)
        near_ref[:, value_cols] = sum_values[:half]
        far_ref[:, value_cols] = sum_values[half:].astype(LOW)


def row_mean(value):
    return jnp.mean(value, axis=-1, keepdims=True)


def column_sums(out, *values):
    out[...] = jnp.zeros_like(out)
    for index, value in enumerate(values):
        out[index : index + 1, :] = jnp.sum(value, axis=0, keepdims=True)


def out_kernel(bits, a0, a1, a2, a3, weight, tokens, table, hidden, low, normed, scale):
    _, z, _ = indices(bits)
    size = a0.shape[1]
    branch = jnp.zeros(hidden.shape, WIDE)
    for r, piece in enumerate((a0, a1, a2, a3)):
        branch += dot(piece[...], weight[at((z ^ r) * size, size), :])
    middle = tokens[...].astype(WIDE) + (branch + table[2:3, :])
    centered = middle - row_mean(middle)
    inverse = lax.rsqrt(row_mean(centered * centered) + NORM_EPSILON)
    unit = centered * inverse
    value = unit * table[-4:-3, :] + table[-3:-2, :]
    hidden[...] = value
    low[...] = value.astype(LOW)
    normed[...] = unit
    scale[...] = jnp.broadcast_to(inverse, scale.shape)


def store_parts(product, own, to_b, to_a, far_first, far_second):
    count = own.shape[0]
    half = count // 2
    own[...] = product[:count]
    to_b[...] = product[count : 2 * count]
    to_a[...] = product[2 * count : 3 * count]
    far_first[...] = product[3 * count : 3 * count + half].astype(LOW)
    far_second[...] = product[3 * count + half :].astype(LOW)


def feed_up_kernel(bits, h0, h1, h2, h3, h4, up, bias, act, slope):
    hidden = jnp.concatenate([ref[...] for ref in (h0, h1, h2, h3, h4)], axis=0)
    upward = dot(hidden, up[...]) + bias[...]
    half = (1.0 + lax.erf(upward * (0.5**0.5))) * 0.5
    act[...] = (upward * half).astype(LOW)
    bell = jnp.exp(upward * upward * -0.5) * (0.5 * 2.0**0.5 * math.pi**-0.5)
    slope[...] = (half + upward * bell).astype(LOW)


def feed_down_kernel(bits, act, down, *parts):
    store_parts(dot(act[...], down[...]), *parts)


def norm_two_kernel(bits, own, from_b, from_a, hidden, cot, table, output, grad, low, sums):
    downward = own[...] + from_b[...].astype(WIDE) + from_a[...].astype(WIDE)
    value = hidden[...] + (downward + table[-5:-4, :])
    centered = value - row_mean(value)
    inverse = lax.rsqrt(row_mean(centered * centered) + NORM_EPSILON)
    unit = centered * inverse
    gain = table[-2:-1, :]
    output[...] = (unit * gain + table[-1:, :]).astype(LOW)
    cotangent = cot[...].astype(WIDE)
    inner = cotangent * gain
    result = inverse * (inner - row_mean(inner) - unit * row_mean(inner * unit))
    grad[...] = result
    rounded = result.astype(LOW)
    low[...] = rounded
    column_sums(sums, rounded.astype(WIDE), cotangent * unit, cotangent)


def feed_back_kernel(bits, g0, g1, g2, g3, g4, down, up, slope, grad_up, sums, *parts):
    grads = jnp.concatenate([ref[...] for ref in (g0, g1, g2, g3, g4)], axis=0)
    upward = (against(grads, down[...]) * slope[...].astype(WIDE)).astype(LOW)
    grad_up[...] = upward
    column_sums(sums, upward.astype(WIDE))
    store_parts(against(upward, up[...]), *parts)


def feed_grad_kernel(
    bits, act, g0, g1, g2, g3, g4, h0, h1, h2, h3, h4, grad_up, near, far, down_full, up_full
):
    iy, ix, ih, il, ic = (bits[i] for i in range(5))
    grads = jnp.concatenate([ref[...] for ref in (g0, g1, g2, g3, g4)], axis=0)
    hidden = jnp.concatenate([ref[...] for ref in (h0, h1, h2, h3, h4)], axis=0)
    down_full[...] = cross(act[...], grads).astype(LOW)
    up_full[...] = cross(hidden, grad_up[...]).astype(LOW)
    own = up_full.shape[0] // 32
    size = down_full.shape[0] // 8
    for p in range(4):
        y, h = iy ^ (p // 2), ih ^ (p % 2)
        base = p * (4 * own + size)
        for q in range(4):
            x, l = ix ^ (q // 2), il ^ (q % 2)
            start = ((((y * 2 + x) * 2 + h) * 2 + l) * 2) * own
            to = base + q * own
            near[to : to + own, :] = up_full[at(start + ic * own, own), :]
            far[to : to + own, :] = up_full[at(start + (1 - ic) * own, own), :]
        start = (y * 2 + h) * 2
        to = base + 4 * own
        near[to : to + size, :] = down_full[at((start + ic) * size, size), :]
        far[to : to + size, :] = down_full[at((start + 1 - ic) * size, size), :]


def norm_one_kernel(
    bits, own, from_b, from_a, above, normed, scale, weight, table, grad, low, sums, *pieces
):
    _, z, _ = indices(bits)
    hidden = own[...] + from_b[...].astype(WIDE) + from_a[...].astype(WIDE)
    hidden = above[...] + hidden
    unit = normed[...]
    inner = hidden * table[-4:-3, :]
    result = scale[:, 0:1] * (inner - row_mean(inner) - unit * row_mean(inner * unit))
    grad[...] = result
    rounded = result.astype(LOW)
    low[...] = rounded
    column_sums(sums, rounded.astype(WIDE), hidden * unit, hidden)
    size = pieces[0].shape[1]
    for r, piece in enumerate(pieces):
        piece[...] = against(rounded, weight[at((z ^ r) * size, size), :]).astype(LOW)


def split_rows(bits, full, near, far, order=(0, 1, 2, 3)):
    d, z, c = indices(bits)
    own = full.shape[0] // 32
    for p in range(4):
        for s in range(4):
            start = (d ^ order[p]) * 8 * own + (z ^ order[s]) * 2 * own
            to = (4 * p + s) * own
            near[to : to + own, :] = full[at(start + c * own, own), :]
            far[to : to + own, :] = full[at(start + (1 - c) * own, own), :]


def out_grad_kernel(bits, a0, a1, a2, a3, grad, near, far, full):
    _, z, _ = indices(bits)
    size = a0.shape[1]
    for r, piece in enumerate((a0, a1, a2, a3)):
        full[at((z ^ r) * size, size), :] = cross(piece[...], grad[...]).astype(LOW)
    split_rows(bits, full, near, far, order=(0, 2, 1, 3))


def qkv_grad_kernel(
    bits, t0, t1, t2, t3, dq, dkv, other, heads, one, two, up, near, far, grads, full, extra
):
    d, z, c = indices(bits)
    tokens = jnp.concatenate([t0[...], t1[...], t2[...], t3[...]], axis=0)
    size = dq.shape[1]
    both = (dkv[...] + other[...].astype(WIDE)).astype(LOW)
    grads[:, :size] = dq[...]
    grads[:, size:] = both
    full[...] = cross(tokens, grads[...]).astype(LOW)
    own = full.shape[0] // 32
    tile = full.shape[0] // 8
    lanes = full.shape[1] // tile
    tall = near.shape[0] // 16
    extra[...] = jnp.zeros_like(extra)
    ratio = up.shape[1] // size
    rows = [(one, 0)] + [None] * ratio + [(two, 0), (one, 1), (one, 2), (two, 1), (two, 2)]
    for k in range(8):
        values = []
        for row in range(2):
            value = heads[row : row + 1, k % 2 * tile : (k % 2 + 1) * tile]
            values.append(jnp.where(z == k // 2, value, 0.0))
        for index, source in enumerate(rows):
            if source is None:
                y, x = (index - 1) // 2, (index - 1) % 2
                lane = ((y * 2 + k // 4) * 2 + k % 2) * tile
                mine = jnp.logical_and(bits[1] == x, bits[3] == k // 2 % 2)
                values.append(jnp.where(mine, up[0:1, lane : lane + tile], 0.0))
            else:
                ref, row = source
                values.append(ref[row : row + 1, k * tile : (k + 1) * tile])
        for column, value in enumerate(values):
            row, lane = column // lanes, column % lanes * tile
            extra[k, row : row + 1, lane : lane + tile] = value
    for p in range(4):
        for s in range(4):
            start = (d ^ p) * 8 * own + (z ^ s) * 2 * own
            to = (4 * p + s) * tall
            near[to : to + own, :] = full[at(start + c * own, own), :]
            far[to : to + own, :] = full[at(start + (1 - c) * own, own), :]
            rows = extra[(d ^ p) * 2 + (z ^ s) // 2].astype(LOW)
            near[to + own : to + tall, :] = rows
            far[to + own : to + tall, :] = rows


def rows_grad_kernel(bits, grads, weight, above, own, *parts):
    product = against(grads[...], weight[...])
    count = own.shape[0]
    own[...] = above[...] + product[:count]
    for r, part in enumerate(parts):
        part[...] = product[(r + 1) * count : (r + 2) * count].astype(LOW)


def squares_kernel(bits, down, out, u0, u1, u2, u3, p0, p1, p2, p3, result, small):
    _, _, c = indices(bits)
    own = out.shape[0]
    values = [ref[...].astype(WIDE) for ref in (down, out, u0, u1, u2, u3)]
    values += [ref[:own, :].astype(WIDE) for ref in (p0, p1, p2, p3)]
    rows = sum(ref[own:, :].astype(WIDE) for ref in (p0, p1, p2, p3))
    small[...] = rows
    lane = lax.broadcasted_iota(jnp.int32, rows.shape, 1) % 128
    mine = (lane // own) == bits[3] * 2 + c
    values.append(jnp.where(mine, rows, 0.0))
    total = jnp.zeros((1, 1), WIDE)
    for value in values:
        total += jnp.sum(jnp.sum(value * value, axis=0, keepdims=True), axis=1, keepdims=True)
    result[...] = jnp.broadcast_to(total, result.shape)


def update_kernel(
    plans, bits, t0, t1, t2, t3, small_grad, small_weight, small_moment, small_second, *refs
):
    count = len(plans)
    total = sum(plan[2] for plan in plans)
    sources, refs = refs[:total], refs[total:]
    norm_ref, *small_results = refs[6 * count : 6 * count + 4]
    refs = refs[: 6 * count] + refs[6 * count + 4 :]
    grads, refs = refs[6 * count : 6 * count + total], refs[: 6 * count] + refs[6 * count + total :]
    brought = refs[-3]
    fetches = [
        pltpu.make_async_copy(sources[i], grads[i], brought.at[i]) for i in range(total)
    ]
    for fetch in fetches:
        fetch.start()
    states, results = refs[: 3 * count], refs[3 * count : 6 * count]
    held, made = refs[6 * count : 9 * count], refs[9 * count : 12 * count]
    arrive, leave = refs[-2:]
    loads = [
        pltpu.make_async_copy(states[i], held[i], arrive.at[i]) for i in range(3 * count)
    ]
    stores = [
        pltpu.make_async_copy(made[i], results[i], leave.at[i]) for i in range(3 * count)
    ]
    for load in loads:
        load.start()
    norm = jnp.sqrt((t0[...] + t1[...]) + (t2[...] + t3[...]))
    norm_ref[...] = norm
    factor = jnp.minimum(1.0, CLIP_LIMIT / (norm[0:1, 0:1] + 1e-06))
    values = adam_update(
        small_weight[...],
        small_grad[...] * factor,
        small_moment[...],
        small_second[...],
        RATE_SMALL,
        0.0,
    )
    for ref, value in zip(small_results, values):
        ref[...] = value
    _, z, _ = indices(bits)
    first = 0
    for index, (rate, places, pieces) in enumerate(plans):
        mine = slice(3 * index, 3 * index + 3)
        for load in loads[mine] + fetches[first : first + pieces]:
            load.wait()
        own = held[3 * index].shape[0]
        for r in range(pieces):
            piece = grads[first + r]
            for source, target in places(bits, z, r, piece.shape[1]):
                grad = piece[:own, source].astype(WIDE) * factor
                weight, moment, second = (ref[:, target] for ref in held[mine])
                values = adam_update(weight, grad, moment, second, rate, WEIGHT_DECAY)
                for ref, value in zip(made[mine], values):
                    ref[:, target] = value
        for store in stores[mine]:
            store.start()
        first += pieces
    for store in stores:
        store.wait()


def whole_places(bits, z, r, columns):
    return [(slice(None), slice(None))]


def qkv_places(bits, z, r, columns):
    size = columns // 3
    return [
        (slice(kind * size, (kind + 1) * size), at(kind * 4 * size + (z ^ r) * size, size))
        for kind in range(3)
    ]


def up_places(bits, z, r, columns):
    size = columns // 4
    x, l = bits[1] ^ (r // 2), bits[3] ^ (r % 2)
    return [
        (
            slice((2 * y + h) * size, (2 * y + h + 1) * size),
            at((((y * 2 + x) * 2 + h) * 2 + l) * size, size),
        )
        for y in range(2)
        for h in range(2)
    ]


def on_square(
    tokens,
    cotangent,
    weight_qkv,
    weight_out,
    weight_up,
    weight_down,
    small_params,
    moment_qkv,
    moment_out,
    moment_up,
    moment_down,
    moment_small,
    second_qkv,
    second_out,
    second_up,
    second_down,
    second_small,
):
    rows = tokens[0]
    count, width = rows.shape
    own = weight_qkv.shape[0]
    down_rows = weight_down.shape[0]
    ratio = weight_up.shape[1] // width
    columns = small_params.shape[1]
    part = width // 4
    units = weight_up.shape[1] // 4
    pad = 8
    tall = own + pad
    iy, ix, ih, il, ic = (lax.axis_index(name) for name in AXES)
    bits = jnp.stack([iy, ix, ih, il, ic]).astype(jnp.int32)
    at_dp, at_z = 2 * iy + ix, 2 * ih + il
    place = 8 * at_dp + 2 * at_z + ic

    low_small = small_params.astype(LOW).T.reshape(1, own * columns)
    low_small = jnp.pad(low_small, ((0, pad - 1), (0, 3 * part - own * columns)))
    with jax.named_scope("weight_qkv"):
        pieces = call(pack_qkv_kernel, [((tall, 3 * part), LOW)] * 4, bits, weight_qkv, low_small)
    with jax.named_scope("tokens"):
        token_l, token_h = swap(rows, ("l",)), swap(rows, ("h",))
    low_out, low_down, up_near, up_far = call(
        pack_rest_kernel,
        [((own, width), LOW), ((down_rows, width), LOW)] + [((2 * own, units), LOW)] * 2,
        bits,
        weight_out,
        weight_up,
        weight_down,
    )
    with jax.named_scope("weight_qkv"):
        near_qkv = jnp.concatenate(exchange(pieces, "h", "l"), axis=0)
        near_qkv = after(near_qkv, token_l, low_out)
    with jax.named_scope("weight_up"):
        up_far = send(up_far, ("x",), start=(near_qkv,))
        up_last = swap(jnp.concatenate([up_near[own:], up_far[own:]], axis=0), ("l",))
        near_up = [up_near[:own], up_last[:own], up_far[:own], up_last[own:]]
        near_up = jnp.concatenate(near_up, axis=0)
    with jax.named_scope("weight_out"):
        out_other = send(low_out, ("l",), start=(near_qkv,))
    with jax.named_scope("weight_qkv"):
        near_qkv = jnp.concatenate(exchange([near_qkv] * 4, "y", "x"), axis=0)
    near_qkv, token_h, near_up, out_other = tie(near_qkv, token_h, near_up, out_other)
    with jax.named_scope("weight_qkv"):
        far_qkv = swap(near_qkv, ("c",))
    with jax.named_scope("tokens"):
        token_parts = [rows, token_l, token_h, swap(token_h, ("l",))]
    with jax.named_scope("weight_up"):
        up_other = swap(near_up, ("h",))
    rows_of = lambda v: v.reshape(16, tall, 3 * part)[:, own, : own * columns]
    blocks = jnp.concatenate([rows_of(near_qkv), rows_of(far_qkv)], axis=0).astype(WIDE)
    index = jnp.arange(32)
    owner = (((index // 4) % 4) ^ at_dp) * 8 + ((index % 4) ^ at_z) * 2 + ((index // 16) ^ ic)
    chosen = (owner[None, :] == index[:, None]).astype(WIDE)
    blocks = jnp.dot(chosen, blocks)
    table = blocks.reshape(32, columns, own).transpose(1, 0, 2).reshape(columns, width)
    bias_heads = lax.dynamic_slice_in_dim(table[0:2], at_z * part, part, axis=1)
    bias_units = table[3 : 3 + ratio].reshape(2, 2, 2, 2, units // 4)
    bias_units = lax.dynamic_slice(bias_units, (0, ix, 0, il, 0), (2, 1, 2, 1, units // 4))
    bias_units = bias_units.reshape(1, units)

    far_qkv, token_parts[3], table, bias_heads, bias_units = tie(
        far_qkv, token_parts[3], table, bias_heads, bias_units
    )
    with jax.named_scope("weight_out"):
        near_out = jnp.concatenate([low_out, after(out_other, token_parts[3])], axis=0)
        out_other = swap(near_out, ("h",))
    far_qkv, up_other = tie(far_qkv, after(up_other, far_qkv))

    vmem, hbm = pl.BlockSpec(memory_space=pltpu.VMEM), pl.BlockSpec(memory_space=pltpu.HBM)
    q, kv, full_qkv = pl.pallas_call(
        project_kernel,
        name="project_kernel",
        in_specs=[pl.BlockSpec(memory_space=pltpu.SMEM), vmem] + [hbm] * 6,
        out_specs=[vmem] * 3,
        out_shape=[
            jax.ShapeDtypeStruct((4 * count, part), LOW),
            jax.ShapeDtypeStruct((4 * count, 2 * part), LOW),
            jax.ShapeDtypeStruct((width, 3 * part), LOW),
        ],
        scratch_shapes=[
            pltpu.VMEM(near_qkv.shape, LOW),
            pltpu.VMEM(far_qkv.shape, LOW),
            pltpu.VMEM((4 * count, width), LOW),
            pltpu.SemaphoreType.DMA((6,)),
        ],
        compiler_params=pltpu.CompilerParams(vmem_limit_bytes=48 * 2**20),
        cost_estimate=pl.CostEstimate(flops=1, bytes_accessed=1, transcendentals=0),
    )(bits, bias_heads, near_qkv, far_qkv, *token_parts)
    kv, out_other = tie(kv, out_other)
    with jax.named_scope("keys_values"):
        kv_far = swap(kv, ("c",))
    with jax.named_scope("weight_out"):
        near_out = jnp.concatenate([near_out, out_other], axis=0)
        out_parts = exchange([near_out] * 4, "y", "x")
    late_q, late_down, late_up = tie(q, after(low_down, kv_far), near_up)
    with jax.named_scope("weight_up"):
        near_up = jnp.concatenate([late_up, up_other], axis=0)
        up_other = swap(near_up, ("y",))
    with jax.named_scope("weight_down"):
        down_other = swap(late_down, ("h",))
    *attended, lse = call(
        forward_kernel,
        [((count, part), LOW)] * 4 + [((4, 4 * count), WIDE)],
        bits,
        late_q,
        kv,
        kv_far,
    )
    out_parts = [near_out] + [after(piece, lse) for piece in out_parts[1:]]
    near_out = jnp.concatenate(out_parts, axis=0)
    *attended, down_other, near_out = tie(*attended, after(down_other, lse), near_out)
    with jax.named_scope("attended"):
        attended = exchange(attended, "h", "l")
    with jax.named_scope("weight_out"):
        far_out = swap(near_out, ("c",))
        (full_out,) = call(lay_qkv_kernel, [((width, width), LOW)], bits, near_out, far_out)
    attended[1:], up_other, down_other = lax.optimization_barrier(
        (attended[1:], up_other, down_other)
    )
    with jax.named_scope("weight_up"):
        near_up = jnp.concatenate([near_up, up_other], axis=0)
        far_up = swap(near_up, ("c",))
    with jax.named_scope("weight_down"):
        near_down = jnp.concatenate([low_down, down_other], axis=0)
        down_other = swap(near_down, ("y",))
    hidden, hidden_low, normed, scale = call(
        out_kernel,
        [((count, width), WIDE), ((count, width), LOW), ((count, width), WIDE), ((count, 128), WIDE)],
        bits,
        *attended,
        full_out,
        rows,
        table,
    )

    half = count // 2
    with jax.named_scope("hidden"):
        from_l, from_x = swap(hidden_low, ("l",)), swap(hidden_low, ("x",))
    from_l, from_x, far_up, down_other = tie(
        from_l, from_x, after(far_up, from_l, from_x), after(down_other, from_l, from_x)
    )
    with jax.named_scope("hidden"):
        hidden_parts = [hidden_low, from_l, from_x]
        hidden_parts += [swap(from_x[:half], ("l",)), swap(from_l[half:], ("x",))]
    with jax.named_scope("weight_down"):
        near_down = jnp.concatenate([near_down, down_other], axis=0)
        far_down = swap(near_down, ("c",))
    (full_up,) = call(lay_up_kernel, [((width, units), LOW)], bits, near_up, far_up)
    (full_down,) = call(lay_down_kernel, [((units, width), LOW)], bits, near_down, far_down)
    parts_shape = [((count, width), WIDE)] * 3 + [((count // 2, width), LOW)] * 2
    hidden_parts[3], full_down = tie(hidden_parts[3], full_down)
    act, slope = call(
        feed_up_kernel,
        [((4 * count, units), LOW)] * 2,
        bits,
        *hidden_parts,
        full_up,
        bias_units,
        flops=10**9,
    )
    parts = call(feed_down_kernel, parts_shape, bits, act, full_down)
    terms = scatter_square(parts, "x", "l")
    output, grad_two, grad_down, sums_two = call(
        norm_two_kernel,
        [((count, width), LOW), ((count, width), WIDE), ((count, width), LOW), ((8, width), WIDE)],
        bits,
        *terms,
        hidden,
        cotangent[0],
        table,
    )

    with jax.named_scope("grad_down"):
        grad_parts = gather_square(grad_down, "x", "l")
    grad_up, sums_up, *parts = call(
        feed_back_kernel,
        [((4 * count, units), LOW), ((8, units), WIDE)] + parts_shape,
        bits,
        *grad_parts,
        full_down,
        full_up,
        slope,
        flops=2 * 10**9,
    )
    with jax.named_scope("grad_hidden"):
        terms = scatter_square(parts, "x", "l")

    feed_near, feed_far = call(
        feed_grad_kernel,
        [((16 * own + 4 * down_rows, width), LOW)] * 2,
        bits,
        act,
        *grad_parts,
        *hidden_parts,
        grad_up,
        scratch=[pltpu.VMEM((units, width), LOW), pltpu.VMEM((width, units), LOW)],
    )

    def halve(value, axis, start=(), use=()):
        size = value.shape[0] // 2
        other = send(value[size:].astype(LOW), (axis,), start, use)
        return value[:size].astype(WIDE) + other.astype(WIDE)

    with jax.named_scope("grad_weight_feed"):
        feed_other = swap(feed_far, ("c",))
        feed_sum = (feed_near.astype(WIDE) + feed_other.astype(WIDE)).astype(LOW)
    *terms, feed_sum = lax.optimization_barrier((*terms, feed_sum))
    grad_middle, grad_branch, sums_one, *douts = call(
        norm_one_kernel,
        [((count, width), WIDE), ((count, width), LOW), ((8, width), WIDE)]
        + [((count, part), LOW)] * 4,
        bits,
        *terms,
        grad_two,
        normed,
        scale,
        full_out,
        table,
    )
    with jax.named_scope("grad_attended"):
        douts = exchange(douts, "h", "l")
    back = tuple(douts[1:])
    out_near, out_far = call(
        out_grad_kernel,
        [((16 * own, width), LOW)] * 2,
        bits,
        *attended,
        grad_branch,
        scratch=[pltpu.VMEM((width, width), LOW)],
    )
    with jax.named_scope("grad_weight_feed"):
        feed_other = swap(feed_sum[feed_sum.shape[0] // 2 :], ("y",))
    with jax.named_scope("grad_weight_out"):
        out_other = send(out_far, ("c",), use=back)
        out_sum = (out_near.astype(WIDE) + out_other.astype(WIDE)).astype(LOW)
    late_lse, out_sum = tie(lse, out_sum)
    dq, dkv_near, dkv_far, sums_heads = call(
        backward_kernel,
        [
            ((4 * count, part), LOW),
            ((4 * count, 2 * part), WIDE),
            ((4 * count, 2 * part), LOW),
            ((8, part), WIDE),
        ],
        bits,
        q,
        kv,
        kv_far,
        late_lse,
        *douts,
    )
    with jax.named_scope("grad_weight_out"):
        out_sum = halve(out_sum, "x", use=(dq,)).astype(LOW)
    def add_first(value, other):
        return value[: other.shape[0]].astype(WIDE) + other.astype(WIDE)

    feed_sum = add_first(feed_sum, after(feed_other, dq)).astype(LOW)
    dkv_far, out_sum, feed_sum = tie(dkv_far, out_sum, feed_sum)
    up_size = 4 * own
    rows_of_part = lambda start, size: jnp.concatenate(
        [feed_sum[start : start + size], feed_sum[start + up_size + down_rows :][:size]], axis=0
    )
    up_sum, down_sum = rows_of_part(0, up_size), rows_of_part(up_size, down_rows)
    with jax.named_scope("grad_keys_values"):
        dkv_other = swap(dkv_far, ("c",))
    with jax.named_scope("grad_weight_up"):
        up_other = swap(up_sum[up_size:], ("h",))
    with jax.named_scope("grad_weight_out"):
        out_other = swap(out_sum[out_sum.shape[0] // 2 :], ("y",))
    near, far, grad_projected = call(
        qkv_grad_kernel,
        [((16 * tall, 3 * part), LOW)] * 2 + [((4 * count, 3 * part), LOW)],
        bits,
        *token_parts,
        dq,
        dkv_near,
        dkv_other,
        sums_heads,
        sums_one,
        sums_two,
        sums_up,
        scratch=[pltpu.VMEM((width, 3 * part), LOW), pltpu.VMEM((8, 8, 3 * part), WIDE)],
    )
    out_sum = add_first(out_sum, after(out_other, near)).astype(LOW)
    owned_up = add_first(up_sum, after(up_other, near)).astype(LOW)
    far, out_sum, owned_up, down_sum = tie(far, out_sum, owned_up, down_sum)
    with jax.named_scope("grad_weight_qkv"):
        far_other = swap(far, ("c",))
        qkv_sum = (near.astype(WIDE) + far_other.astype(WIDE)).astype(LOW)
    with jax.named_scope("grad_weight_out"):
        out_other = swap(out_sum[2 * own :], ("l",))
    with jax.named_scope("grad_weight_up"):
        up_other = swap(owned_up[2 * own :], ("x",))
    with jax.named_scope("grad_weight_down"):
        down_other = swap(down_sum[down_rows:], ("h",))
    qkv_sum, up_other = tie(qkv_sum, after(up_other, far_other))
    with jax.named_scope("grad_weight_up"):
        up_last = swap(jnp.concatenate([owned_up[own : 2 * own], up_other[own:]], axis=0), ("l",))
    parts = call(
        rows_grad_kernel,
        [((count, width), WIDE)] + [((count, width), LOW)] * 3,
        bits,
        after(grad_projected, far_other),
        full_qkv,
        grad_middle,
    )
    with jax.named_scope("grad_weight_qkv"):
        blocks = [qkv_sum[i * 4 * tall : (i + 1) * 4 * tall] for i in range(4)]
        blocks = exchange(blocks, "y", "x")
        owned_qkv = sum(block.astype(WIDE) for block in blocks).astype(LOW)
    late = tuple(blocks[1:])
    out_sum = add_first(out_sum, after(out_other, *late)).astype(LOW)
    owned_down = add_first(down_sum, after(down_other, *late))
    owned_qkv, owned_down, up_last, out_sum, *parts = tie(
        owned_qkv, owned_down, after(up_last, *late), out_sum, *parts
    )
    up_pieces = [owned_up[:own], up_last[:own], up_other[:own], up_last[own:]]
    with jax.named_scope("grad_weight_qkv"):
        qkv_pieces = exchange([owned_qkv[i * tall : (i + 1) * tall] for i in range(4)], "h", "l")
    with jax.named_scope("grad_weight_out"):
        owned_out = add_first(out_sum, send(out_sum[own:], ("h",), use=(qkv_pieces[1],)))

    total, small_tile = call(
        squares_kernel,
        [((8, 128), WIDE), ((8, 3 * part), WIDE)],
        bits,
        owned_down,
        owned_out,
        *up_pieces,
        *qkv_pieces,
    )
    tile = width // 8
    lanes = 3 * part // tile
    small_tile = small_tile[:2].reshape(2 * lanes, tile)[:columns]
    owned_small = lax.dynamic_slice_in_dim(small_tile, (2 * il + ic) * own, own, axis=1)
    def four(terms):
        return (terms[0] + terms[1]) + (terms[2] + terms[3])

    with jax.named_scope("norm"):
        total = total + swap(total, ("c",))
        total = four(exchange([total] * 4, "h", "l"))
    with jax.named_scope("grad_tokens"):
        far_l = send(parts[3], ("l",), start=late, use=(qkv_pieces[1],))
        to_h = (parts[2].astype(WIDE) + far_l.astype(WIDE)).astype(LOW)
    total, to_h = tie(total, to_h)
    with jax.named_scope("grad_tokens"):
        from_h = swap(to_h, ("h",))
        from_l = send(parts[1], ("l",), start=(total,))
    with jax.named_scope("norm"):
        totals = exchange([total] * 4, "y", "x")
    grad_rows = parts[0] + from_l.astype(WIDE) + from_h.astype(WIDE)
    states = [
        (weight_down, moment_down, second_down),
        (weight_out, moment_out, second_out),
        (weight_up, moment_up, second_up),
        (weight_qkv, moment_qkv, second_qkv),
    ]
    plans = [
        (RATE_MATRIX, whole_places, 1),
        (RATE_OUTPUT, whole_places, 1),
        (RATE_MATRIX, up_places, 4),
        (RATE_MATRIX, qkv_places, 4),
    ]
    grads = [owned_down, owned_out, *up_pieces, *qkv_pieces]
    flat = [array for group in states for array in group]
    results = pl.pallas_call(
        functools.partial(update_kernel, plans),
        name="update_kernel",
        in_specs=[pl.BlockSpec(memory_space=pltpu.SMEM)]
        + [vmem] * 8
        + [hbm] * (len(grads) + 12),
        out_specs=[hbm] * 12 + [vmem] * 4,
        out_shape=[jax.ShapeDtypeStruct(array.shape, WIDE) for array in flat]
        + [jax.ShapeDtypeStruct((8, 128), WIDE)]
        + [jax.ShapeDtypeStruct((columns, own), WIDE)] * 3,
        scratch_shapes=[pltpu.VMEM(grad.shape, grad.dtype) for grad in grads]
        + [pltpu.VMEM(array.shape, WIDE) for array in flat * 2]
        + [pltpu.SemaphoreType.DMA((len(grads),))]
        + [pltpu.SemaphoreType.DMA((12,))] * 2,
        compiler_params=pltpu.CompilerParams(vmem_limit_bytes=60 * 2**20),
        cost_estimate=pl.CostEstimate(flops=1, bytes_accessed=1, transcendentals=0),
    )(
        bits,
        *totals,
        owned_small,
        small_params.T,
        moment_small.T,
        second_small.T,
        *grads,
        *flat,
    )
    new_down, new_moment_down, new_second_down = results[0:3]
    new_out, new_moment_out, new_second_out = results[3:6]
    new_up, new_moment_up, new_second_up = results[6:9]
    new_qkv, new_moment_qkv, new_second_qkv = results[9:12]
    grad_norm = results[12][0, 0]
    new_small, new_moment_small, new_second_small = (value.T for value in results[13:16])
    return (
        output[None],
        grad_rows[None],
        grad_norm,
        new_qkv,
        new_out,
        new_up,
        new_down,
        new_small,
        new_moment_qkv,
        new_moment_out,
        new_moment_up,
        new_moment_down,
        new_moment_small,
        new_second_qkv,
        new_second_out,
        new_second_up,
        new_second_down,
        new_second_small,
    )


def solution(mesh):
    sizes = (mesh.shape["dp"], mesh.shape["seq"])
    if sizes == (4, 8):
        squares = Mesh(mesh.devices.reshape(2, 2, 2, 2, 2), AXES)
        dp, seq = ("y", "x"), ("h", "l", "c")
        body, mesh = on_square, squares
        every = P(AXES, None)
        over = P(dp, seq, None)
    else:
        body = on_device
        every = P(("dp", "seq"), None)
        over = P("dp", "seq", None)
    return jax.shard_map(
        body,
        mesh=mesh,
        in_specs=(over,) * 2 + (every,) * 15,
        out_specs=(over,) * 2 + (P(),) + (every,) * 15,
        check_vma=False,
    )
```

```python
import functools
import math

import jax
import jax.numpy as jnp
from jax import lax
from jax.experimental import pallas as pl
from jax.experimental.pallas import tpu as pltpu
from jax.sharding import Mesh
from jax.sharding import PartitionSpec as P

HEAD = 64
STEP = 5


NORM_EPSILON = 1e-05
ADAM_EPSILON = 1e-08
BETA_FIRST = 0.5
BETA_SECOND = 0.55
CLIP_LIMIT = 1.0
RATE_MATRIX = 0.04
RATE_OUTPUT = 0.5
RATE_SMALL = 0.3
WEIGHT_DECAY = 0.01
SCORE_SCALE = 0.125


def layer_norm(value, gain, shift):
    center = jnp.mean(value, axis=-1, keepdims=True)
    centered = value - center
    variance = jnp.mean(centered * centered, axis=-1, keepdims=True)
    return centered * lax.rsqrt(variance + NORM_EPSILON) * gain + shift


def exact_gelu(value):
    return jax.nn.gelu(value, approximate=False)


def unpack(table_low):
    table = table_low.astype(jnp.float32)
    ratio = table.shape[1] - 8
    bias_up = table[:, 3 : 3 + ratio].T.reshape(-1)
    return (
        table[:, 0],
        table[:, 1],
        table[:, 2],
        bias_up,
        table[:, 3 + ratio],
        table[:, 4 + ratio],
        table[:, 5 + ratio],
        table[:, 6 + ratio],
        table[:, 7 + ratio],
    )


def cross(left, right):
    return lax.dot_general(
        left, right, (((0,), (0,)), ((), ())), preferred_element_type=jnp.float32
    )


def against(left, right):
    return lax.dot_general(
        left, right, (((1,), (1,)), ((), ())), preferred_element_type=jnp.float32
    )


def take_block(source, index, block, heads):
    piece = lax.dynamic_slice_in_dim(source, index * block, block, 0)
    return piece.reshape(block, heads, HEAD)


def scores_of(query_heads, key_heads):
    return (
        jnp.einsum("qhd,khd->hqk", query_heads, key_heads, preferred_element_type=jnp.float32)
        * SCORE_SCALE
    )


def block_grads(query_heads, key_heads, value_heads, dout_heads, log_total, delta):
    scores = scores_of(query_heads, key_heads)
    probs = jnp.exp(scores - log_total[..., None])
    grad_probs = jnp.einsum(
        "qhd,khd->hqk", dout_heads, value_heads, preferred_element_type=jnp.float32
    )
    grad_scores = (probs * (grad_probs - delta[..., None])).astype(jnp.bfloat16)
    return (probs, grad_scores)


def attention_forward(query_heads, keys_all, values_all, block):
    count_rows, heads = (query_heads.shape[0], query_heads.shape[1])
    count = keys_all.shape[0] // block

    def stats_step(index, carry):
        run_top, run_total = carry
        scores = scores_of(query_heads, take_block(keys_all, index, block, heads))
        new_top = jnp.maximum(run_top, jnp.max(scores, axis=-1))
        run_total = run_total * jnp.exp(run_top - new_top) + jnp.sum(
            jnp.exp(scores - new_top[..., None]), axis=-1
        )
        return (new_top, run_total)

    start_top = jnp.full((heads, count_rows), -1e30, jnp.float32)
    start_total = jnp.zeros((heads, count_rows), jnp.float32)
    run_top, run_total = lax.fori_loop(0, count, stats_step, (start_top, start_total))
    log_total = run_top + jnp.log(run_total)

    def value_step(index, accum):
        scores = scores_of(query_heads, take_block(keys_all, index, block, heads))
        weights = jnp.exp(scores - log_total[..., None]).astype(jnp.bfloat16)
        return accum + jnp.einsum(
            "hqk,khd->qhd",
            weights,
            take_block(values_all, index, block, heads),
            preferred_element_type=jnp.float32,
        )

    accum = lax.fori_loop(0, count, value_step, jnp.zeros((count_rows, heads, HEAD), jnp.float32))
    return (accum.reshape(count_rows, heads * HEAD), log_total)


def adam_update(weight, grad, moment, second, rate, decay):
    moment_new = BETA_FIRST * moment + (1.0 - BETA_FIRST) * grad
    second_new = BETA_SECOND * second + (1.0 - BETA_SECOND) * grad * grad
    direction = (
        moment_new
        / (1.0 - BETA_FIRST**STEP)
        / (jnp.sqrt(second_new / (1.0 - BETA_SECOND**STEP)) + ADAM_EPSILON)
    )
    return (weight - rate * (direction + decay * weight), moment_new, second_new)


def on_device(
    tokens,
    cotangent,
    weight_qkv,
    weight_out,
    weight_up,
    weight_down,
    small_params,
    moment_qkv,
    moment_out,
    moment_up,
    moment_down,
    moment_small,
    second_qkv,
    second_out,
    second_up,
    second_down,
    second_small,
):
    rows = tokens[0]
    count_rows = rows.shape[0]
    width = rows.shape[1]
    heads = width // HEAD
    block = 4 * count_rows
    full_qkv, full_out, full_up, full_down, full_small = (
        lax.all_gather(weight_qkv.astype(jnp.bfloat16), ("dp", "seq"), axis=0, tiled=True),
        lax.all_gather(weight_out.astype(jnp.bfloat16), ("dp", "seq"), axis=0, tiled=True),
        lax.all_gather(weight_up.astype(jnp.bfloat16), ("dp", "seq"), axis=0, tiled=True),
        lax.all_gather(weight_down.astype(jnp.bfloat16), ("dp", "seq"), axis=0, tiled=True),
        lax.all_gather(small_params.astype(jnp.bfloat16), ("dp", "seq"), axis=0, tiled=True),
    )
    (
        bias_query,
        bias_value,
        bias_out,
        bias_up,
        bias_down,
        gain_one,
        shift_one,
        gain_two,
        shift_two,
    ) = unpack(full_small)
    projected = jnp.dot(rows, full_qkv, preferred_element_type=jnp.float32)
    query = (projected[:, :width] + bias_query).astype(jnp.bfloat16)
    key_rows = projected[:, width : 2 * width].astype(jnp.bfloat16)
    value_rows = (projected[:, 2 * width :] + bias_value).astype(jnp.bfloat16)
    keys_all, values_all = (
        lax.all_gather(key_rows, "seq", axis=0, tiled=True),
        lax.all_gather(value_rows, "seq", axis=0, tiled=True),
    )
    query_heads = query.reshape(count_rows, heads, HEAD)
    attended, log_total = attention_forward(query_heads, keys_all, values_all, block)
    attended_low = attended.astype(jnp.bfloat16)
    branch = jnp.dot(attended_low, full_out, preferred_element_type=jnp.float32) + bias_out
    middle = rows.astype(jnp.float32) + branch
    hidden, norm_one_back = jax.vjp(layer_norm, middle, gain_one, shift_one)
    hidden_low = hidden.astype(jnp.bfloat16)
    upward = jnp.dot(hidden_low, full_up, preferred_element_type=jnp.float32) + bias_up
    activation, gelu_back = jax.vjp(exact_gelu, upward)
    activation_low = activation.astype(jnp.bfloat16)
    downward = jnp.dot(activation_low, full_down, preferred_element_type=jnp.float32) + bias_down
    output, norm_two_back = jax.vjp(layer_norm, hidden + downward, gain_two, shift_two)
    back_qkv, back_out, back_up, back_down = (full_qkv, full_out, full_up, full_down)
    grad_sum_two, grad_gain_two, grad_shift_two = norm_two_back(cotangent[0].astype(jnp.float32))
    grad_down_low = grad_sum_two.astype(jnp.bfloat16)
    grad_bias_down = jnp.sum(grad_down_low.astype(jnp.float32), axis=0)
    grad_weight_down = cross(activation_low, grad_down_low)
    grad_activation = against(grad_down_low, back_down)
    grad_up_low = gelu_back(grad_activation)[0].astype(jnp.bfloat16)
    grad_bias_up = jnp.sum(grad_up_low.astype(jnp.float32), axis=0)
    grad_weight_up = cross(hidden_low, grad_up_low)
    grad_hidden = grad_sum_two + against(grad_up_low, back_up)
    grad_middle, grad_gain_one, grad_shift_one = norm_one_back(grad_hidden)
    grad_branch_low = grad_middle.astype(jnp.bfloat16)
    grad_bias_out = jnp.sum(grad_branch_low.astype(jnp.float32), axis=0)
    grad_weight_out = cross(attended_low, grad_branch_low)
    grad_attended = against(grad_branch_low, back_out).astype(jnp.bfloat16)
    delta = jnp.sum(
        (grad_attended.astype(jnp.float32) * attended).reshape(count_rows, heads, HEAD), axis=-1
    ).T
    dout_heads = grad_attended.reshape(count_rows, heads, HEAD)
    count = keys_all.shape[0] // block

    def both_step(index, carry):
        grad_query, grad_keys, grad_values = carry
        key_heads = take_block(keys_all, index, block, heads)
        value_heads = take_block(values_all, index, block, heads)
        probs, grad_scores = block_grads(
            query_heads, key_heads, value_heads, dout_heads, log_total, delta
        )
        grad_query = (
            grad_query
            + jnp.einsum("hqk,khd->qhd", grad_scores, key_heads, preferred_element_type=jnp.float32)
            * SCORE_SCALE
        )
        part_keys = (
            jnp.einsum("hqk,qhd->khd", grad_scores, query_heads, preferred_element_type=jnp.float32)
            * SCORE_SCALE
        )
        part_values = jnp.einsum(
            "hqk,qhd->khd",
            probs.astype(jnp.bfloat16),
            dout_heads,
            preferred_element_type=jnp.float32,
        )
        grad_keys = lax.dynamic_update_slice_in_dim(
            grad_keys, part_keys.reshape(block, width), index * block, 0
        )
        grad_values = lax.dynamic_update_slice_in_dim(
            grad_values, part_values.reshape(block, width), index * block, 0
        )
        return (grad_query, grad_keys, grad_values)

    start = (
        jnp.zeros((count_rows, heads, HEAD), jnp.float32),
        jnp.zeros((keys_all.shape[0], width), jnp.float32),
        jnp.zeros((keys_all.shape[0], width), jnp.float32),
    )
    grad_query, grad_keys, grad_values = lax.fori_loop(0, count, both_step, start)
    summed_keys, summed_values = (
        lax.psum_scatter(
            grad_keys.astype(jnp.bfloat16), "seq", scatter_dimension=0, tiled=True
        ).astype(jnp.float32),
        lax.psum_scatter(
            grad_values.astype(jnp.bfloat16), "seq", scatter_dimension=0, tiled=True
        ).astype(jnp.float32),
    )
    grad_query_low = grad_query.reshape(count_rows, width).astype(jnp.bfloat16)
    grad_value_low = summed_values.astype(jnp.bfloat16)
    grad_projected = jnp.concatenate(
        [grad_query_low, summed_keys.astype(jnp.bfloat16), grad_value_low], axis=1
    )
    grad_weight_qkv = cross(rows, grad_projected)
    grad_bias_query = jnp.sum(grad_query_low.astype(jnp.float32), axis=0)
    grad_bias_value = jnp.sum(grad_value_low.astype(jnp.float32), axis=0)
    grad_rows = grad_middle + against(grad_projected, back_qkv)
    ratio = full_up.shape[1] // width
    grad_small = jnp.concatenate(
        [
            jnp.stack([grad_bias_query, grad_bias_value, grad_bias_out], axis=1),
            grad_bias_up.reshape(ratio, width).T,
            jnp.stack(
                [grad_bias_down, grad_gain_one, grad_shift_one, grad_gain_two, grad_shift_two],
                axis=1,
            ),
        ],
        axis=1,
    )
    owned_qkv, owned_out, owned_up, owned_down, owned_small = (
        lax.psum_scatter(grad_weight_qkv, ("dp", "seq"), scatter_dimension=0, tiled=True),
        lax.psum_scatter(grad_weight_out, ("dp", "seq"), scatter_dimension=0, tiled=True),
        lax.psum_scatter(grad_weight_up, ("dp", "seq"), scatter_dimension=0, tiled=True),
        lax.psum_scatter(grad_weight_down, ("dp", "seq"), scatter_dimension=0, tiled=True),
        lax.psum_scatter(grad_small, ("dp", "seq"), scatter_dimension=0, tiled=True),
    )
    squares = jnp.sum(owned_qkv * owned_qkv) + jnp.sum(owned_out * owned_out)
    squares = squares + jnp.sum(owned_up * owned_up) + jnp.sum(owned_down * owned_down)
    squares = squares + jnp.sum(owned_small * owned_small)
    total = lax.psum(squares, ("dp", "seq"))
    grad_norm = jnp.sqrt(total)
    factor = jnp.minimum(1.0, CLIP_LIMIT / (grad_norm + 1e-06))
    new_qkv, new_moment_qkv, new_second_qkv = adam_update(
        weight_qkv, owned_qkv * factor, moment_qkv, second_qkv, RATE_MATRIX, WEIGHT_DECAY
    )
    new_out, new_moment_out, new_second_out = adam_update(
        weight_out, owned_out * factor, moment_out, second_out, RATE_OUTPUT, WEIGHT_DECAY
    )
    new_up, new_moment_up, new_second_up = adam_update(
        weight_up, owned_up * factor, moment_up, second_up, RATE_MATRIX, WEIGHT_DECAY
    )
    new_down, new_moment_down, new_second_down = adam_update(
        weight_down, owned_down * factor, moment_down, second_down, RATE_MATRIX, WEIGHT_DECAY
    )
    new_small, new_moment_small, new_second_small = adam_update(
        small_params, owned_small * factor, moment_small, second_small, RATE_SMALL, 0.0
    )
    return (
        output.astype(jnp.bfloat16)[None],
        grad_rows[None],
        grad_norm,
        new_qkv,
        new_out,
        new_up,
        new_down,
        new_small,
        new_moment_qkv,
        new_moment_out,
        new_moment_up,
        new_moment_down,
        new_moment_small,
        new_second_qkv,
        new_second_out,
        new_second_up,
        new_second_down,
        new_second_small,
    )


AXES = ("y", "x", "h", "l", "c")
LOW = jnp.bfloat16
WIDE = jnp.float32


def swap(value, axes):
    axes = tuple(name for name in AXES if name in axes)
    last = 2 ** len(axes) - 1
    return lax.ppermute(value, axes, [(i, i ^ last) for i in range(last + 1)])


def after(value, *events):
    return lax.optimization_barrier((value, *events))[0]


def tie(*values):
    return lax.optimization_barrier(values)


def send(value, axes, start=(), use=()):
    got = swap(after(value, *start) if start else value, axes)
    return after(got, *use) if use else got


def exchange(parts, a, b, start=(), use=()):
    ways = ((b,), (a,), (a, b))
    return [parts[0]] + [send(part, way, start, use) for part, way in zip(parts[1:], ways)]


def gather_square(value, a, b):
    half = value.shape[0] // 2
    from_a, from_b = swap(value, (a,)), swap(value, (b,))
    return [value, from_b, from_a, swap(from_a[:half], (b,)), swap(from_b[half:], (a,))]


def scatter_square(parts, a, b):
    own, to_b, to_a, far_first, far_second = parts
    half = own.shape[0] // 2
    first = swap(far_first, (a,))
    second = swap(far_second, (b,))
    to_b = jnp.concatenate([to_b[:half] + first.astype(WIDE), to_b[half:]], axis=0).astype(LOW)
    to_a = jnp.concatenate([to_a[:half], to_a[half:] + second.astype(WIDE)], axis=0).astype(LOW)
    return own, swap(to_b, (b,)), swap(to_a, (a,))


def gather_ring(value, a, b, start=(), use=()):
    from_b = send(value, (b,), start, use)
    from_a = swap(after(value, *start) if start else value, (a,))
    far = send(from_a, (b,), use=use)
    return [value, from_b, after(from_a, *use) if use else from_a, far]


def dot(left, right):
    return jnp.dot(left, right, preferred_element_type=WIDE)


def call(kernel, outs, *args, scratch=(), flops=10**9, scalars=0):
    outs = [jax.ShapeDtypeStruct(shape, kind) for shape, kind in outs]
    return pl.pallas_call(
        kernel,
        name=getattr(kernel, "func", kernel).__name__,
        in_specs=[pl.BlockSpec(memory_space=pltpu.SMEM)] * (1 + scalars)
        + [pl.BlockSpec(memory_space=pltpu.VMEM)] * (len(args) - 1 - scalars),
        out_specs=[pl.BlockSpec(memory_space=pltpu.VMEM)] * len(outs),
        out_shape=outs,
        scratch_shapes=list(scratch),
        compiler_params=pltpu.CompilerParams(vmem_limit_bytes=48 * 2**20),
        cost_estimate=pl.CostEstimate(flops=1, bytes_accessed=1, transcendentals=0),
    )(*args)


def at(start, size):
    return pl.ds(pl.multiple_of(start, size), size)


def indices(bits):
    iy, ix, ih, il, ic = (bits[i] for i in range(5))
    return 2 * iy + ix, 2 * ih + il, ic


def pack_qkv_kernel(bits, weight, small, *outs):
    _, z, _ = indices(bits)
    own = weight.shape[0]
    size = outs[0].shape[1] // 3
    for r, out in enumerate(outs):
        for kind in range(3):
            start = kind * 4 * size + (z ^ r) * size
            out[:own, kind * size : (kind + 1) * size] = weight[:, at(start, size)].astype(LOW)
        out[own:, :] = small[...]


def pack_rest_kernel(bits, out_weight, up, down, low_out, low_down, near_up, far_up):
    iy, ix, ih, il, ic = (bits[i] for i in range(5))
    own = up.shape[0]
    size = up.shape[1] // 16
    low_out[...] = out_weight[...].astype(LOW)
    low_down[...] = down[...].astype(LOW)
    for r in range(4):
        out, rows = (near_up, far_up)[r // 2], slice(r % 2 * own, (r % 2 + 1) * own)
        x, l = ix ^ (r // 2), il ^ (r % 2)
        for y in range(2):
            for h in range(2):
                start = (((y * 2 + x) * 2 + h) * 2 + l) * size
                to = (y * 2 + h) * size
                out[rows, to : to + size] = up[:, at(start, size)].astype(LOW)


def lay_rows(bits, full, pieces, own, stride, c):
    d, z, _ = indices(bits)
    for p, piece in enumerate(pieces):
        for s in range(4):
            to = (d ^ p) * 8 * own + (z ^ s) * 2 * own + c * own
            full[at(to, own), :] = piece[s * stride : s * stride + own, :]


def lay_qkv_kernel(bits, near, far, full):
    own = full.shape[0] // 32
    stride = near.shape[0] // 16
    c = bits[4]
    for ref, core in ((near, c), (far, 1 - c)):
        pieces = [ref.at[p * 4 * stride : (p + 1) * 4 * stride] for p in range(4)]
        lay_rows(bits, full, pieces, own, stride, core)


def lay_up_kernel(bits, near, far, full):
    iy, ix, ih, il, ic = (bits[i] for i in range(5))
    own = full.shape[0] // 32
    for ref, core in ((near, ic), (far, 1 - ic)):
        for p in range(4):
            y, h = iy ^ (p // 2), ih ^ (p % 2)
            for q in range(4):
                x, l = ix ^ (q // 2), il ^ (q % 2)
                to = ((((y * 2 + x) * 2 + h) * 2 + l) * 2 + core) * own
                full[at(to, own), :] = ref[(4 * p + q) * own : (4 * p + q + 1) * own, :]


def lay_down_kernel(bits, near, far, full):
    iy, _, ih, _, ic = (bits[i] for i in range(5))
    size = full.shape[0] // 8
    for ref, core in ((near, ic), (far, 1 - ic)):
        for p in range(4):
            to = (((iy ^ (p // 2)) * 2 + (ih ^ (p % 2))) * 2 + core) * size
            full[at(to, size), :] = ref[p * size : (p + 1) * size, :]


def project_kernel(
    bits, bias, near_ref, far_ref, t0, t1, t2, t3, q_ref, kv_ref, full_ref, near, far, rows, sems
):
    d, z, c = indices(bits)
    count = t0.shape[0]
    own = full_ref.shape[0] // 32
    tall = near.shape[0] // 16
    size = q_ref.shape[1]
    pairs = [(near_ref, near), (far_ref, far)]
    pairs += [(ref, rows.at[i * count : (i + 1) * count]) for i, ref in enumerate((t0, t1, t2, t3))]
    copies = [pltpu.make_async_copy(*pair, sems.at[i]) for i, pair in enumerate(pairs)]
    for copy in copies:
        copy.start()
    for copy in copies[:2]:
        copy.wait()
    for ref, core in ((near, c), (far, 1 - c)):
        for p in range(4):
            for s in range(4):
                to = (d ^ p) * 8 * own + (z ^ s) * 2 * own + core * own
                full_ref[at(to, own), :] = ref[(4 * p + s) * tall : (4 * p + s) * tall + own, :]
    for copy in copies[2:]:
        copy.wait()
    projected = dot(rows[...], full_ref[...])
    query = (projected[:, :size] + bias[0:1, :]).astype(LOW)
    q_ref[...] = (query.astype(WIDE) * SCORE_SCALE).astype(LOW)
    kv_ref[:, :size] = projected[:, size : 2 * size].astype(LOW)
    kv_ref[:, size:] = (projected[:, 2 * size :] + bias[1:2, :]).astype(LOW)


def head_mask(shape, axis, head):
    lane = lax.broadcasted_iota(jnp.int32, shape, axis)
    return (lane < HEAD) if head == 0 else (lane >= HEAD)


def forward_kernel(bits, q_ref, near, far, *outs):
    lse_ref = outs[-1]
    count = outs[0].shape[0]
    width = q_ref.shape[1]
    pair = 2 * HEAD
    for group in range(width // pair):
        cols = slice(group * pair, (group + 1) * pair)
        value_cols = slice(width + group * pair, width + (group + 1) * pair)
        keys = jnp.concatenate([near[:, cols], far[:, cols]], axis=0)
        values_t = jnp.concatenate([near[:, value_cols], far[:, value_cols]], axis=0).T
        for piece in range(2):
            rows = slice(2 * piece * count, 2 * (piece + 1) * count)
            queries = q_ref[rows, cols]
            zero = jnp.zeros_like(queries)
            halves = []
            for head in range(2):
                query = jnp.where(head_mask(queries.shape, 1, head), queries, zero)
                scores = against(keys, query)
                top = jnp.max(scores, axis=0, keepdims=True)
                weights = jnp.exp(scores - top)
                total = jnp.sum(weights, axis=0, keepdims=True)
                at_head = 2 * group + head
                lse_ref[at_head : at_head + 1, rows] = top + jnp.log(total)
                halves.append(dot(values_t, weights.astype(LOW)) * (1.0 / total))
            mask = head_mask(halves[0].shape, 0, 0)
            result = jnp.where(mask, halves[0], halves[1]).T.astype(LOW)
            outs[2 * piece][:, cols] = result[:count]
            outs[2 * piece + 1][:, cols] = result[count:]


def backward_kernel(
    bits, q_ref, near, far, lse_ref, d0, d1, d2, d3, dq_ref, near_ref, far_ref, sums
):
    count = d0.shape[0]
    length = 2 * near.shape[0]
    width = q_ref.shape[1]
    pair = 2 * HEAD
    for group in range(width // pair):
        cols = slice(group * pair, (group + 1) * pair)
        value_cols = slice(width + group * pair, width + (group + 1) * pair)
        keys = jnp.concatenate([near[:, cols], far[:, cols]], axis=0)
        values = jnp.concatenate([near[:, value_cols], far[:, value_cols]], axis=0)
        keys_t = keys.T
        sum_keys = jnp.zeros((length, pair), WIDE)
        sum_values = jnp.zeros((length, pair), WIDE)
        bias_query = jnp.zeros((1, pair), WIDE)
        for piece in range(2):
            rows = slice(2 * piece * count, 2 * (piece + 1) * count)
            queries = q_ref[rows, cols]
            refs = (d0, d1) if piece == 0 else (d2, d3)
            douts = jnp.concatenate([refs[0][:, cols], refs[1][:, cols]], axis=0)
            zero = jnp.zeros_like(queries)
            all_probs, all_grads, all_query, all_dout, halves = [], [], [], [], []
            for head in range(2):
                mask = head_mask(queries.shape, 1, head)
                query = jnp.where(mask, queries, zero)
                dout = jnp.where(mask, douts, zero)
                at_head = 2 * group + head
                scores = against(keys, query)
                probs = jnp.exp(scores - lse_ref[at_head : at_head + 1, rows])
                grad_probs = against(values, dout)
                delta = jnp.sum(probs * grad_probs, axis=0, keepdims=True)
                grads = (probs * (grad_probs - delta)).astype(LOW)
                all_probs.append(probs.astype(LOW))
                all_grads.append(grads)
                all_query.append(query)
                all_dout.append(dout)
                halves.append(dot(keys_t, grads))
            mask = head_mask(halves[0].shape, 0, 0)
            dq = jnp.where(mask, halves[0], halves[1]) * SCORE_SCALE
            dq = dq.T.astype(LOW)
            dq_ref[rows, cols] = dq
            bias_query += jnp.sum(dq.astype(WIDE), axis=0, keepdims=True)
            sum_keys += dot(jnp.concatenate(all_grads, axis=1), jnp.concatenate(all_query, axis=0))
            sum_values += dot(jnp.concatenate(all_probs, axis=1), jnp.concatenate(all_dout, axis=0))
        half = length // 2
        near_ref[:, cols] = sum_keys[:half]
        far_ref[:, cols] = sum_keys[half:].astype(LOW)
        sums[0:1, cols] = bias_query
        sums[1:2, cols] = jnp.sum(sum_values, axis=0, keepdims=True)
        near_ref[:, value_cols] = sum_values[:half]
        far_ref[:, value_cols] = sum_values[half:].astype(LOW)


def row_mean(value):
    return jnp.mean(value, axis=-1, keepdims=True)


def column_sums(out, *values):
    out[...] = jnp.zeros_like(out)
    for index, value in enumerate(values):
        out[index : index + 1, :] = jnp.sum(value, axis=0, keepdims=True)


def out_kernel(bits, a0, a1, a2, a3, weight, tokens, table, hidden, low, normed, scale):
    _, z, _ = indices(bits)
    size = a0.shape[1]
    branch = jnp.zeros(hidden.shape, WIDE)
    for r, piece in enumerate((a0, a1, a2, a3)):
        branch += dot(piece[...], weight[at((z ^ r) * size, size), :])
    middle = tokens[...].astype(WIDE) + (branch + table[2:3, :])
    centered = middle - row_mean(middle)
    inverse = lax.rsqrt(row_mean(centered * centered) + NORM_EPSILON)
    unit = centered * inverse
    value = unit * table[-4:-3, :] + table[-3:-2, :]
    hidden[...] = value
    low[...] = value.astype(LOW)
    normed[...] = unit
    scale[...] = jnp.broadcast_to(inverse, scale.shape)


def store_parts(product, own, to_b, to_a, far_first, far_second):
    count = own.shape[0]
    half = count // 2
    own[...] = product[:count]
    to_b[...] = product[count : 2 * count]
    to_a[...] = product[2 * count : 3 * count]
    far_first[...] = product[3 * count : 3 * count + half].astype(LOW)
    far_second[...] = product[3 * count + half :].astype(LOW)


def feed_up_kernel(bits, h0, h1, h2, h3, h4, up, bias, act, slope):
    hidden = jnp.concatenate([ref[...] for ref in (h0, h1, h2, h3, h4)], axis=0)
    upward = dot(hidden, up[...]) + bias[...]
    half = (1.0 + lax.erf(upward * (0.5**0.5))) * 0.5
    act[...] = (upward * half).astype(LOW)
    bell = jnp.exp(upward * upward * -0.5) * (0.5 * 2.0**0.5 * math.pi**-0.5)
    slope[...] = (half + upward * bell).astype(LOW)


def feed_down_kernel(bits, act, down, *parts):
    store_parts(dot(act[...], down[...]), *parts)


def norm_two_kernel(bits, own, from_b, from_a, hidden, cot, table, output, grad, low, sums):
    downward = own[...] + from_b[...].astype(WIDE) + from_a[...].astype(WIDE)
    value = hidden[...] + (downward + table[-5:-4, :])
    centered = value - row_mean(value)
    inverse = lax.rsqrt(row_mean(centered * centered) + NORM_EPSILON)
    unit = centered * inverse
    gain = table[-2:-1, :]
    output[...] = (unit * gain + table[-1:, :]).astype(LOW)
    cotangent = cot[...].astype(WIDE)
    inner = cotangent * gain
    result = inverse * (inner - row_mean(inner) - unit * row_mean(inner * unit))
    grad[...] = result
    rounded = result.astype(LOW)
    low[...] = rounded
    column_sums(sums, rounded.astype(WIDE), cotangent * unit, cotangent)


def feed_back_kernel(bits, g0, g1, g2, g3, g4, down, up, slope, grad_up, sums, *parts):
    grads = jnp.concatenate([ref[...] for ref in (g0, g1, g2, g3, g4)], axis=0)
    upward = (against(grads, down[...]) * slope[...].astype(WIDE)).astype(LOW)
    grad_up[...] = upward
    column_sums(sums, upward.astype(WIDE))
    store_parts(against(upward, up[...]), *parts)


def feed_grad_kernel(
    bits, act, g0, g1, g2, g3, g4, h0, h1, h2, h3, h4, grad_up, near, far, down_full, up_full
):
    iy, ix, ih, il, ic = (bits[i] for i in range(5))
    grads = jnp.concatenate([ref[...] for ref in (g0, g1, g2, g3, g4)], axis=0)
    hidden = jnp.concatenate([ref[...] for ref in (h0, h1, h2, h3, h4)], axis=0)
    down_full[...] = cross(act[...], grads).astype(LOW)
    up_full[...] = cross(hidden, grad_up[...]).astype(LOW)
    own = up_full.shape[0] // 32
    size = down_full.shape[0] // 8
    for p in range(4):
        y, h = iy ^ (p // 2), ih ^ (p % 2)
        base = p * (4 * own + size)
        for q in range(4):
            x, l = ix ^ (q // 2), il ^ (q % 2)
            start = ((((y * 2 + x) * 2 + h) * 2 + l) * 2) * own
            to = base + q * own
            near[to : to + own, :] = up_full[at(start + ic * own, own), :]
            far[to : to + own, :] = up_full[at(start + (1 - ic) * own, own), :]
        start = (y * 2 + h) * 2
        to = base + 4 * own
        near[to : to + size, :] = down_full[at((start + ic) * size, size), :]
        far[to : to + size, :] = down_full[at((start + 1 - ic) * size, size), :]


def norm_one_kernel(
    bits, own, from_b, from_a, above, normed, scale, weight, table, grad, low, sums, *pieces
):
    _, z, _ = indices(bits)
    hidden = own[...] + from_b[...].astype(WIDE) + from_a[...].astype(WIDE)
    hidden = above[...] + hidden
    unit = normed[...]
    inner = hidden * table[-4:-3, :]
    result = scale[:, 0:1] * (inner - row_mean(inner) - unit * row_mean(inner * unit))
    grad[...] = result
    rounded = result.astype(LOW)
    low[...] = rounded
    column_sums(sums, rounded.astype(WIDE), hidden * unit, hidden)
    size = pieces[0].shape[1]
    for r, piece in enumerate(pieces):
        piece[...] = against(rounded, weight[at((z ^ r) * size, size), :]).astype(LOW)


def split_rows(bits, full, near, far, order=(0, 1, 2, 3)):
    d, z, c = indices(bits)
    own = full.shape[0] // 32
    for p in range(4):
        for s in range(4):
            start = (d ^ order[p]) * 8 * own + (z ^ order[s]) * 2 * own
            to = (4 * p + s) * own
            near[to : to + own, :] = full[at(start + c * own, own), :]
            far[to : to + own, :] = full[at(start + (1 - c) * own, own), :]


def out_grad_kernel(bits, a0, a1, a2, a3, grad, near, far, full):
    _, z, _ = indices(bits)
    size = a0.shape[1]
    for r, piece in enumerate((a0, a1, a2, a3)):
        full[at((z ^ r) * size, size), :] = cross(piece[...], grad[...]).astype(LOW)
    split_rows(bits, full, near, far, order=(0, 2, 1, 3))


def qkv_grad_kernel(
    bits, t0, t1, t2, t3, dq, dkv, other, heads, one, two, up, near, far, grads, full, extra
):
    d, z, c = indices(bits)
    tokens = jnp.concatenate([t0[...], t1[...], t2[...], t3[...]], axis=0)
    size = dq.shape[1]
    both = (dkv[...] + other[...].astype(WIDE)).astype(LOW)
    grads[:, :size] = dq[...]
    grads[:, size:] = both
    full[...] = cross(tokens, grads[...]).astype(LOW)
    own = full.shape[0] // 32
    tile = full.shape[0] // 8
    lanes = full.shape[1] // tile
    tall = near.shape[0] // 16
    extra[...] = jnp.zeros_like(extra)
    ratio = up.shape[1] // size
    rows = [(one, 0)] + [None] * ratio + [(two, 0), (one, 1), (one, 2), (two, 1), (two, 2)]
    for k in range(8):
        values = []
        for row in range(2):
            value = heads[row : row + 1, k % 2 * tile : (k % 2 + 1) * tile]
            values.append(jnp.where(z == k // 2, value, 0.0))
        for index, source in enumerate(rows):
            if source is None:
                y, x = (index - 1) // 2, (index - 1) % 2
                lane = ((y * 2 + k // 4) * 2 + k % 2) * tile
                mine = jnp.logical_and(bits[1] == x, bits[3] == k // 2 % 2)
                values.append(jnp.where(mine, up[0:1, lane : lane + tile], 0.0))
            else:
                ref, row = source
                values.append(ref[row : row + 1, k * tile : (k + 1) * tile])
        for column, value in enumerate(values):
            row, lane = column // lanes, column % lanes * tile
            extra[k, row : row + 1, lane : lane + tile] = value
    for p in range(4):
        for s in range(4):
            start = (d ^ p) * 8 * own + (z ^ s) * 2 * own
            to = (4 * p + s) * tall
            near[to : to + own, :] = full[at(start + c * own, own), :]
            far[to : to + own, :] = full[at(start + (1 - c) * own, own), :]
            rows = extra[(d ^ p) * 2 + (z ^ s) // 2].astype(LOW)
            near[to + own : to + tall, :] = rows
            far[to + own : to + tall, :] = rows


def rows_grad_kernel(bits, grads, weight, above, own, *parts):
    product = against(grads[...], weight[...])
    count = own.shape[0]
    own[...] = above[...] + product[:count]
    for r, part in enumerate(parts):
        part[...] = product[(r + 1) * count : (r + 2) * count].astype(LOW)


def squares_kernel(bits, down, out, u0, u1, u2, u3, p0, p1, p2, p3, result, small):
    _, _, c = indices(bits)
    own = out.shape[0]
    values = [ref[...].astype(WIDE) for ref in (down, out, u0, u1, u2, u3)]
    values += [ref[:own, :].astype(WIDE) for ref in (p0, p1, p2, p3)]
    rows = sum(ref[own:, :].astype(WIDE) for ref in (p0, p1, p2, p3))
    small[...] = rows
    lane = lax.broadcasted_iota(jnp.int32, rows.shape, 1) % 128
    mine = (lane // own) == bits[3] * 2 + c
    values.append(jnp.where(mine, rows, 0.0))
    total = jnp.zeros((1, 1), WIDE)
    for value in values:
        total += jnp.sum(jnp.sum(value * value, axis=0, keepdims=True), axis=1, keepdims=True)
    result[...] = jnp.broadcast_to(total, result.shape)


def update_kernel(
    plans, bits, t0, t1, t2, t3, small_grad, small_weight, small_moment, small_second, *refs
):
    count = len(plans)
    total = sum(plan[2] for plan in plans)
    sources, refs = refs[:total], refs[total:]
    norm_ref, *small_results = refs[6 * count : 6 * count + 4]
    refs = refs[: 6 * count] + refs[6 * count + 4 :]
    grads, refs = refs[6 * count : 6 * count + total], refs[: 6 * count] + refs[6 * count + total :]
    brought = refs[-3]
    fetches = [
        pltpu.make_async_copy(sources[i], grads[i], brought.at[i]) for i in range(total)
    ]
    for fetch in fetches:
        fetch.start()
    states, results = refs[: 3 * count], refs[3 * count : 6 * count]
    held, made = refs[6 * count : 9 * count], refs[9 * count : 12 * count]
    arrive, leave = refs[-2:]
    loads = [
        pltpu.make_async_copy(states[i], held[i], arrive.at[i]) for i in range(3 * count)
    ]
    stores = [
        pltpu.make_async_copy(made[i], results[i], leave.at[i]) for i in range(3 * count)
    ]
    for load in loads:
        load.start()
    norm = jnp.sqrt((t0[...] + t1[...]) + (t2[...] + t3[...]))
    norm_ref[...] = norm
    factor = jnp.minimum(1.0, CLIP_LIMIT / (norm[0:1, 0:1] + 1e-06))
    values = adam_update(
        small_weight[...],
        small_grad[...] * factor,
        small_moment[...],
        small_second[...],
        RATE_SMALL,
        0.0,
    )
    for ref, value in zip(small_results, values):
        ref[...] = value
    _, z, _ = indices(bits)
    first = 0
    for index, (rate, places, pieces) in enumerate(plans):
        mine = slice(3 * index, 3 * index + 3)
        for load in loads[mine] + fetches[first : first + pieces]:
            load.wait()
        own = held[3 * index].shape[0]
        for r in range(pieces):
            piece = grads[first + r]
            for source, target in places(bits, z, r, piece.shape[1]):
                grad = piece[:own, source].astype(WIDE) * factor
                weight, moment, second = (ref[:, target] for ref in held[mine])
                values = adam_update(weight, grad, moment, second, rate, WEIGHT_DECAY)
                for ref, value in zip(made[mine], values):
                    ref[:, target] = value
        for store in stores[mine]:
            store.start()
        first += pieces
    for store in stores:
        store.wait()


def whole_places(bits, z, r, columns):
    return [(slice(None), slice(None))]


def qkv_places(bits, z, r, columns):
    size = columns // 3
    return [
        (slice(kind * size, (kind + 1) * size), at(kind * 4 * size + (z ^ r) * size, size))
        for kind in range(3)
    ]


def up_places(bits, z, r, columns):
    size = columns // 4
    x, l = bits[1] ^ (r // 2), bits[3] ^ (r % 2)
    return [
        (
            slice((2 * y + h) * size, (2 * y + h + 1) * size),
            at((((y * 2 + x) * 2 + h) * 2 + l) * size, size),
        )
        for y in range(2)
        for h in range(2)
    ]


def on_square(
    tokens,
    cotangent,
    weight_qkv,
    weight_out,
    weight_up,
    weight_down,
    small_params,
    moment_qkv,
    moment_out,
    moment_up,
    moment_down,
    moment_small,
    second_qkv,
    second_out,
    second_up,
    second_down,
    second_small,
):
    rows = tokens[0]
    count, width = rows.shape
    own = weight_qkv.shape[0]
    down_rows = weight_down.shape[0]
    ratio = weight_up.shape[1] // width
    columns = small_params.shape[1]
    part = width // 4
    units = weight_up.shape[1] // 4
    pad = 16
    tall = own + pad
    iy, ix, ih, il, ic = (lax.axis_index(name) for name in AXES)
    bits = jnp.stack([iy, ix, ih, il, ic]).astype(jnp.int32)
    at_dp, at_z = 2 * iy + ix, 2 * ih + il
    place = 8 * at_dp + 2 * at_z + ic

    low_small = small_params.astype(LOW).T.reshape(1, own * columns)
    low_small = jnp.pad(low_small, ((0, pad - 1), (0, 3 * part - own * columns)))
    with jax.named_scope("weight_qkv"):
        pieces = call(pack_qkv_kernel, [((tall, 3 * part), LOW)] * 4, bits, weight_qkv, low_small)
    with jax.named_scope("tokens"):
        token_l, token_h = swap(rows, ("l",)), swap(rows, ("h",))
    low_out, low_down, up_near, up_far = call(
        pack_rest_kernel,
        [((own, width), LOW), ((down_rows, width), LOW)] + [((2 * own, units), LOW)] * 2,
        bits,
        weight_out,
        weight_up,
        weight_down,
    )
    with jax.named_scope("weight_qkv"):
        near_qkv = jnp.concatenate(exchange(pieces, "h", "l"), axis=0)
        near_qkv = after(near_qkv, token_l, low_out)
    with jax.named_scope("weight_up"):
        up_far = send(up_far, ("x",), start=(near_qkv,))
        up_last = swap(jnp.concatenate([up_near[own:], up_far[own:]], axis=0), ("l",))
        near_up = [up_near[:own], up_last[:own], up_far[:own], up_last[own:]]
        near_up = jnp.concatenate(near_up, axis=0)
    with jax.named_scope("weight_out"):
        out_other = send(low_out, ("l",), start=(near_qkv,))
    with jax.named_scope("weight_qkv"):
        near_qkv = jnp.concatenate(exchange([near_qkv] * 4, "y", "x"), axis=0)
    near_qkv, token_h, near_up, out_other = tie(near_qkv, token_h, near_up, out_other)
    with jax.named_scope("weight_qkv"):
        far_qkv = swap(near_qkv, ("c",))
    with jax.named_scope("tokens"):
        token_parts = [rows, token_l, token_h, swap(token_h, ("l",))]
    with jax.named_scope("weight_up"):
        up_other = swap(near_up, ("h",))
    rows_of = lambda v: v.reshape(16, tall, 3 * part)[:, own, : own * columns]
    blocks = jnp.concatenate([rows_of(near_qkv), rows_of(far_qkv)], axis=0).astype(WIDE)
    index = jnp.arange(32)
    owner = (((index // 4) % 4) ^ at_dp) * 8 + ((index % 4) ^ at_z) * 2 + ((index // 16) ^ ic)
    chosen = (owner[None, :] == index[:, None]).astype(WIDE)
    blocks = jnp.dot(chosen, blocks)
    table = blocks.reshape(32, columns, own).transpose(1, 0, 2).reshape(columns, width)
    bias_heads = lax.dynamic_slice_in_dim(table[0:2], at_z * part, part, axis=1)
    bias_units = table[3 : 3 + ratio].reshape(2, 2, 2, 2, units // 4)
    bias_units = lax.dynamic_slice(bias_units, (0, ix, 0, il, 0), (2, 1, 2, 1, units // 4))
    bias_units = bias_units.reshape(1, units)

    far_qkv, token_parts[3], table, bias_heads, bias_units = tie(
        far_qkv, token_parts[3], table, bias_heads, bias_units
    )
    with jax.named_scope("weight_out"):
        near_out = jnp.concatenate([low_out, after(out_other, token_parts[3])], axis=0)
        out_other = swap(near_out, ("h",))
    far_qkv, up_other = tie(far_qkv, after(up_other, far_qkv))

    vmem, hbm = pl.BlockSpec(memory_space=pltpu.VMEM), pl.BlockSpec(memory_space=pltpu.HBM)
    q, kv, full_qkv = pl.pallas_call(
        project_kernel,
        name="project_kernel",
        in_specs=[pl.BlockSpec(memory_space=pltpu.SMEM), vmem] + [hbm] * 6,
        out_specs=[vmem] * 3,
        out_shape=[
            jax.ShapeDtypeStruct((4 * count, part), LOW),
            jax.ShapeDtypeStruct((4 * count, 2 * part), LOW),
            jax.ShapeDtypeStruct((width, 3 * part), LOW),
        ],
        scratch_shapes=[
            pltpu.VMEM(near_qkv.shape, LOW),
            pltpu.VMEM(far_qkv.shape, LOW),
            pltpu.VMEM((4 * count, width), LOW),
            pltpu.SemaphoreType.DMA((6,)),
        ],
        compiler_params=pltpu.CompilerParams(vmem_limit_bytes=48 * 2**20),
        cost_estimate=pl.CostEstimate(flops=1, bytes_accessed=1, transcendentals=0),
    )(bits, bias_heads, near_qkv, far_qkv, *token_parts)
    kv, out_other = tie(kv, out_other)
    with jax.named_scope("keys_values"):
        kv_far = swap(kv, ("c",))
    with jax.named_scope("weight_out"):
        near_out = jnp.concatenate([near_out, out_other], axis=0)
        out_parts = exchange([near_out] * 4, "y", "x")
    late_q, late_down, late_up = tie(q, after(low_down, kv_far), near_up)
    with jax.named_scope("weight_up"):
        near_up = jnp.concatenate([late_up, up_other], axis=0)
        up_other = swap(near_up, ("y",))
    with jax.named_scope("weight_down"):
        down_other = swap(late_down, ("h",))
    *attended, lse = call(
        forward_kernel,
        [((count, part), LOW)] * 4 + [((4, 4 * count), WIDE)],
        bits,
        late_q,
        kv,
        kv_far,
    )
    out_parts = [near_out] + [after(piece, lse) for piece in out_parts[1:]]
    near_out = jnp.concatenate(out_parts, axis=0)
    *attended, down_other, near_out = tie(*attended, after(down_other, lse), near_out)
    with jax.named_scope("attended"):
        attended = exchange(attended, "h", "l")
    with jax.named_scope("weight_out"):
        far_out = swap(near_out, ("c",))
        (full_out,) = call(lay_qkv_kernel, [((width, width), LOW)], bits, near_out, far_out)
    attended[1:], up_other, down_other = lax.optimization_barrier(
        (attended[1:], up_other, down_other)
    )
    with jax.named_scope("weight_up"):
        near_up = jnp.concatenate([near_up, up_other], axis=0)
        far_up = swap(near_up, ("c",))
    with jax.named_scope("weight_down"):
        near_down = jnp.concatenate([low_down, down_other], axis=0)
        down_other = swap(near_down, ("y",))
    hidden, hidden_low, normed, scale = call(
        out_kernel,
        [((count, width), WIDE), ((count, width), LOW), ((count, width), WIDE), ((count, 128), WIDE)],
        bits,
        *attended,
        full_out,
        rows,
        table,
    )

    half = count // 2
    with jax.named_scope("hidden"):
        from_l, from_x = swap(hidden_low, ("l",)), swap(hidden_low, ("x",))
    from_l, from_x, far_up, down_other = tie(
        from_l, from_x, after(far_up, from_l, from_x), after(down_other, from_l, from_x)
    )
    with jax.named_scope("hidden"):
        hidden_parts = [hidden_low, from_l, from_x]
        hidden_parts += [swap(from_x[:half], ("l",)), swap(from_l[half:], ("x",))]
    with jax.named_scope("weight_down"):
        near_down = jnp.concatenate([near_down, down_other], axis=0)
        far_down = swap(near_down, ("c",))
    (full_up,) = call(lay_up_kernel, [((width, units), LOW)], bits, near_up, far_up)
    (full_down,) = call(lay_down_kernel, [((units, width), LOW)], bits, near_down, far_down)
    parts_shape = [((count, width), WIDE)] * 3 + [((count // 2, width), LOW)] * 2
    hidden_parts[3], full_down = tie(hidden_parts[3], full_down)
    act, slope = call(
        feed_up_kernel,
        [((4 * count, units), LOW)] * 2,
        bits,
        *hidden_parts,
        full_up,
        bias_units,
        flops=10**9,
    )
    parts = call(feed_down_kernel, parts_shape, bits, act, full_down)
    terms = scatter_square(parts, "x", "l")
    output, grad_two, grad_down, sums_two = call(
        norm_two_kernel,
        [((count, width), LOW), ((count, width), WIDE), ((count, width), LOW), ((8, width), WIDE)],
        bits,
        *terms,
        hidden,
        cotangent[0],
        table,
    )

    with jax.named_scope("grad_down"):
        grad_parts = gather_square(grad_down, "x", "l")
    grad_up, sums_up, *parts = call(
        feed_back_kernel,
        [((4 * count, units), LOW), ((8, units), WIDE)] + parts_shape,
        bits,
        *grad_parts,
        full_down,
        full_up,
        slope,
        flops=2 * 10**9,
    )
    with jax.named_scope("grad_hidden"):
        terms = scatter_square(parts, "x", "l")

    feed_near, feed_far = call(
        feed_grad_kernel,
        [((16 * own + 4 * down_rows, width), LOW)] * 2,
        bits,
        act,
        *grad_parts,
        *hidden_parts,
        grad_up,
        scratch=[pltpu.VMEM((units, width), LOW), pltpu.VMEM((width, units), LOW)],
    )

    def halve(value, axis, start=(), use=()):
        size = value.shape[0] // 2
        other = send(value[size:].astype(LOW), (axis,), start, use)
        return value[:size].astype(WIDE) + other.astype(WIDE)

    with jax.named_scope("grad_weight_feed"):
        feed_other = swap(feed_far, ("c",))
        feed_sum = (feed_near.astype(WIDE) + feed_other.astype(WIDE)).astype(LOW)
    *terms, feed_sum = lax.optimization_barrier((*terms, feed_sum))
    grad_middle, grad_branch, sums_one, *douts = call(
        norm_one_kernel,
        [((count, width), WIDE), ((count, width), LOW), ((8, width), WIDE)]
        + [((count, part), LOW)] * 4,
        bits,
        *terms,
        grad_two,
        normed,
        scale,
        full_out,
        table,
    )
    with jax.named_scope("grad_attended"):
        douts = exchange(douts, "h", "l")
    back = tuple(douts[1:])
    out_near, out_far = call(
        out_grad_kernel,
        [((16 * own, width), LOW)] * 2,
        bits,
        *attended,
        grad_branch,
        scratch=[pltpu.VMEM((width, width), LOW)],
    )
    with jax.named_scope("grad_weight_feed"):
        feed_other = swap(feed_sum[feed_sum.shape[0] // 2 :], ("y",))
    with jax.named_scope("grad_weight_out"):
        out_other = send(out_far, ("c",), use=back)
        out_sum = (out_near.astype(WIDE) + out_other.astype(WIDE)).astype(LOW)
    late_lse, out_sum = tie(lse, out_sum)
    dq, dkv_near, dkv_far, sums_heads = call(
        backward_kernel,
        [
            ((4 * count, part), LOW),
            ((4 * count, 2 * part), WIDE),
            ((4 * count, 2 * part), LOW),
            ((8, part), WIDE),
        ],
        bits,
        q,
        kv,
        kv_far,
        late_lse,
        *douts,
    )
    with jax.named_scope("grad_weight_out"):
        out_sum = halve(out_sum, "x", use=(dq,)).astype(LOW)
    def add_first(value, other):
        return value[: other.shape[0]].astype(WIDE) + other.astype(WIDE)

    feed_sum = add_first(feed_sum, after(feed_other, dq)).astype(LOW)
    dkv_far, out_sum, feed_sum = tie(dkv_far, out_sum, feed_sum)
    up_size = 4 * own
    rows_of_part = lambda start, size: jnp.concatenate(
        [feed_sum[start : start + size], feed_sum[start + up_size + down_rows :][:size]], axis=0
    )
    up_sum, down_sum = rows_of_part(0, up_size), rows_of_part(up_size, down_rows)
    with jax.named_scope("grad_keys_values"):
        dkv_other = swap(dkv_far, ("c",))
    with jax.named_scope("grad_weight_up"):
        up_other = swap(up_sum[up_size:], ("h",))
    with jax.named_scope("grad_weight_out"):
        out_other = swap(out_sum[out_sum.shape[0] // 2 :], ("y",))
    near, far, grad_projected = call(
        qkv_grad_kernel,
        [((16 * tall, 3 * part), LOW)] * 2 + [((4 * count, 3 * part), LOW)],
        bits,
        *token_parts,
        dq,
        dkv_near,
        dkv_other,
        sums_heads,
        sums_one,
        sums_two,
        sums_up,
        scratch=[pltpu.VMEM((width, 3 * part), LOW), pltpu.VMEM((8, pad, 3 * part), WIDE)],
    )
    out_sum = add_first(out_sum, after(out_other, near)).astype(LOW)
    owned_up = add_first(up_sum, after(up_other, near)).astype(LOW)
    far, out_sum, owned_up, down_sum = tie(far, out_sum, owned_up, down_sum)
    with jax.named_scope("grad_weight_qkv"):
        far_other = swap(far, ("c",))
        qkv_sum = (near.astype(WIDE) + far_other.astype(WIDE)).astype(LOW)
    with jax.named_scope("grad_weight_out"):
        out_other = swap(out_sum[2 * own :], ("l",))
    with jax.named_scope("grad_weight_up"):
        up_other = swap(owned_up[2 * own :], ("x",))
    with jax.named_scope("grad_weight_down"):
        down_other = swap(down_sum[down_rows:], ("h",))
    qkv_sum, up_other = tie(qkv_sum, after(up_other, far_other))
    with jax.named_scope("grad_weight_up"):
        up_last = swap(jnp.concatenate([owned_up[own : 2 * own], up_other[own:]], axis=0), ("l",))
    parts = call(
        rows_grad_kernel,
        [((count, width), WIDE)] + [((count, width), LOW)] * 3,
        bits,
        after(grad_projected, far_other),
        full_qkv,
        grad_middle,
    )
    with jax.named_scope("grad_weight_qkv"):
        blocks = [qkv_sum[i * 4 * tall : (i + 1) * 4 * tall] for i in range(4)]
        blocks = exchange(blocks, "y", "x")
        owned_qkv = sum(block.astype(WIDE) for block in blocks).astype(LOW)
    late = tuple(blocks[1:])
    out_sum = add_first(out_sum, after(out_other, *late)).astype(LOW)
    owned_down = add_first(down_sum, after(down_other, *late))
    owned_qkv, owned_down, up_last, out_sum, *parts = tie(
        owned_qkv, owned_down, after(up_last, *late), out_sum, *parts
    )
    up_pieces = [owned_up[:own], up_last[:own], up_other[:own], up_last[own:]]
    with jax.named_scope("grad_weight_qkv"):
        qkv_pieces = exchange([owned_qkv[i * tall : (i + 1) * tall] for i in range(4)], "h", "l")
    with jax.named_scope("grad_weight_out"):
        owned_out = add_first(out_sum, send(out_sum[own:], ("h",), use=(qkv_pieces[1],)))

    total, small_tile = call(
        squares_kernel,
        [((8, 128), WIDE), ((pad, 3 * part), WIDE)],
        bits,
        owned_down,
        owned_out,
        *up_pieces,
        *qkv_pieces,
    )
    tile = width // 8
    lanes = 3 * part // tile
    small_tile = small_tile[:2].reshape(2 * lanes, tile)[:columns]
    owned_small = lax.dynamic_slice_in_dim(small_tile, (2 * il + ic) * own, own, axis=1)
    def four(terms):
        return (terms[0] + terms[1]) + (terms[2] + terms[3])

    with jax.named_scope("norm"):
        total = total + swap(total, ("c",))
        total = four(exchange([total] * 4, "h", "l"))
    with jax.named_scope("grad_tokens"):
        far_l = send(parts[3], ("l",), start=late, use=(qkv_pieces[1],))
        to_h = (parts[2].astype(WIDE) + far_l.astype(WIDE)).astype(LOW)
    total, to_h = tie(total, to_h)
    with jax.named_scope("grad_tokens"):
        from_h = swap(to_h, ("h",))
        from_l = send(parts[1], ("l",), start=(total,))
    with jax.named_scope("norm"):
        totals = exchange([total] * 4, "y", "x")
    grad_rows = parts[0] + from_l.astype(WIDE) + from_h.astype(WIDE)
    states = [
        (weight_down, moment_down, second_down),
        (weight_out, moment_out, second_out),
        (weight_up, moment_up, second_up),
        (weight_qkv, moment_qkv, second_qkv),
    ]
    plans = [
        (RATE_MATRIX, whole_places, 1),
        (RATE_OUTPUT, whole_places, 1),
        (RATE_MATRIX, up_places, 4),
        (RATE_MATRIX, qkv_places, 4),
    ]
    grads = [owned_down, owned_out, *up_pieces, *qkv_pieces]
    flat = [array for group in states for array in group]
    results = pl.pallas_call(
        functools.partial(update_kernel, plans),
        name="update_kernel",
        in_specs=[pl.BlockSpec(memory_space=pltpu.SMEM)]
        + [vmem] * 8
        + [hbm] * (len(grads) + 12),
        out_specs=[hbm] * 12 + [vmem] * 4,
        out_shape=[jax.ShapeDtypeStruct(array.shape, WIDE) for array in flat]
        + [jax.ShapeDtypeStruct((8, 128), WIDE)]
        + [jax.ShapeDtypeStruct((columns, own), WIDE)] * 3,
        scratch_shapes=[pltpu.VMEM(grad.shape, grad.dtype) for grad in grads]
        + [pltpu.VMEM(array.shape, WIDE) for array in flat * 2]
        + [pltpu.SemaphoreType.DMA((len(grads),))]
        + [pltpu.SemaphoreType.DMA((12,))] * 2,
        compiler_params=pltpu.CompilerParams(vmem_limit_bytes=60 * 2**20),
        cost_estimate=pl.CostEstimate(flops=1, bytes_accessed=1, transcendentals=0),
    )(
        bits,
        *totals,
        owned_small,
        small_params.T,
        moment_small.T,
        second_small.T,
        *grads,
        *flat,
    )
    new_down, new_moment_down, new_second_down = results[0:3]
    new_out, new_moment_out, new_second_out = results[3:6]
    new_up, new_moment_up, new_second_up = results[6:9]
    new_qkv, new_moment_qkv, new_second_qkv = results[9:12]
    grad_norm = results[12][0, 0]
    new_small, new_moment_small, new_second_small = (value.T for value in results[13:16])
    return (
        output[None],
        grad_rows[None],
        grad_norm,
        new_qkv,
        new_out,
        new_up,
        new_down,
        new_small,
        new_moment_qkv,
        new_moment_out,
        new_moment_up,
        new_moment_down,
        new_moment_small,
        new_second_qkv,
        new_second_out,
        new_second_up,
        new_second_down,
        new_second_small,
    )


def solution(mesh):
    sizes = (mesh.shape["dp"], mesh.shape["seq"])
    if sizes == (4, 8):
        squares = Mesh(mesh.devices.reshape(2, 2, 2, 2, 2), AXES)
        dp, seq = ("y", "x"), ("h", "l", "c")
        body, mesh = on_square, squares
        every = P(AXES, None)
        over = P(dp, seq, None)
    else:
        body = on_device
        every = P(("dp", "seq"), None)
        over = P("dp", "seq", None)
    return jax.shard_map(
        body,
        mesh=mesh,
        in_specs=(over,) * 2 + (every,) * 15,
        out_specs=(over,) * 2 + (P(),) + (every,) * 15,
        check_vma=False,
    )
```
